32 devices in a mesh: fsdp: 8 (over z, x), dp: 4 (over y, core).
Axes of the slice: x: 2, y: 2, z: 4, core: 2. Of those that a mesh axis runs over, the one named last changes fastest.
Arguments:
- tokens: bfloat16 [64, 237, 768], P(('fsdp', 'dp')), may hold values from -6 to 6
- token_type: int32 [64, 237], P(('fsdp', 'dp')), may hold values from 0 to 1, as said below
- mlm_mask: int32 [64, 237], P(('fsdp', 'dp')), may hold values from 0 to 1, as said below
- cotangent: bfloat16 [64, 237, 768], P(('fsdp', 'dp')), may hold values from -6 to 6
- ln1_gain: bfloat16 [768], P('fsdp'), may hold values from 0.5 to 1.5
- ln1_bias: bfloat16 [768], P('fsdp'), may hold values from -2 to 2
- w_qkv: bfloat16 [768, 2304], P('fsdp'), may hold values from -0.21875 to 0.21875
- w_out: bfloat16 [768, 768], P('fsdp'), may hold values from -0.875 to 0.875
- ln2_gain: bfloat16 [768], P('fsdp'), may hold values from 0.5 to 1.5
- ln2_bias: bfloat16 [768], P('fsdp'), may hold values from -2 to 2
- w_up: bfloat16 [2, 768, 3072], P(None, 'fsdp'), may hold values from -0.21875 to 0.21875
- w_down: bfloat16 [2, 3072, 768], P(None, None, 'fsdp'), may hold values from -0.109375 to 0.109375
Outputs:
- mixed: bfloat16 [64, 237, 768], P(('fsdp', 'dp'))
- input_grad: float32 [64, 237, 768], P(('fsdp', 'dp'))
- ln1_gain_grad: float32 [768], P('fsdp')
- ln1_bias_grad: float32 [768], P('fsdp')
- qkv_grad: float32 [768, 2304], P('fsdp')
- out_grad: float32 [768, 768], P('fsdp')
- ln2_gain_grad: float32 [768], P('fsdp')
- ln2_bias_grad: float32 [768], P('fsdp')
- up_grad: float32 [2, 768, 3072], P(None, 'fsdp')
- down_grad: float32 [2, 3072, 768], P(None, None, 'fsdp')
- expert_counts: int32 [2], replicated
The draws below stay inside these ranges and needn't reach their ends.
Inputs may be any that keep to these rules, and one draw needn't show every extreme that they name: `token_type`: in each sequence, 1 marks exactly the first 197 positions (an image-caption pair) or no position (a text-only sequence); sequence 0 is a pair. `mlm_mask`: the last position of every sequence is 1, and so is the first position of sequence 0.
All inputs are finite; a program needn't handle non-finite values.
Results may differ from the reference program's by a relative error of at most 0.012.
Values may be sent and summed in bfloat16 or wider, within the bound.
No kernel may reach another device: no remote copies, remote signals or barrier semaphores. Data moves between devices by JAX's collectives and lax.ppermute only.
A program may use at most 320 MiB of HBM per device.

```python
import jax
import jax.numpy as jnp
from jax import lax

D = 768
HEADS = 12
HEAD = 64
FF = 3072
PATCHES = 197
LEN = 237
SEQS = 64


def sequence_pairs(key):
    kinds = jax.random.randint(jax.random.fold_in(key, 101), (SEQS,), 0, 4)
    return (kinds > 0) | (jnp.arange(SEQS) == 0)


def draw_token_type(key, part):
    pairs = sequence_pairs(key)
    places = jnp.arange(LEN)[None, :]
    return ((places < PATCHES) & pairs[:, None]).astype(jnp.int32)


def draw_mlm_mask(key, part):
    pairs = sequence_pairs(key)
    key = jax.random.fold_in(key, 2)
    order = jnp.arange(SEQS)[:, None]
    places = jnp.arange(LEN)[None, :]
    vision = (places < PATCHES) & pairs[:, None]
    rising = 1000 + 2000 * order // max(SEQS - 1, 1)
    heavy = jax.random.randint(jax.random.fold_in(key, 3), (SEQS, 1), 0, 8) == 0
    heavy_rate = rising * jax.random.randint(jax.random.fold_in(key, 4), (SEQS, 1), 15, 34) // 100
    limit = jnp.where(vision, rising // 5, jnp.where(heavy, heavy_rate, rising // 20))
    draws = jax.random.randint(jax.random.fold_in(key, 5), (SEQS, LEN), 0, 1000)
    forced = (places == LEN - 1) | vision & (order == 0) & (places == 0)
    return ((draws < limit) | forced).astype(jnp.int32)


def levels(stream_key, dims, split, smallest, top_value):
    factor_of, own = 1.0, jax.random.fold_in(stream_key, 6)
    for position, blocks in split:
        steps = jnp.exp(jax.random.uniform(jax.random.fold_in(own, position), (blocks,), jnp.float32, smallest / len(split), top_value / len(split)))
        factor_of = factor_of * jnp.repeat(steps, dims[position] // blocks).reshape([-1 if axis == position else 1 for axis in range(len(dims))])
    return factor_of


def centred(stream_key, extent, deviation, most, shards=(), dtype=jnp.bfloat16):
    loudness = levels(stream_key, extent, shards, -0.22, 0.18) if shards else 1.0
    result = jax.random.normal(stream_key, extent, jnp.float32) * deviation * loudness
    return jnp.minimum(jnp.maximum(result, -most), most).astype(dtype)


def setup_inputs(seed: int = 0) -> dict:
    arg_keys = jax.random.split(jax.random.key(seed), 13)
    tokens = centred(arg_keys[0], (SEQS, LEN, D), 1.0, 6.0, ((0, 32),))
    token_type = draw_token_type(jax.random.fold_in(arg_keys[12], 71), 0)
    mlm_mask = draw_mlm_mask(jax.random.fold_in(arg_keys[12], 71), 0)
    cotangent = centred(arg_keys[3], (SEQS, LEN, D), 1.0, 6.0, ((0, 32),))
    ln1_gain = jnp.clip(1.0 + 0.1 * jax.random.normal(arg_keys[4], (D,), jnp.float32), 0.5, 1.5).astype(jnp.bfloat16)
    ln1_bias = centred(arg_keys[5], (D,), 0.3, 2.0, ((0, 8),))
    w_qkv = centred(arg_keys[6], (D, 3 * D), D ** -0.5, 0.21875, ((0, 8),))
    w_out = centred(arg_keys[7], (D, D), (D // 16) ** -0.5, 0.875, ((0, 8),))
    ln2_gain = jnp.clip(1.0 + 0.1 * jax.random.normal(arg_keys[8], (D,), jnp.float32), 0.5, 1.5).astype(jnp.bfloat16)
    ln2_bias = centred(arg_keys[9], (D,), 0.3, 2.0, ((0, 8),))
    w_up = centred(arg_keys[10], (2, D, FF), D ** -0.5, 0.21875, ((1, 8),))
    w_down = centred(arg_keys[11], (2, FF, D), FF ** -0.5, 0.109375, ((2, 8),))
    return dict(tokens=tokens, token_type=token_type, mlm_mask=mlm_mask, cotangent=cotangent, ln1_gain=ln1_gain, ln1_bias=ln1_bias, w_qkv=w_qkv, w_out=w_out, ln2_gain=ln2_gain, ln2_bias=ln2_bias, w_up=w_up, w_down=w_down)


@jax.custom_vjp
def low(v):
    return lax.optimization_barrier(v.astype(jnp.bfloat16)).astype(jnp.float32)

@jax.custom_vjp
def low_back(v):
    return v

def low_keep(v):
    return (low(v), None)

def low_pass(kept, grad):
    return (grad,)

def back_keep(v):
    return (v, None)

def back_low(kept, grad):
    return (low(grad),)
low.defvjp(low_keep, low_pass)
low_back.defvjp(back_keep, back_low)

def normalize(values, gain_vec, bias_vec):
    center = values - lax.optimization_barrier(jnp.mean(values, -1, keepdims=True))
    spread = lax.optimization_barrier(jnp.mean(center * center, -1, keepdims=True))
    return center * lax.rsqrt(spread + 1e-06) * gain_vec + bias_vec

def matmul(left, right):
    return jnp.dot(left, right, precision=lax.Precision.HIGHEST, preferred_element_type=jnp.float32)

def layer_forward(params, states, token_kind):
    gain_one, bias_one, proj_qkv, proj_out, gain_two, bias_two, proj_up, proj_down = params
    group_size = states.shape[0]
    row_block = states.reshape(group_size * LEN, D)
    first_in = low(normalize(row_block, gain_one, bias_one))
    qkv_all = low_back(low(matmul(first_in, proj_qkv))).reshape(group_size, LEN, 3, HEADS, HEAD)
    query_part = qkv_all[:, :, 0]
    key_part = qkv_all[:, :, 1]
    value_part = qkv_all[:, :, 2]
    scores = jnp.einsum('gqhe,gkhe->ghqk', query_part, key_part, precision=lax.Precision.HIGHEST)
    scores = low_back(scores * HEAD ** (-0.5))
    attn_probs = low(jax.nn.softmax(scores, axis=-1))
    context = jnp.einsum('ghqk,gkhe->gqhe', attn_probs, value_part, precision=lax.Precision.HIGHEST)
    context = low_back(low(context.reshape(group_size * LEN, D)))
    hidden = row_block + low_back(matmul(context, proj_out))
    second_in = low(normalize(hidden, gain_two, bias_two))
    branches = []
    for expert in range(2):
        pre_act = low_back(matmul(second_in, proj_up[expert]))
        post_act = low(jax.nn.gelu(pre_act, approximate=False))
        branches.append(low_back(matmul(post_act, proj_down[expert])))
    is_image = token_kind.reshape(group_size * LEN, 1) == 1
    branch = jnp.where(is_image, branches[1], branches[0])
    return (hidden + branch).reshape(group_size, LEN, D)

def reference(tokens, token_type, mlm_mask, cotangent, ln1_gain, ln1_bias, w_qkv, w_out, ln2_gain, ln2_bias, w_up, w_down):
    params = tuple((weight.astype(jnp.float32) for weight in (ln1_gain, ln1_bias, w_qkv, w_out, ln2_gain, ln2_bias, w_up, w_down)))
    states = tokens.astype(jnp.float32)
    per_group = 16

    def run_all(params_in, states_in):
        grouped = states_in.reshape(SEQS // per_group, per_group, LEN, D)
        kinds = token_type.reshape(SEQS // per_group, per_group, LEN)

        def one_group(group_pair):
            return layer_forward(params_in, group_pair[0], group_pair[1])
        outputs = lax.map(jax.checkpoint(one_group), (grouped, kinds))
        return outputs.reshape(SEQS, LEN, D)
    mixed, pull_back = jax.vjp(run_all, params, states)
    out_grad = cotangent.astype(jnp.float32) * mlm_mask[..., None].astype(jnp.float32)
    param_grads, input_grad = pull_back(out_grad)
    counts = jnp.stack([jnp.sum(mlm_mask * (1 - token_type)), jnp.sum(mlm_mask * token_type)]).astype(jnp.int32)
    divisor = counts.astype(jnp.float32)[:, None, None]
    up_grad = param_grads[6] / divisor
    down_grad = param_grads[7] / divisor
    return (mixed.astype(jnp.bfloat16), input_grad, param_grads[0], param_grads[1], param_grads[2], param_grads[3], param_grads[4], param_grads[5], up_grad, down_grad, counts)
```

```python
import functools

import jax
import jax.numpy as jnp
from jax import lax
from jax.experimental import pallas as pl
from jax.experimental.pallas import tpu as pltpu
from jax.sharding import PartitionSpec as P

HEADS = 12
HEAD = 64
TILE = 256
PATCHES = 197
MIB = 1024 * 1024
BF = jnp.bfloat16
F32 = jnp.float32


def dot(left, right, left_dim=1, right_dim=0):
    return lax.dot_general(
        left, right, (((left_dim,), (right_dim,)), ((), ())), preferred_element_type=F32
    )


def moments(values):
    center = values - jnp.mean(values, -1, keepdims=True)
    inverse = lax.rsqrt(jnp.mean(center * center, -1, keepdims=True) + 1e-06)
    return center * inverse, inverse


def norm_backward(grad, unit, inverse, gain):
    scaled = grad * gain
    slope = jnp.mean(scaled * unit, -1, keepdims=True)
    result = inverse * (scaled - jnp.mean(scaled, -1, keepdims=True) - unit * slope)
    return result, jnp.sum(grad * unit, 0, keepdims=True), jnp.sum(grad, 0, keepdims=True)


def gelu_parts(pre):
    share = 0.5 + 0.5 * lax.erf(pre * 0.7071067811865476)
    density = jnp.exp(-0.5 * pre * pre) * 0.3989422804014327
    return pre * share, share + pre * density


def run_copies(copies):
    for copy in copies:
        copy.start()
    for copy in copies:
        copy.wait()


def attention_copies(place, pieces, weights, sems, rows):
    copies = []
    for piece in pieces:
        for part in range(piece.shape[0]):
            at = len(copies)
            first = pl.multiple_of(place[2 * at + 1], 32)
            copies.append(
                pltpu.make_async_copy(
                    piece.at[part, pl.ds(0, rows)],
                    weights.at[place[2 * at], pl.ds(first, rows)],
                    sems.at[at],
                )
            )
    return copies


def tile(at):
    return pl.ds(pl.multiple_of(at * TILE, TILE), TILE)


def every(count, body):
    lax.fori_loop(0, count, lambda at, carry: (body(at), carry)[1], 0)


def attention_forward(rows, length, place, tok, gains, *refs):
    pieces, rest = refs[:-8], refs[-8:]
    first_in, qkv, probs, context, hidden, second_in, weights, sems = rest
    copies = attention_copies(place, pieces, weights, sems, rows)
    for copy in copies:
        copy.start()
    inputs = tok[...].astype(F32)
    padded, width = inputs.shape
    tiles = width // TILE
    unit, _ = moments(inputs)
    first_in[...] = (unit * gains[0:1] + gains[1:2]).astype(BF)
    for copy in copies:
        copy.wait()

    def project(at):
        block = weights[at // tiles, :, tile(at % tiles)]
        qkv[:, tile(at)] = dot(first_in[...], block).astype(BF)

    every(3 * tiles, project)
    pair = 2 * HEAD
    low_half = lax.broadcasted_iota(jnp.int32, (padded, pair), 1) < HEAD
    real = lax.broadcasted_iota(jnp.int32, (padded, padded), 1) < length

    def heads(at):
        lanes = pl.multiple_of(at * pair, pair)
        query = qkv[:, pl.ds(lanes, pair)]
        key = qkv[:, pl.ds(width + lanes, pair)]
        value = qkv[:, pl.ds(2 * width + lanes, pair)]
        total = jnp.zeros((padded, pair), F32)
        for half in range(2):
            keep = low_half if half == 0 else jnp.logical_not(low_half)
            scores = dot(jnp.where(keep, query, 0), key, 1, 1) * HEAD ** (-0.5)
            scores = jnp.where(real, scores, -1e30)
            grown = jnp.exp(scores - jnp.max(scores, -1, keepdims=True))
            prob = (grown / jnp.sum(grown, -1, keepdims=True)).astype(BF)
            probs[2 * at + half] = prob
            total += dot(prob, jnp.where(keep, value, 0))
        context[:, pl.ds(lanes, pair)] = total.astype(BF)

    every(HEADS // 2, heads)

    def project_out(at):
        added = dot(context[...], weights[3, :, tile(at)])
        hidden[:, tile(at)] = tok[:, tile(at)].astype(F32) + added

    every(tiles, project_out)
    unit, _ = moments(hidden[...])
    second_in[...] = (unit * gains[2:3] + gains[3:4]).astype(BF)


def block_copies(sources, target, sems, main, tail, first=0):
    copies = []
    for at, source in enumerate(sources):
        left = source.shape[0] - tail
        copies.append(
            pltpu.make_async_copy(
                source.at[pl.ds(0, main)], target.at[at], sems.at[first + 2 * at]
            )
        )
        copies.append(
            pltpu.make_async_copy(
                source.at[pl.ds(tail, left)],
                target.at[len(sources), pl.ds(at * left, left)],
                sems.at[first + 2 * at + 1],
            )
        )
    return copies


def expert_copies(place, pieces, weights, sems):
    copies = []
    for at, piece in enumerate(pieces):
        first = pl.multiple_of(place[at], 32)
        copies.append(
            pltpu.make_async_copy(
                piece, weights.at[:, pl.ds(first, piece.shape[1])], sems.at[at]
            )
        )
    return copies


def expert_layer(half, main, tail, place, kinds, *refs):
    states, grads = refs[:4], refs[4:8]
    pieces, rest = refs[8:-14], refs[-14:]
    act, dpre, keep_grad, send_grad, keep_out, send_out = rest[:6]
    weights, state, grad, state_out, grad_out, sems, state_sems, grad_sems = rest[6:]
    width, hidden = weights.shape[1:]
    left = keep_grad.shape[1] - tail
    copies = expert_copies(place, pieces, weights, sems)
    copies += block_copies(states, state, state_sems, main, tail)
    copies += block_copies([ref.at[half] for ref in grads], grad, grad_sems, main, tail)
    for copy in copies:
        copy.start()
    spare = main - 4 * left
    state[4, 4 * left :] = jnp.zeros((spare, width), BF)
    grad[4, 4 * left :] = jnp.zeros((spare, width), BF)
    for copy in copies:
        copy.wait()
    spot = lax.broadcasted_iota(jnp.int32, (main, 1), 0)
    image = spot < PATCHES
    text = (spot % left + tail >= PATCHES) & (spot < 4 * left)
    tiles = hidden // TILE

    def forward(step):
        at, columns = step // tiles, tile(step % tiles)
        expert = kinds[at]
        pre = dot(state[at], weights[expert, :, columns])
        dact = dot(grad[at], weights[2 + expert, :, columns])
        value, slope = gelu_parts(pre)
        mine = (image & (at < 4)) | (text & (at == 4))
        act[at, :, columns] = jnp.where(mine, value, 0).astype(BF)
        dpre[at, :, columns] = jnp.where(mine, dact * slope, 0).astype(BF)

    every(5 * tiles, forward)
    wide = width // TILE

    def outputs(step):
        at, columns = step // wide, tile(step % wide)
        expert = kinds[at]
        grad_out[at, :, columns] = dot(dpre[at], weights[expert, columns], 1, 1).astype(BF)
        state_out[at, :, columns] = dot(act[at], weights[2 + expert, columns], 1, 1).astype(BF)

    every(5 * wide, outputs)
    for rel in range(4):
        for source, target in (
            (grad_out, send_grad if rel % 2 else keep_grad),
            (state_out, send_out if rel % 2 else keep_out),
        ):
            target[rel // 2, :tail] = source[rel, :tail]
            both = source[4, rel * left : rel * left + main - tail]
            target[rel // 2, tail:main] = source[rel, tail:main] + both
            rest_rows = source[4, rel * left + main - tail : (rel + 1) * left]
            target[rel // 2, main:] = rest_rows


def expert_weight_grads(main, tail, halves, pieces, place, kinds, *refs):
    states, refs = refs[: 4 * halves], refs[4 * halves :]
    grads, refs = refs[:4], refs[4:]
    acts, refs = refs[:halves], refs[halves:]
    dpres, refs = refs[:halves], refs[halves:]
    outs, rest = refs[:pieces], refs[pieces:]
    total, rounded, state, grad, act, dpre, sems, state_sems, grad_sems, rest_sems = rest
    width, hidden = total.shape[1:]
    blocks = 5 * halves
    left = states[0].shape[0] - tail
    copies = []
    for half in range(halves):
        there = pl.ds(5 * half, 5)
        copies += block_copies(
            states[4 * half : 4 * half + 4], state.at[there], state_sems, main, tail, 8 * half
        )
        copies += block_copies(
            [ref.at[half] for ref in grads], grad.at[there], grad_sems, main, tail, 8 * half
        )
        copies.append(pltpu.make_async_copy(acts[half], act.at[there], rest_sems.at[2 * half]))
        copies.append(
            pltpu.make_async_copy(dpres[half], dpre.at[there], rest_sems.at[2 * half + 1])
        )
    for copy in copies:
        copy.start()
    for half in range(halves):
        spare = main - 4 * left
        state[5 * half + 4, 4 * left :] = jnp.zeros((spare, width), BF)
        grad[5 * half + 4, 4 * left :] = jnp.zeros((spare, width), BF)
    total[...] = jnp.zeros(total.shape, F32)
    for copy in copies:
        copy.wait()
    tiles = width // TILE

    def accumulate(step):
        at, columns = step // tiles, tile(step % tiles)
        expert = kinds[at]
        total[expert, columns] += dot(state[at, :, columns], dpre[at], 0, 0)
        total[2 + expert, columns] += dot(grad[at, :, columns], act[at], 0, 0)

    every(blocks * tiles, accumulate)
    rounded[...] = total[...].astype(BF)
    copies = []
    for at, out in enumerate(outs):
        first = pl.multiple_of(place[at], 32)
        copies.append(
            pltpu.make_async_copy(rounded.at[:, pl.ds(first, out.shape[1])], out, sems.at[at])
        )
    run_copies(copies)


def attention_backward(rows, length, place, tok, gains, near, far, dmixed, qkv, probs, hidden, *refs):
    pieces, rest = refs[:-7], refs[-7:]
    low, dqkv, input_grad, norm_grads, weights, total, sems = rest
    copies = attention_copies(place, pieces, weights, sems, rows)
    for copy in copies:
        copy.start()
    padded, width = tok.shape
    tiles = width // TILE
    unit, inverse = moments(hidden[...])
    second = near[...].astype(F32) + far[...].astype(F32)
    part, gain_two, bias_two = norm_backward(second, unit, inverse, gains[2:3])
    low[...] = (dmixed[...].astype(F32) + part).astype(BF)
    norm_grads[2:3] = gain_two
    norm_grads[3:4] = bias_two
    for copy in copies:
        copy.wait()

    def project_out(at):
        dqkv[:, tile(at)] = dot(low[...], weights[3, tile(at)], 1, 1).astype(BF)

    every(tiles, project_out)
    pair = 2 * HEAD
    low_half = lax.broadcasted_iota(jnp.int32, (padded, pair), 1) < HEAD

    def heads(at):
        lanes = pl.multiple_of(at * pair, pair)
        query = qkv[:, pl.ds(lanes, pair)]
        key = qkv[:, pl.ds(width + lanes, pair)]
        value = qkv[:, pl.ds(2 * width + lanes, pair)]
        upper = dqkv[:, pl.ds(lanes, pair)]
        dquery = jnp.zeros((padded, pair), F32)
        dkey = jnp.zeros((padded, pair), F32)
        dvalue = jnp.zeros((padded, pair), F32)
        for half in range(2):
            keep = low_half if half == 0 else jnp.logical_not(low_half)
            prob = probs[2 * at + half]
            wide = prob.astype(F32)
            upper_half = jnp.where(keep, upper, 0)
            dprob = dot(upper_half, value, 1, 1)
            dscore = (wide * (dprob - jnp.sum(dprob * wide, -1, keepdims=True))).astype(BF)
            dquery += dot(dscore, jnp.where(keep, key, 0))
            dkey += dot(dscore, jnp.where(keep, query, 0), 0, 0)
            dvalue += dot(prob, upper_half, 0, 0)
        dqkv[:, pl.ds(lanes, pair)] = (dquery * HEAD ** (-0.5)).astype(BF)
        dqkv[:, pl.ds(width + lanes, pair)] = (dkey * HEAD ** (-0.5)).astype(BF)
        dqkv[:, pl.ds(2 * width + lanes, pair)] = dvalue.astype(BF)

    every(HEADS // 2, heads)

    def project(at):
        part = dot(dqkv[:, 0:width], weights[0, tile(at)], 1, 1)
        part += dot(dqkv[:, width : 2 * width], weights[1, tile(at)], 1, 1)
        part += dot(dqkv[:, 2 * width : 3 * width], weights[2, tile(at)], 1, 1)
        total[:, tile(at)] = part

    every(tiles, project)
    unit, inverse = moments(tok[...].astype(F32))
    part, gain_one, bias_one = norm_backward(total[...], unit, inverse, gains[0:1])
    norm_grads[0:1] = gain_one
    norm_grads[1:2] = bias_one
    unit, inverse = moments(hidden[...])
    second = near[...].astype(F32) + far[...].astype(F32)
    upper, _, _ = norm_backward(second, unit, inverse, gains[2:3])
    input_grad[...] = (part + (dmixed[...].astype(F32) + upper))[:length]


def attention_weight_grads(halves, rows, extra, parts, place, *refs):
    firsts, refs = refs[:halves], refs[halves:]
    contexts, refs = refs[:halves], refs[halves:]
    lows, refs = refs[:halves], refs[halves:]
    dqkvs, refs = refs[:halves], refs[halves:]
    norms, refs = refs[:halves], refs[halves:]
    keep, send, rounded, vectors, sems = refs
    width = firsts[0].shape[1]
    tiles = width // TILE

    def project(step):
        part, columns = step // tiles, tile(step % tiles)
        there = pl.ds(pl.multiple_of(part * width, width), width)
        total = dot(firsts[0][:, columns], dqkvs[0][:, there], 0, 0)
        for first, dqkv in zip(firsts[1:], dqkvs[1:]):
            total += dot(first[:, columns], dqkv[:, there], 0, 0)
        rounded[part, columns] = total.astype(BF)

    every(3 * tiles, project)

    def project_out(step):
        columns = tile(step)
        total = dot(contexts[0][:, columns], lows[0][...], 0, 0)
        for context, low in zip(contexts[1:], lows[1:]):
            total += dot(context[:, columns], low[...], 0, 0)
        rounded[3, columns] = total.astype(BF)

    every(tiles, project_out)
    if extra:
        norm = norms[0][...]
        for ref in norms[1:]:
            norm += ref[...]
        spot = lax.broadcasted_iota(jnp.int32, (extra, width), 0)
        lane = lax.broadcasted_iota(jnp.int32, (extra, width), 1)
        inside = (spot == 0) & (lane < rows)
        for part in range(4):
            for shard in range(width // rows):
                row = jnp.broadcast_to(norm[part : part + 1], (extra, width))
                if shard:
                    row = pltpu.roll(row, width - shard * rows, 1)
                vectors[part, shard] = jnp.where(inside, row, 0.0).astype(BF)
    copies = []
    for at in range(4 * parts):
        side, index = divmod(at, 2 * parts)
        ref = keep if side == 0 else send
        outer, inner = divmod(index, parts)
        quarter, shard = place[2 * at], place[2 * at + 1]
        first_row = pl.multiple_of(shard * rows, 32)
        copies.append(
            pltpu.make_async_copy(
                rounded.at[quarter, pl.ds(first_row, rows)],
                ref.at[outer, inner, pl.ds(0, rows)],
                sems.at[len(copies)],
            )
        )
        if extra:
            copies.append(
                pltpu.make_async_copy(
                    vectors.at[quarter, shard],
                    ref.at[outer, inner, pl.ds(rows, extra)],
                    sems.at[len(copies)],
                )
            )
    run_copies(copies)


ANYWHERE = pl.BlockSpec(memory_space=pl.ANY)
SCALARS = pl.BlockSpec(memory_space=pltpu.SMEM)
WHOLE = pl.BlockSpec(memory_space=pltpu.VMEM)


def one_of(array, index):
    tail = (0,) * (array.ndim - 1)
    return pl.BlockSpec((None,) + array.shape[1:], lambda step: (index,) + tail)


def shaped(shape, dtype=BF):
    return jax.ShapeDtypeStruct(shape, dtype)


def call(kernel, out_shape, in_specs, out_specs, scratch, args, flops, moved):
    return pl.pallas_call(
        kernel,
        grid=(1,),
        out_shape=out_shape,
        in_specs=in_specs,
        out_specs=out_specs,
        scratch_shapes=scratch,
        compiler_params=pltpu.CompilerParams(vmem_limit_bytes=50 * MIB),
        cost_estimate=pl.CostEstimate(flops=flops, bytes_accessed=moved, transcendentals=0),
    )(*args)


def add(left, right):
    return (left.astype(F32) + right.astype(F32)).astype(BF)


def per_device(
    tokens,
    token_type,
    mlm_mask,
    cotangent,
    ln1_gain,
    ln1_bias,
    w_qkv,
    w_out,
    ln2_gain,
    ln2_bias,
    w_up,
    w_down,
):
    halves, length, width = tokens.shape
    shards, replicas = lax.axis_size("fsdp"), lax.axis_size("dp")
    shard, replica = lax.axis_index("fsdp"), lax.axis_index("dp")
    rows = width // shards
    lines = shards // 2
    line, side = shard // 2, shard % 2
    columns = w_up.shape[2] // replicas
    padded = -(-length // 16) * 16
    main = -(-PATCHES // 16) * 16
    tail = PATCHES // 16 * 16
    ringed = rows % 32 == 0
    extra = 16 if ringed else 0
    spans = rows if ringed else width

    def swap(axis, size, bit):
        return lambda value: lax.ppermute(value, axis, [(i, i ^ bit) for i in range(size)])

    swap_core = swap("dp", replicas, 1)
    swap_row = swap("dp", replicas, 2)
    swap_side = swap("fsdp", shards, 1)

    def step_line(value):
        return lax.ppermute(value, "fsdp", [(i, (i + 2) % shards) for i in range(shards)])

    def owner(steps, other):
        return 2 * jnp.mod(line - steps, lines) + jnp.bitwise_xor(side, other)

    order = [(steps, other) for steps in range(lines) for other in range(2)]

    block = jnp.where(
        replica < 3,
        lax.dynamic_slice(w_qkv, (0, jnp.minimum(replica, 2) * width), (rows, width)),
        w_out,
    )
    vectors = jnp.stack([ln1_gain, ln1_bias, ln2_gain, ln2_bias])
    if ringed:
        line_block = jnp.zeros((extra, width), BF).at[0, : 4 * rows].set(vectors.reshape(-1))
        block = jnp.concatenate([block, line_block], 0)
        held = jnp.stack([block, swap_side(block)])
        ring = [held]
        for _ in range(lines - 1):
            ring.append(step_line(ring[-1]))
        found = jnp.concatenate([part[:, rows, : 4 * rows] for part in ring], 0)
        wanted = jnp.arange(shards)
        found = found[
            2 * jnp.mod(line - wanted // 2, lines) + jnp.bitwise_xor(wanted % 2, side)
        ]
        gains = found.reshape(shards, 4, rows).transpose(1, 0, 2).reshape(4, width)
    else:
        ring = [lax.all_gather(block, "fsdp", axis=0, tiled=True)[None]]
        gains = lax.all_gather(vectors, "fsdp", axis=1, tiled=True)
    gains = gains.astype(F32)
    attn_pieces, attn_place = [], []
    for steps, part in enumerate(ring):
        across = swap_row(part)
        for rel, copy in enumerate((part, swap_core(part), across, swap_core(across))):
            attn_pieces.append(copy)
            for other in range(part.shape[0]):
                attn_place.append(jnp.bitwise_xor(replica, rel))
                attn_place.append(owner(steps, other) * rows if ringed else jnp.int32(0))
    attn_place = jnp.stack(attn_place).astype(jnp.int32)

    expert_block = jnp.concatenate(
        [
            lax.dynamic_slice(w_up, (0, 0, replica * columns), (2, rows, columns)),
            lax.dynamic_slice(w_down, (0, replica * columns, 0), (2, columns, rows)).transpose(
                0, 2, 1
            ),
        ],
        0,
    )
    if ringed:
        expert_pieces, current = [], expert_block
        for steps in range(lines):
            expert_pieces += [current, swap_side(current)]
            if steps < lines - 1:
                current = step_line(current)
        expert_place = jnp.stack([owner(*at) * rows for at in order]).astype(jnp.int32)
    else:
        expert_pieces = [lax.all_gather(expert_block, "fsdp", axis=1, tiled=True)]
        expert_place = jnp.zeros((1,), jnp.int32)

    kinds_here = token_type[:, 0]
    image_count = jnp.sum(mlm_mask * token_type)
    counts = jnp.stack([jnp.sum(mlm_mask) - image_count, image_count])
    bits = jnp.sum(kinds_here << jnp.arange(halves))

    def note(bits_now, counts_now):
        return jnp.zeros((8, 128), jnp.int32).at[0, :3].set(
            jnp.concatenate([bits_now[None], counts_now])
        )

    heard = swap_core(note(bits, counts))[0]
    bits, counts = bits | (heard[0] << halves), counts + heard[1:3]
    heard = swap_row(note(bits, counts))[0]
    bits, counts = bits | (heard[0] << (2 * halves)), counts + heard[1:3]
    stride = 1
    while stride < shards:
        heard = swap("fsdp", shards, stride)(note(bits, counts))[0]
        counts = counts + heard[1:3]
        stride *= 2
    kinds = (bits >> jnp.arange(4 * halves)) & 1
    kinds = kinds.reshape(4, halves).T
    kinds = jnp.concatenate([kinds, jnp.zeros((halves, 1), jnp.int32)], 1)

    gap = ((0, 0), (0, padded - length), (0, 0))
    tok = jnp.pad(tokens, gap)
    dmixed = jnp.pad(cotangent * mlm_mask[..., None].astype(BF), gap)
    dmixed_row = swap_row(dmixed)
    grads = [dmixed, swap_core(dmixed), dmixed_row, swap_core(dmixed_row)]

    attn_sems = pltpu.SemaphoreType.DMA((attn_place.shape[0] // 2,))
    attn_weights = pltpu.VMEM((4, width, width), BF)
    states_of, kept = [], []
    for half in range(halves):
        first_in, qkv, probs, context, hidden, second_in = call(
            functools.partial(attention_forward, spans, length),
            [
                shaped((padded, width)),
                shaped((padded, 3 * width)),
                shaped((HEADS, padded, padded)),
                shaped((padded, width)),
                shaped((padded, width), F32),
                shaped((padded, width)),
            ],
            [SCALARS, one_of(tok, half), WHOLE] + [ANYWHERE] * len(attn_pieces),
            [WHOLE] * 6,
            [attn_weights, attn_sems],
            (attn_place, tok, gains, *attn_pieces),
            flops=10 * padded * width * width,
            moved=16 * MIB,
        )
        kept.append((first_in, qkv, probs, context, hidden))
        across = swap_row(second_in)
        states_of.append([second_in, swap_core(second_in), across, swap_core(across)])

    expert_scratch = [
        pltpu.VMEM((4, width, columns), BF),
        *[pltpu.VMEM((5, main, width), BF)] * 4,
        pltpu.SemaphoreType.DMA((len(expert_pieces),)),
        pltpu.SemaphoreType.DMA((8,)),
        pltpu.SemaphoreType.DMA((8,)),
    ]
    acts, dpres, outs, arriving = [], [], [], []
    for half in range(halves):
        act, dpre, keep_grad, send_grad, keep_out, send_out = call(
            functools.partial(expert_layer, half, main, tail),
            [shaped((5, main, columns))] * 2 + [shaped((2, padded, width))] * 4,
            [SCALARS] * 2 + [ANYWHERE] * (8 + len(expert_pieces)),
            [WHOLE] * 6,
            expert_scratch,
            (expert_place, kinds[half], *states_of[half], *grads, *expert_pieces),
            flops=32 * padded * width * columns,
            moved=16 * MIB,
        )
        acts.append(act)
        dpres.append(dpre)
        summed = add(keep_grad, swap_core(send_grad))
        arriving.append((summed, swap_row(summed[1])))
        outs.append(add(keep_out, swap_core(send_out)))

    piece_count = len(expert_pieces)
    expert_parts = call(
        functools.partial(expert_weight_grads, main, tail, halves, piece_count),
        [shaped((4, spans, columns))] * piece_count,
        [SCALARS] * 2 + [ANYWHERE] * (4 * halves + 4 + 2 * halves),
        [ANYWHERE] * piece_count,
        [
            pltpu.VMEM((4, width, columns), F32),
            pltpu.VMEM((4, width, columns), BF),
            *[pltpu.VMEM((5 * halves, main, width), BF)] * 2,
            *[pltpu.VMEM((5 * halves, main, columns), BF)] * 2,
            pltpu.SemaphoreType.DMA((piece_count,)),
            pltpu.SemaphoreType.DMA((8 * halves,)),
            pltpu.SemaphoreType.DMA((8 * halves,)),
            pltpu.SemaphoreType.DMA((2 * halves,)),
        ],
        (
            expert_place,
            kinds.reshape(-1),
            *[state for states in states_of for state in states],
            *grads,
            *acts,
            *dpres,
        ),
        flops=32 * padded * width * columns,
        moved=16 * MIB,
    )

    if ringed:
        near = {}
        for steps in [*range(1, lines), 0]:
            near[steps] = add(expert_parts[2 * steps], swap_side(expert_parts[2 * steps + 1]))
        current = near[1]
        for steps in range(1, lines):
            current = add(step_line(current), near[(steps + 1) % lines])
    else:
        current = lax.psum_scatter(expert_parts[0], "fsdp", scatter_dimension=1, tiled=True)

    def all_replicas(value):
        across = swap_row(value)
        return jnp.stack([value, swap_core(value), across, swap_core(across)])

    def in_order(found):
        return [
            lax.dynamic_index_in_dim(found, jnp.bitwise_xor(replica, at), 0, keepdims=False)
            for at in range(4)
        ]

    expert_all = in_order(all_replicas(current))
    divisor = counts.astype(F32)[:, None, None]
    up_grad = jnp.concatenate([part[:2] for part in expert_all], 2).astype(F32) / divisor
    down_grad = (
        jnp.concatenate([part[2:] for part in expert_all], 2).astype(F32).transpose(0, 2, 1)
        / divisor
    )

    out_sum = jnp.stack(outs)
    out_rest = swap_row(out_sum[:, 1])
    mixed = jnp.stack(
        [
            (kept[h][4] + out_sum[h, 0].astype(F32) + out_rest[h].astype(F32))[:length]
            for h in range(halves)
        ]
    ).astype(BF)

    lows, dqkvs, norm_parts, input_grads = [], [], [], []
    for half in range(halves):
        first_in, qkv, probs, context, hidden = kept[half]
        summed, far = arriving[half]
        low, dqkv, input_grad, norm_grads = call(
            functools.partial(attention_backward, spans, length),
            [
                shaped((padded, width)),
                shaped((padded, 3 * width)),
                shaped((length, width), F32),
                shaped((4, width), F32),
            ],
            [SCALARS, one_of(tok, half), WHOLE, one_of(summed, 0), WHOLE, one_of(dmixed, half)]
            + [WHOLE] * 3
            + [ANYWHERE] * len(attn_pieces),
            [WHOLE] * 4,
            [attn_weights, pltpu.VMEM((padded, width), F32), attn_sems],
            (attn_place, tok, gains, summed, far, dmixed, qkv, probs, hidden, *attn_pieces),
            flops=20 * padded * width * width,
            moved=16 * MIB,
        )
        lows.append(low)
        dqkvs.append(dqkv)
        norm_parts.append(norm_grads)
        input_grads.append(input_grad)
    input_grad = jnp.stack(input_grads)

    parts = shards if ringed else 1
    grad_place = []
    for core in range(2):
        for row in range(2):
            if ringed:
                spots = [owner(steps, other) for other in range(2) for steps in range(lines)]
            else:
                spots = [jnp.int32(0)]
            for spot in spots:
                grad_place += [jnp.bitwise_xor(replica, 2 * row + core), spot]
    grad_place = jnp.stack(grad_place).astype(jnp.int32)
    keep, send = call(
        functools.partial(attention_weight_grads, halves, spans, extra, parts),
        [shaped((2, parts, spans + extra, width))] * 2,
        [SCALARS] + [WHOLE] * (5 * halves),
        [ANYWHERE] * 2,
        [
            pltpu.VMEM((4, width, width), BF),
            pltpu.VMEM((4, parts, max(extra, 16), width), BF),
            pltpu.SemaphoreType.DMA((8 * parts,)),
        ],
        (
            grad_place,
            *[kept[h][0] for h in range(halves)],
            *[kept[h][3] for h in range(halves)],
            *lows,
            *dqkvs,
            *norm_parts,
        ),
        flops=8 * halves * padded * width * width,
        moved=16 * MIB,
    )
    summed = add(keep, swap_core(send))
    summed = add(summed[0], swap_row(summed[1]))
    if ringed:
        summed = summed.reshape(2, lines, spans + extra, width)
        summed = add(summed[0], swap_side(summed[1]))
        current = summed[1 % lines]
        for steps in range(1, lines):
            current = add(step_line(current), summed[(steps + 1) % lines])
        attn_all = in_order(all_replicas(current))
        vector_grads = [part[rows, :rows].astype(F32) for part in attn_all]
    else:
        current = lax.psum_scatter(summed[0], "fsdp", scatter_dimension=0, tiled=True)
        attn_all = in_order(all_replicas(current))
        norm_sum = functools.reduce(jnp.add, norm_parts)
        norm_sum = lax.psum_scatter(norm_sum, "fsdp", scatter_dimension=1, tiled=True)
        vector_grads = list(lax.psum(norm_sum, "dp"))
    attn_all = [part[:rows].astype(F32) for part in attn_all]
    return (
        mixed,
        input_grad,
        vector_grads[0],
        vector_grads[1],
        jnp.concatenate(attn_all[:3], 1),
        attn_all[3],
        vector_grads[2],
        vector_grads[3],
        up_grad,
        down_grad,
        counts,
    )


def solution(mesh):
    return jax.shard_map(
        per_device,
        mesh=mesh,
        in_specs=(
            P(("fsdp", "dp"), None, None),
            P(("fsdp", "dp"), None),
            P(("fsdp", "dp"), None),
            P(("fsdp", "dp"), None, None),
            P("fsdp"),
            P("fsdp"),
            P("fsdp", None),
            P("fsdp", None),
            P("fsdp"),
            P("fsdp"),
            P(None, "fsdp", None),
            P(None, None, "fsdp"),
        ),
        out_specs=(
            P(("fsdp", "dp"), None, None),
            P(("fsdp", "dp"), None, None),
            P("fsdp"),
            P("fsdp"),
            P("fsdp", None),
            P("fsdp", None),
            P("fsdp"),
            P("fsdp"),
            P(None, "fsdp", None),
            P(None, None, "fsdp"),
            P(),
        ),
        check_vma=False,
    )
```

```python
import functools

import jax
import jax.numpy as jnp
from jax import lax
from jax.experimental import pallas as pl
from jax.experimental.pallas import tpu as pltpu
from jax.sharding import PartitionSpec as P

HEADS = 12
HEAD = 64
TILE = 256
PATCHES = 197
MIB = 1024 * 1024
BF = jnp.bfloat16
F32 = jnp.float32


def dot(left, right, left_dim=1, right_dim=0):
    return lax.dot_general(
        left, right, (((left_dim,), (right_dim,)), ((), ())), preferred_element_type=F32
    )


def moments(values):
    center = values - jnp.mean(values, -1, keepdims=True)
    inverse = lax.rsqrt(jnp.mean(center * center, -1, keepdims=True) + 1e-06)
    return center * inverse, inverse


def norm_backward(grad, unit, inverse, gain):
    scaled = grad * gain
    slope = jnp.mean(scaled * unit, -1, keepdims=True)
    result = inverse * (scaled - jnp.mean(scaled, -1, keepdims=True) - unit * slope)
    return result, jnp.sum(grad * unit, 0, keepdims=True), jnp.sum(grad, 0, keepdims=True)


def gelu_parts(pre):
    share = 0.5 + 0.5 * lax.erf(pre * 0.7071067811865476)
    density = jnp.exp(-0.5 * pre * pre) * 0.3989422804014327
    return pre * share, share + pre * density


def run_copies(copies):
    for copy in copies:
        copy.start()
    for copy in copies:
        copy.wait()


def tile(at):
    return pl.ds(pl.multiple_of(at * TILE, TILE), TILE)


def every(count, body):
    lax.fori_loop(0, count, lambda at, carry: (body(at), carry)[1], 0, unroll=3)


def start_copies(pairs, sems):
    copies = [
        pltpu.make_async_copy(source, target, sems.at[at])
        for at, (source, target) in enumerate(pairs)
    ]
    for copy in copies:
        copy.start()
    return copies


def wait_copies(copies):
    for copy in copies:
        copy.wait()


def gather_vectors(facts, count, rows, width):
    lane = lax.broadcasted_iota(jnp.int32, (8, width), 1)
    vectors = [jnp.zeros((8, width), F32)] * 4
    for owner in range(count):
        sent = facts[0, owner, 0:8].astype(F32)
        inside = (lane >= owner * rows) & (lane < (owner + 1) * rows)
        for at in range(4):
            shift = (owner - at) * rows % width
            moved = pltpu.roll(sent, shift, 1) if shift else sent
            row = jnp.broadcast_to(moved[0:1], (8, width))
            vectors[at] = jnp.where(inside, row, vectors[at])
    return jnp.concatenate([vector[0:1] for vector in vectors], 0)


def attention_forward(rows, length, pieces, place, tok, *refs):
    fresh = rows > 0
    if fresh:
        gains, refs = refs[-1], refs[:-1]
    else:
        gains, refs = refs[0], refs[1:]
    sources, refs = refs[:pieces], refs[pieces:]
    if fresh:
        step = rows + 16
        sources = [
            ref.at[pl.ds(first, step)] for ref in sources for first in range(0, ref.shape[0], step)
        ]
        pieces = len(sources)
    first_out, qkv_out, probs_out, context_out, hidden_out, second_out = refs[:6]
    if fresh:
        weights_out, facts_out, gains_out, refs = refs[6], refs[7], refs[8], refs[9:]
        facts, fact_sems, refs = refs[0], refs[1], refs[2:]
    else:
        refs = refs[6:]
    first_in, qkv, probs, context, hidden, second_in, weights, sems, out_sems = refs
    if fresh:
        fact_copies = [
            pltpu.make_async_copy(
                source.at[pl.ds(rows, 16)], facts.at[place[2 * at], place[2 * pieces + at]], fact_sems.at[at]
            )
            for at, source in enumerate(sources)
        ]
        for copy in fact_copies:
            copy.start()
        pairs = [
            (
                source.at[pl.ds(0, rows)],
                weights.at[place[2 * at], pl.ds(pl.multiple_of(place[2 * at + 1], 32), rows)],
            )
            for at, source in enumerate(sources)
        ]
    else:
        pairs = [(source, weights) for source in sources]
    copies = start_copies(pairs, sems)
    if fresh:
        wait_copies(fact_copies)
        shards = facts.shape[1]
        gains[...] = gather_vectors(facts, shards, rows, tok.shape[1])
        gains_out[...] = gains[...]
        fact_copy = pltpu.make_async_copy(facts, facts_out, fact_sems.at[0])
        fact_copy.start()
    inputs = tok[...].astype(F32)
    padded, width = inputs.shape
    tiles = width // TILE
    unit, _ = moments(inputs)
    first_in[...] = (unit * gains[0:1] + gains[1:2]).astype(BF)
    wait_copies(copies)
    results = [pltpu.make_async_copy(first_in, first_out, out_sems.at[0])]
    results[0].start()
    if fresh:
        results.append(pltpu.make_async_copy(weights, weights_out, out_sems.at[6]))
        results[-1].start()
        results.append(fact_copy)

    def project(at):
        block = weights[at // tiles, :, tile(at % tiles)]
        qkv[:, tile(at)] = dot(first_in[...], block).astype(BF)

    every(3 * tiles, project)
    results.append(pltpu.make_async_copy(qkv, qkv_out, out_sems.at[1]))
    results[-1].start()
    pair = 2 * HEAD
    low_half = lax.broadcasted_iota(jnp.int32, (padded, pair), 1) < HEAD
    real = lax.broadcasted_iota(jnp.int32, (padded, padded), 1) < length

    def heads(at):
        lanes = pl.multiple_of(at * pair, pair)
        query = qkv[:, pl.ds(lanes, pair)]
        key = qkv[:, pl.ds(width + lanes, pair)]
        value = qkv[:, pl.ds(2 * width + lanes, pair)]
        total = jnp.zeros((padded, pair), F32)
        for half in range(2):
            keep = low_half if half == 0 else jnp.logical_not(low_half)
            scores = dot(jnp.where(keep, query, 0), key, 1, 1) * HEAD ** (-0.5)
            scores = jnp.where(real, scores, -1e30)
            grown = jnp.exp(scores - jnp.max(scores, -1, keepdims=True))
            prob = (grown / jnp.sum(grown, -1, keepdims=True)).astype(BF)
            probs[2 * at + half] = prob
            total += dot(prob, jnp.where(keep, value, 0))
        context[:, pl.ds(lanes, pair)] = total.astype(BF)

    every(HEADS // 2, heads)
    results.append(pltpu.make_async_copy(probs, probs_out, out_sems.at[2]))
    results[-1].start()
    results.append(pltpu.make_async_copy(context, context_out, out_sems.at[3]))
    results[-1].start()

    def project_out(at):
        added = dot(context[...], weights[3, :, tile(at)])
        hidden[:, tile(at)] = tok[:, tile(at)].astype(F32) + added

    every(tiles, project_out)
    results.append(pltpu.make_async_copy(hidden, hidden_out, out_sems.at[4]))
    results[-1].start()
    unit, _ = moments(hidden[...])
    second_in[...] = (unit * gains[2:3] + gains[3:4]).astype(BF)
    results.append(pltpu.make_async_copy(second_in, second_out, out_sems.at[5]))
    results[-1].start()
    wait_copies(results)


def block_copies(sources, target, sems, main, tail):
    left = sources[0].shape[0] - tail
    pairs = [
        (source.at[pl.ds(tail, left)], target.at[0, pl.ds(at * left, left)])
        for at, source in enumerate(sources)
    ]
    pairs += [(source.at[pl.ds(0, main)], target.at[1 + at]) for at, source in enumerate(sources)]
    return [
        pltpu.make_async_copy(source, there, sems.at[at])
        for at, (source, there) in enumerate(pairs)
    ]


def expert_copies(place, pieces, weights, sems):
    copies = []
    for at, piece in enumerate(pieces):
        first = pl.multiple_of(place[at], 32)
        copies.append(
            pltpu.make_async_copy(
                piece, weights.at[:, pl.ds(first, piece.shape[1])], sems.at[at]
            )
        )
    return copies


def expert_layer(half, main, tail, place, kinds, *refs):
    states, grads = refs[:4], refs[4:8]
    pieces, refs = refs[8:-21], refs[-21:]
    act_out, dpre_out = refs[:2]
    results = refs[2:6]
    weights, state, grad, act, dpre, state_end, grad_end, *held = refs[6:]
    sems, state_sems, grad_sems, out_sems, held = held[-4], held[-3], held[-2], held[-1], held[:-4]
    width, hidden = weights.shape[1:]
    left = state_end.shape[0] // 4
    state_copies = block_copies(states, state, state_sems, main, tail)
    grad_copies = block_copies([ref.at[half] for ref in grads], grad, grad_sems, main, tail)
    copies = expert_copies(place, pieces, weights, sems)
    copies += state_copies[:4] + grad_copies[:4]
    for copy in copies + state_copies[4:] + grad_copies[4:]:
        copy.start()
    spare = main - 4 * left
    state[0, 4 * left :] = jnp.zeros((spare, width), BF)
    grad[0, 4 * left :] = jnp.zeros((spare, width), BF)
    wait_copies(copies)
    spot = lax.broadcasted_iota(jnp.int32, (main, 1), 0)
    image = spot < PATCHES
    text = (spot % left + tail >= PATCHES) & (spot < 4 * left)

    def forward(at, expert, mine):
        def body(step):
            columns = tile(step)
            pre = dot(state[at], weights[expert, :, columns])
            dact = dot(grad[at], weights[2 + expert, :, columns])
            value, slope = gelu_parts(pre)
            act[at, :, columns] = jnp.where(mine, value, 0).astype(BF)
            dpre[at, :, columns] = jnp.where(mine, dact * slope, 0).astype(BF)

        every(hidden // TILE, body)

    forward(0, 0, text)
    outs = []
    for index, (source, target) in enumerate(((act, act_out), (dpre, dpre_out))):
        outs.append(pltpu.make_async_copy(source.at[0], target.at[0], out_sems.at[index]))
        outs[-1].start()

    def end_body(step):
        columns = tile(step)
        rows = pl.ds(0, 4 * left)
        grad_end[:, columns] = dot(dpre[0, rows], weights[0, columns], 1, 1).astype(BF)
        state_end[:, columns] = dot(act[0, rows], weights[2, columns], 1, 1).astype(BF)

    every(width // TILE, end_body)
    for rel in range(4):
        at = rel + 1
        expert = kinds[rel]
        state_copies[4 + rel].wait()
        grad_copies[4 + rel].wait()
        forward(at, expert, image)
        for index, (source, target) in enumerate(((act, act_out), (dpre, dpre_out))):
            outs.append(
                pltpu.make_async_copy(source.at[at], target.at[at], out_sems.at[2 * at + index])
            )
            outs[-1].start()
        grad_to, out_to = held[rel % 2], held[2 + rel % 2]
        place_at = rel // 2
        end = rel * left

        def body(step):
            columns = tile(step)
            there = pl.ds(0, main)
            for source, weight, target, ends in (
                (dpre, weights.at[expert], grad_to, grad_end),
                (act, weights.at[2 + expert], out_to, state_end),
            ):
                value = dot(source[at], weight[columns], 1, 1)
                target[place_at, 0:tail, columns] = value[:tail].astype(BF)
                shared = ends[end : end + main - tail, columns].astype(F32)
                target[place_at, tail:main, columns] = (value[tail:] + shared).astype(BF)
                target[place_at, main:, columns] = ends[end + main - tail : end + left, columns]

        every(width // TILE, body)
    for index, (source, target) in enumerate(zip(held, results)):
        outs.append(pltpu.make_async_copy(source, target, out_sems.at[10 + index]))
        outs[-1].start()
    wait_copies(outs)


def expert_weight_grads(main, tail, halves, pieces, place, kinds, *refs):
    states, refs = refs[: 4 * halves], refs[4 * halves :]
    grads, refs = refs[:4], refs[4:]
    acts, refs = refs[:halves], refs[halves:]
    dpres, refs = refs[:halves], refs[halves:]
    outs, rest = refs[:pieces], refs[pieces:]
    total, rounded, state, grad, act, dpre, sems, state_sems, grad_sems, rest_sems = rest
    width, hidden = total.shape[1:]
    left = states[0].shape[0] - tail
    ready = []
    for half in range(halves):
        there = pl.ds(5 * half, 5)
        moves = block_copies(
            states[4 * half : 4 * half + 4], state.at[there], state_sems.at[half], main, tail
        )
        grad_moves = block_copies(
            [ref.at[half] for ref in grads], grad.at[there], grad_sems.at[half], main, tail
        )
        for block in range(5):
            spot = 5 * half + block
            needed = [
                pltpu.make_async_copy(
                    acts[half].at[block], act.at[spot], rest_sems.at[half, block, 0]
                ),
                pltpu.make_async_copy(
                    dpres[half].at[block], dpre.at[spot], rest_sems.at[half, block, 1]
                ),
            ]
            chosen = slice(0, 4) if block == 0 else slice(3 + block, 4 + block)
            needed += moves[chosen] + grad_moves[chosen]
            ready.append(needed)
    for needed in ready:
        for copy in needed:
            copy.start()
    spare = main - 4 * left
    for half in range(halves):
        state[5 * half, 4 * left :] = jnp.zeros((spare, width), BF)
        grad[5 * half, 4 * left :] = jnp.zeros((spare, width), BF)
    total[1] = jnp.zeros(total.shape[1:], F32)
    total[3] = jnp.zeros(total.shape[1:], F32)
    for at, needed in enumerate(ready):
        half, block = divmod(at, 5)
        expert = kinds[4 * half + block - 1] if block else 0
        wait_copies(needed)

        def body(step):
            columns = tile(step)
            up = dot(state[at, :, columns], dpre[at], 0, 0)
            down = dot(grad[at, :, columns], act[at], 0, 0)
            if at == 0:
                total[0, columns] = up
                total[2, columns] = down
            else:
                total[expert, columns] += up
                total[2 + expert, columns] += down

        every(width // TILE, body)
    rounded[...] = total[...].astype(BF)
    copies = []
    for at, out in enumerate(outs):
        first = pl.multiple_of(place[at], 32)
        copies.append(
            pltpu.make_async_copy(rounded.at[:, pl.ds(first, out.shape[1])], out, sems.at[at])
        )
    run_copies(copies)


def attention_backward(length, tok, gains, near, far, dmixed, hidden, *refs):
    qkv_from, probs_from, weights_from, refs = refs[0], refs[1], refs[2], refs[4:]
    low, dqkv, input_grad, norm_grads, qkv, probs, weights, total, sems = refs
    copies = start_copies(
        [(weights_from.at[pl.ds(3, 1)], weights.at[pl.ds(3, 1)])]
        + [(qkv_from, qkv), (probs_from, probs)]
        + [(weights_from.at[pl.ds(0, 3)], weights.at[pl.ds(0, 3)])],
        sems,
    )
    padded, width = tok.shape
    tiles = width // TILE
    unit, inverse = moments(hidden[...])
    second = near[...].astype(F32) + far[...].astype(F32)
    part, gain_two, bias_two = norm_backward(second, unit, inverse, gains[2:3])
    dhidden = dmixed[...].astype(F32) + part
    low[...] = dhidden.astype(BF)
    total[...] = dhidden
    norm_grads[2:3] = gain_two
    norm_grads[3:4] = bias_two
    copies[0].wait()

    def project_out(at):
        dqkv[:, tile(at)] = dot(low[...], weights[3, tile(at)], 1, 1).astype(BF)

    every(tiles, project_out)
    pair = 2 * HEAD
    low_half = lax.broadcasted_iota(jnp.int32, (padded, pair), 1) < HEAD
    copies[1].wait()
    copies[2].wait()

    def heads(at):
        lanes = pl.multiple_of(at * pair, pair)
        query = qkv[:, pl.ds(lanes, pair)]
        key = qkv[:, pl.ds(width + lanes, pair)]
        value = qkv[:, pl.ds(2 * width + lanes, pair)]
        upper = dqkv[:, pl.ds(lanes, pair)]
        dquery = jnp.zeros((padded, pair), F32)
        dkey = jnp.zeros((padded, pair), F32)
        dvalue = jnp.zeros((padded, pair), F32)
        for half in range(2):
            keep = low_half if half == 0 else jnp.logical_not(low_half)
            prob = probs[2 * at + half]
            wide = prob.astype(F32)
            upper_half = jnp.where(keep, upper, 0)
            dprob = dot(upper_half, value, 1, 1)
            dscore = (wide * (dprob - jnp.sum(dprob * wide, -1, keepdims=True))).astype(BF)
            dquery += dot(dscore, jnp.where(keep, key, 0))
            dkey += dot(dscore, jnp.where(keep, query, 0), 0, 0)
            dvalue += dot(prob, upper_half, 0, 0)
        dqkv[:, pl.ds(lanes, pair)] = (dquery * HEAD ** (-0.5)).astype(BF)
        dqkv[:, pl.ds(width + lanes, pair)] = (dkey * HEAD ** (-0.5)).astype(BF)
        dqkv[:, pl.ds(2 * width + lanes, pair)] = dvalue.astype(BF)

    every(HEADS // 2, heads)
    copies[3].wait()
    dfirst = []
    for at in range(tiles):
        columns = slice(at * TILE, (at + 1) * TILE)
        part = dot(dqkv[:, 0:width], weights[0, columns], 1, 1)
        part += dot(dqkv[:, width : 2 * width], weights[1, columns], 1, 1)
        part += dot(dqkv[:, 2 * width : 3 * width], weights[2, columns], 1, 1)
        dfirst.append(part)
    unit, inverse = moments(tok[...].astype(F32))
    part, gain_one, bias_one = norm_backward(
        jnp.concatenate(dfirst, 1), unit, inverse, gains[0:1]
    )
    norm_grads[0:1] = gain_one
    norm_grads[1:2] = bias_one
    input_grad[...] = (part + total[...])[:length]


def attention_weight_grads(halves, place, *refs):
    firsts, refs = refs[:halves], refs[halves:]
    contexts, refs = refs[:halves], refs[halves:]
    lows, refs = refs[:halves], refs[halves:]
    dqkvs, refs = refs[:halves], refs[halves:]
    norms, refs = refs[:halves], refs[halves:]
    keep, send, total, vectors, sems = refs
    width = firsts[0].shape[1]
    owners, _, rows, columns = total.shape
    part = width // 2
    group = owners // 2

    def project(step):
        which, chosen = step // 2, pl.ds(pl.multiple_of(step % 2 * part, 128), part)
        there = pl.ds(pl.multiple_of(which * width, width), width)
        value = dot(firsts[0][:, chosen], dqkvs[0][:, there], 0, 0)
        for first, dqkv in zip(firsts[1:], dqkvs[1:]):
            value += dot(first[:, chosen], dqkv[:, there], 0, 0)
        owner = pl.ds(step % 2 * group, group)
        total[owner, :, :, there] = value.astype(BF).reshape(group, 2, rows, width)

    def project_out(step):
        chosen = pl.ds(pl.multiple_of(step * part, 128), part)
        value = dot(contexts[0][:, chosen], lows[0][...], 0, 0)
        for context, low in zip(contexts[1:], lows[1:]):
            value += dot(context[:, chosen], low[...], 0, 0)
        owner = pl.ds(step * group, group)
        there = slice(3 * width, 4 * width)
        total[owner, :, :, there] = value.astype(BF).reshape(group, 2, rows, width)

    lax.fori_loop(0, 6, lambda at, carry: (project(at), carry)[1], 0, unroll=2)
    lax.fori_loop(0, 2, lambda at, carry: (project_out(at), carry)[1], 0)
    norm = norms[0][...]
    for ref in norms[1:]:
        norm += ref[...]
    vectors[...] = jnp.zeros(vectors.shape, BF)
    vectors[0:1, :width] = norm[0:1].astype(BF)
    vectors[0:1, width:] = norm[1:2].astype(BF)
    vectors[1:2, :width] = norm[2:3].astype(BF)
    vectors[1:2, width:] = norm[3:4].astype(BF)
    copies = []
    for side, target in enumerate((keep, send)):
        for row in range(2):
            first = pl.multiple_of(place[2 * row + 1], 128)
            copies.append(
                pltpu.make_async_copy(
                    total.at[:, place[2 * side], :, pl.ds(first, columns // 2)],
                    target.at[pl.ds(row * owners, owners)],
                    sems.at[len(copies)],
                )
            )
        copies.append(
            pltpu.make_async_copy(vectors, target.at[2 * owners], sems.at[len(copies)])
        )
    run_copies(copies)


ANYWHERE = pl.BlockSpec(memory_space=pl.ANY)
SCALARS = pl.BlockSpec(memory_space=pltpu.SMEM)
WHOLE = pl.BlockSpec(memory_space=pltpu.VMEM)


def one_of(array, index):
    tail = (0,) * (array.ndim - 1)
    return pl.BlockSpec((None,) + array.shape[1:], lambda step: (index,) + tail)


def shaped(shape, dtype=BF):
    return jax.ShapeDtypeStruct(shape, dtype)


def call(kernel, out_shape, in_specs, out_specs, scratch, args, time):
    return pl.pallas_call(
        kernel,
        grid=(1,),
        out_shape=out_shape,
        in_specs=in_specs,
        out_specs=out_specs,
        scratch_shapes=scratch,
        compiler_params=pltpu.CompilerParams(vmem_limit_bytes=60 * MIB),
        cost_estimate=pl.CostEstimate(
            flops=1024, bytes_accessed=int(1.5e6 * time), transcendentals=0
        ),
    )(*args)


def add(left, right):
    return (left.astype(F32) + right.astype(F32)).astype(BF)


def per_device(
    tokens,
    token_type,
    mlm_mask,
    cotangent,
    ln1_gain,
    ln1_bias,
    w_qkv,
    w_out,
    ln2_gain,
    ln2_bias,
    w_up,
    w_down,
):
    halves, length, width = tokens.shape
    shards, replicas = lax.axis_size("fsdp"), lax.axis_size("dp")
    shard, replica = lax.axis_index("fsdp"), lax.axis_index("dp")
    rows = width // shards
    lines = shards // 2
    line, side = shard // 2, shard % 2
    columns = w_up.shape[2] // replicas
    padded = -(-length // 16) * 16
    main = -(-PATCHES // 16) * 16
    tail = PATCHES // 16 * 16
    ringed = rows % 32 == 0 and lines == 4
    extra = 16 if ringed else 0
    spans = rows if ringed else width

    def swap(axis, size, bit):
        return lambda value: lax.ppermute(value, axis, [(i, i ^ bit) for i in range(size)])

    swap_core = swap("dp", replicas, 1)
    swap_row = swap("dp", replicas, 2)
    swap_side = swap("fsdp", shards, 1)

    def step_line(value):
        return lax.ppermute(value, "fsdp", [(i, (i + 2) % shards) for i in range(shards)])

    def all_replicas(value):
        across = swap_row(value)
        return jnp.stack([value, swap_core(value), across, swap_core(across)])

    def in_order(found):
        return [
            lax.dynamic_index_in_dim(found, jnp.bitwise_xor(replica, at), 0, keepdims=False)
            for at in range(4)
        ]

    def shift_line(value, steps):
        return lax.ppermute(value, "fsdp", [(i, (i + 2 * steps) % shards) for i in range(shards)])

    def cross(value):
        return lax.ppermute(
            value, "fsdp", [(i, ((i + 6) % shards) ^ 1) for i in range(shards)]
        )

    def owner(steps, other):
        return 2 * jnp.mod(line - steps, lines) + jnp.bitwise_xor(side, other)

    order = [(steps, other) for steps in range(lines) for other in range(2)]

    clock = [jnp.zeros((), jnp.int32)]

    def tied(value):
        return lax.optimization_barrier((value, clock[0]))[0]

    def wait(*values):
        found = lax.optimization_barrier((clock[0], *values))
        clock[0] = found[0]
        return found[1] if len(values) == 1 else found[1:]

    block = jnp.where(
        replica < 3,
        lax.dynamic_slice(w_qkv, (0, jnp.minimum(replica, 2) * width), (rows, width)),
        w_out,
    )
    vectors = jnp.stack([ln1_gain, ln1_bias, ln2_gain, ln2_bias])
    kinds_here = token_type[:, 0]
    image_counts = jnp.sum(mlm_mask * token_type, 1)
    text_counts = jnp.sum(mlm_mask, 1) - image_counts
    if ringed:
        facts = jnp.concatenate([kinds_here, text_counts, image_counts]).astype(BF)
        facts = jnp.concatenate([vectors.reshape(-1), facts])
        fact_row = jnp.zeros((extra, width), BF).at[0, : facts.shape[0]].set(facts)
        block = jnp.concatenate([block, fact_row], 0)
    expert_block = jnp.concatenate(
        [
            lax.dynamic_slice(w_up, (0, 0, replica * columns), (2, rows, columns)),
            lax.dynamic_slice(w_down, (0, replica * columns, 0), (2, columns, rows)).transpose(
                0, 2, 1
            ),
        ],
        0,
    )
    def pad_rows(value):
        return jnp.pad(value, ((0, 0), (0, padded - length), (0, 0)))

    if ringed:
        span = rows
        side_block = swap_side(block)
        ring = [shift_line(block, steps) for steps in range(1, lines)]
        row_block = swap_row(block)
        experts, near = [expert_block, step_line(expert_block)], [swap_side(expert_block)]
        dmixed = pad_rows(cotangent * mlm_mask[..., None].astype(BF))
        dmixed_row = swap_row(dmixed)
        wait(side_block, *ring, row_block)
        lined = jnp.concatenate([side_block, *ring], 0)
        side_ring = swap_side(tied(jnp.concatenate(ring, 0)))
        row_lined = swap_row(tied(lined))
        core_parts = [swap_core(tied(part)) for part in (block, row_block, lined)]
        wait(dmixed_row, near[0], *core_parts)
        grads = [dmixed, swap_core(tied(dmixed)), dmixed_row]
        tok = pad_rows(tied(tokens))
        wait(experts[1])
        experts.append(step_line(tied(experts[1])))
        wait(side_ring, row_lined, tok)
        row_side_ring = swap_row(tied(side_ring))
        near.append(swap_side(tied(experts[1])))
        core_parts += [swap_core(tied(part)) for part in (side_ring, row_lined)]
        wait(*core_parts[3:], grads[1])
        wait(experts[2])
        experts.append(step_line(tied(experts[2])))
        wait(row_side_ring)
        core_parts.append(swap_core(tied(row_side_ring)))
        wait(core_parts[5], near[1])
        near.append(swap_side(tied(experts[2])))
        first_line = [(0, 0)]
        later = [(steps, 0) for steps in range(1, lines)]
        later_sides = [(steps, 1) for steps in range(1, lines)]
        held = [
            (0, block, first_line),
            (0, lined, [(0, 1)] + later),
            (0, side_ring, later_sides),
            (2, row_block, first_line),
            (2, row_lined, [(0, 1)] + later),
            (2, row_side_ring, later_sides),
            (1, core_parts[0], first_line),
            (3, core_parts[1], first_line),
            (1, core_parts[2], [(0, 1)] + later),
            (1, core_parts[3], later_sides),
            (3, core_parts[4], [(0, 1)] + later),
            (3, core_parts[5], later_sides),
        ]
        attn_pieces = [part for _, part, _ in held]
        spots = [(rel, spot) for rel, _, spots_of in held for spot in spots_of]
        attn_place = jnp.stack(
            [
                value
                for rel, spot in spots
                for value in (jnp.bitwise_xor(replica, rel), owner(*spot) * rows)
            ]
            + [owner(*spot) for _, spot in spots]
        ).astype(jnp.int32)
        expert_place = jnp.stack([owner(*at) * rows for at in order]).astype(jnp.int32)
    else:
        span = 0
        whole = lax.all_gather(block, "fsdp", axis=0, tiled=True)
        attn_pieces = [jnp.stack(in_order(all_replicas(whole)))]
        attn_place = jnp.zeros((1,), jnp.int32)
        gains = lax.all_gather(vectors, "fsdp", axis=1, tiled=True).astype(F32)
        expert_pieces = [lax.all_gather(expert_block, "fsdp", axis=1, tiled=True)]
        expert_place = jnp.zeros((1,), jnp.int32)
        kinds = all_replicas(kinds_here).T
        counts = jnp.stack([jnp.sum(text_counts), jnp.sum(image_counts)])
        counts = lax.psum(counts, ("fsdp", "dp"))
        dmixed = pad_rows(cotangent * mlm_mask[..., None].astype(BF))
        tok = pad_rows(tokens)
        dmixed_row = swap_row(dmixed)
        grads = [dmixed, swap_core(dmixed), dmixed_row]
    attn_weights = pltpu.VMEM((4, width, width), BF)
    head_probs = pltpu.VMEM((HEADS, padded, padded), BF)
    states_of, kept = [], []
    for half in range(halves):
        fresh = ringed and half == 0
        sources = attn_pieces if half == 0 or not ringed else [all_weights]
        first_in, qkv, probs, context, hidden, second_in, *found = call(
            functools.partial(attention_forward, span if fresh else 0, length, len(sources)),
            [
                shaped((padded, width)),
                shaped((padded, 3 * width)),
                shaped((HEADS, padded, padded)),
                shaped((padded, width)),
                shaped((padded, width), F32),
                shaped((padded, width)),
            ]
            + [shaped((4, width, width)), shaped((4, shards, 16, width)), shaped((4, width), F32)]
            * fresh,
            [SCALARS, one_of(tok, half)] + [WHOLE] * (not fresh) + [ANYWHERE] * len(sources),
            [ANYWHERE] * 6 + [ANYWHERE, ANYWHERE, WHOLE] * fresh,
            [
                pltpu.VMEM((4, shards, 16, width), BF),
                pltpu.SemaphoreType.DMA((4 * shards,)),
            ]
            * fresh
            + [
                pltpu.VMEM((padded, width), BF),
                pltpu.VMEM((padded, 3 * width), BF),
                head_probs,
                pltpu.VMEM((padded, width), BF),
                pltpu.VMEM((padded, width), F32),
                pltpu.VMEM((padded, width), BF),
                attn_weights,
                pltpu.SemaphoreType.DMA((4 * shards,)),
                pltpu.SemaphoreType.DMA((7,)),
            ]
            + [pltpu.VMEM((4, width), F32)] * fresh,
            (tied(attn_place), tok, *([] if fresh else [gains]), *sources),
            time=9,
        )
        kept.append((first_in, qkv, probs, context, hidden))
        if half == 0:
            all_weights = attn_pieces[0]
            if ringed:
                all_weights, facts, gains = found
                wait(gains)
        if half == 0 or not ringed:
            states_of.append(
                [second_in, swap_core(tied(second_in)), swap_row(tied(second_in))]
            )
        if half == 0 and ringed:
            wait(experts[3], near[2], states_of[0][1])
            near.append(swap_side(tied(experts[3])))
    if ringed:
        wait(second_in, states_of[0][2], near[2], near[3])
        beside_core = swap_core(tied(second_in))
        grads.append(swap_core(tied(dmixed_row)))
        states_of[0].append(swap_core(tied(states_of[0][2])))
        wait(grads[3], beside_core, states_of[0][3])
        before_row = clock[0]
        states_of.append([second_in, beside_core, swap_row(tied(second_in))])
        numbers = facts[:, :, 0, 4 * rows : 4 * rows + 3 * halves].astype(F32)
        kinds = lax.dynamic_index_in_dim(numbers, shard, 1, keepdims=False)
        kinds = jnp.stack(
            [
                lax.dynamic_index_in_dim(kinds, jnp.bitwise_xor(replica, rel), 0, keepdims=False)
                for rel in range(4)
            ]
        )
        kinds = kinds[:, :halves].astype(jnp.int32).T
        counts = numbers.reshape(-1, 3, halves).sum((0, 2))[1:].astype(jnp.int32)
        expert_pieces = [part for both in zip(experts, near) for part in both]
        states_of[1].append(swap_core(states_of[1][2]))
    else:
        grads.append(swap_core(dmixed_row))
        for states in states_of:
            states.append(swap_core(states[2]))

    left = padded - tail
    expert_scratch = [
        pltpu.VMEM((4, width, columns), BF),
        *[pltpu.VMEM((5, main, width), BF)] * 2,
        *[pltpu.VMEM((5, main, columns), BF)] * 2,
        *[pltpu.VMEM((4 * left, width), BF)] * 2,
        *[pltpu.VMEM((2, padded, width), BF)] * 4,
        pltpu.SemaphoreType.DMA((len(expert_pieces),)),
        pltpu.SemaphoreType.DMA((8,)),
        pltpu.SemaphoreType.DMA((8,)),
        pltpu.SemaphoreType.DMA((14,)),
    ]
    acts, dpres, outs, arriving = [], [], [], []
    for half in range(halves):
        act, dpre, keep_grad, send_grad, keep_out, send_out = call(
            functools.partial(expert_layer, half, main, tail),
            [shaped((5, main, columns))] * 2 + [shaped((2, padded, width))] * 4,
            [SCALARS] * 2 + [ANYWHERE] * (8 + len(expert_pieces)),
            [ANYWHERE] * 6,
            expert_scratch,
            (tied(expert_place), kinds[half], *states_of[half], *grads, *expert_pieces),
            time=12.5,
        )
        acts.append(act)
        dpres.append(dpre)
        if half == 0:
            wait(states_of[1][2])
        else:
            wait(arriving[half - 1][1])
        summed = add(keep_grad, swap_core(tied(send_grad)))
        outs.append((keep_out, swap_core(tied(send_out))))
        if half + 1 < halves:
            wait(summed, outs[-1][1])
        arriving.append((summed, swap_row(summed[1])))

    piece_count = len(expert_pieces)
    expert_parts = call(
        functools.partial(expert_weight_grads, main, tail, halves, piece_count),
        [shaped((4, spans, columns))] * piece_count,
        [SCALARS] * 2 + [ANYWHERE] * (4 * halves + 4 + 2 * halves),
        [ANYWHERE] * piece_count,
        [
            pltpu.VMEM((4, width, columns), F32),
            pltpu.VMEM((4, width, columns), BF),
            *[pltpu.VMEM((5 * halves, main, width), BF)] * 2,
            *[pltpu.VMEM((5 * halves, main, columns), BF)] * 2,
            pltpu.SemaphoreType.DMA((piece_count,)),
            pltpu.SemaphoreType.DMA((halves, 8)),
            pltpu.SemaphoreType.DMA((halves, 8)),
            pltpu.SemaphoreType.DMA((halves, 5, 2)),
        ],
        (
            tied(expert_place),
            kinds.reshape(-1),
            *[state for states in states_of for state in states],
            *grads,
            *acts,
            *dpres,
        ),
        time=13.5,
    )

    wait(expert_parts[0])
    sent = {}

    def send_part(steps):
        if ringed:
            sent[steps] = swap_side(tied(expert_parts[2 * steps + 1]))

    def partly(steps):
        return add(expert_parts[2 * steps], wait(sent[steps]))

    send_part(1)
    wait(outs[-1][1])
    out_sum = jnp.stack([add(*pair) for pair in outs])
    out_rest = None
    lows, dqkvs, norm_parts, input_grads = [], [], [], []
    for half in range(halves):
        first_in, qkv, probs, context, hidden = kept[half]
        summed, far = arriving[half]
        low, dqkv, input_grad, norm_grads = call(
            functools.partial(attention_backward, length),
            [
                shaped((padded, width)),
                shaped((padded, 3 * width)),
                shaped((length, width), F32),
                shaped((4, width), F32),
            ],
            [one_of(tok, half), WHOLE, one_of(summed, 0), WHOLE, one_of(dmixed, half), WHOLE]
            + [ANYWHERE] * 4,
            [WHOLE] * 4,
            [
                pltpu.VMEM((padded, 3 * width), BF),
                head_probs,
                attn_weights,
                pltpu.VMEM((padded, width), F32),
                pltpu.SemaphoreType.DMA((4,)),
            ],
            (tok, tied(gains), summed, far, dmixed, hidden, qkv, probs, all_weights, expert_parts[0]),
            time=10,
        )
        wait(norm_grads)
        if half == 0:
            wait(arriving[1][1])
            out_rest = swap_row(tied(out_sum[:, 1]))
            if ringed:
                current = step_line(tied(partly(1)))
                send_part(2)
        lows.append(low)
        dqkvs.append(dqkv)
        norm_parts.append(norm_grads)
        input_grads.append(input_grad)
    input_grad = jnp.stack(input_grads)

    core, row = replica % 2, replica // 2
    grad_place = jnp.stack([core, row * 2 * width, 1 - core, (1 - row) * 2 * width])
    grad_place = grad_place.astype(jnp.int32)
    owners = shards if ringed else 2
    core_rows = width // (2 * owners)
    keep, send = call(
        functools.partial(attention_weight_grads, halves),
        [shaped((2 * owners + 1, core_rows, 2 * width))] * 2,
        [SCALARS] + [WHOLE] * (5 * halves),
        [ANYWHERE] * 2,
        [
            pltpu.VMEM((owners, 2, core_rows, 4 * width), BF),
            pltpu.VMEM((core_rows, 2 * width), BF),
            pltpu.SemaphoreType.DMA((6,)),
        ],
        (
            tied(grad_place),
            *[kept[h][0] for h in range(halves)],
            *[kept[h][3] for h in range(halves)],
            *lows,
            *dqkvs,
            *norm_parts,
        ),
        time=8.5,
    )
    wait(keep, out_rest)
    if ringed:
        ready = add(wait(current), partly(2))
    received = swap_core(tied(send))
    divisor = counts.astype(F32)[:, None, None]

    def join_replicas(value, axis, row_axis):
        across = swap_row(value)
        mine, other = value, swap_core(value)
        far, far_other = across, swap_core(across)
        near_parts = jnp.where(core == 0, mine, other), jnp.where(core == 0, other, mine)
        far_parts = jnp.where(core == 0, far, far_other), jnp.where(core == 0, far_other, far)
        near_part = jnp.concatenate(near_parts, axis)
        far_part = jnp.concatenate(far_parts, axis)
        return jnp.concatenate(
            [jnp.where(row == 0, near_part, far_part), jnp.where(row == 0, far_part, near_part)],
            row_axis,
        )

    if ringed:
        half_shards = shards // 2
        current = step_line(tied(ready))
        send_part(3)
        summed = add(keep, wait(received))
        mine, theirs = summed[:shards], summed[shards:-1]
        vector_block = summed[-1, :8]

        def by_side(value, other):
            pairs_of = value.reshape(-1, 2, *value.shape[1:])
            return lax.dynamic_index_in_dim(
                pairs_of, jnp.bitwise_xor(side, other), 1, keepdims=False
            )

        def with_vectors(value):
            return jnp.concatenate([value.reshape(-1, 2 * width), vector_block], 0)

        def split_vectors(value):
            return value[:-8].reshape(-1, core_rows, 2 * width), value[-8:]

        first_sent = swap_row(tied(with_vectors(theirs[:half_shards])))
        both = jnp.concatenate([mine[half_shards:], theirs[half_shards:]], 0)
        second_sent = swap_side(tied(by_side(both, 1)))
        current = step_line(tied(add(wait(current), partly(3))))
        send_part(0)
        first_done, vectors_done = split_vectors(wait(first_sent))
        first = add(mine[:half_shards], first_done)
        vector_block = add(vector_block, vectors_done)
        first_next = swap_side(tied(with_vectors(by_side(first, 1))))
        second = add(by_side(both, 0), wait(second_sent))
        middle = lines // 2
        second_next = swap_row(tied(second[middle:]))
        first_last, vectors_done = split_vectors(wait(first_next))
        first = add(by_side(first, 0), first_last)
        vector_block = add(vector_block, vectors_done)
        second = add(second[:middle], wait(second_next))
        lined = jnp.concatenate([first, second], 0)

        def lined_block(steps):
            return with_vectors(
                lax.dynamic_index_in_dim(lined, jnp.mod(line - steps, lines), 0)
            )

        expert_mine = add(wait(current), partly(0))
        expert_all = all_replicas(tied(expert_mine))
        arrived = [
            shift_line(tied(lined_block(steps)), lines - steps) for steps in range(1, lines)
        ]
        wait(*arrived)
        reduced = sum([part.astype(F32) for part in arrived], lined_block(0).astype(F32))
        vectors_sum = reduced[core_rows : core_rows + 2].reshape(4, width)
        vectors_sum = lax.dynamic_slice_in_dim(vectors_sum, shard * rows, rows, 1)
        attn_mine = reduced[:core_rows].astype(BF)
        attn_grad = join_replicas(tied(attn_mine), 0, 1)
    else:
        summed = add(keep, received)
        mine = add(summed[:owners], swap_row(summed[owners:-1]))
        attn_grad = join_replicas(mine, 1, 2).reshape(width, 4 * width)
        attn_grad = lax.psum_scatter(attn_grad, "fsdp", scatter_dimension=0, tiled=True)
        vectors_sum = functools.reduce(jnp.add, norm_parts)
        vectors_sum = lax.psum_scatter(vectors_sum, "fsdp", scatter_dimension=1, tiled=True)
        vectors_sum = lax.psum(vectors_sum, "dp")
        expert_mine = lax.psum_scatter(
            expert_parts[0], "fsdp", scatter_dimension=1, tiled=True
        )
        expert_all = all_replicas(expert_mine)
    expert_all = in_order(expert_all)
    up_grad = jnp.concatenate([part[:2] for part in expert_all], 2).astype(F32) / divisor
    down_grad = (
        jnp.concatenate([part[2:] for part in expert_all], 2).astype(F32).transpose(0, 2, 1)
        / divisor
    )
    mixed = jnp.stack(
        [
            (kept[h][4] + out_sum[h, 0].astype(F32) + out_rest[h].astype(F32))[:length]
            for h in range(halves)
        ]
    ).astype(BF)
    vector_grads = [vectors_sum[at] for at in range(4)]
    attn_grad = attn_grad.astype(F32)
    return (
        mixed,
        input_grad,
        vector_grads[0],
        vector_grads[1],
        attn_grad[:, : 3 * width],
        attn_grad[:, 3 * width :],
        vector_grads[2],
        vector_grads[3],
        up_grad,
        down_grad,
        counts,
    )


def solution(mesh):
    return jax.shard_map(
        per_device,
        mesh=mesh,
        in_specs=(
            P(("fsdp", "dp"), None, None),
            P(("fsdp", "dp"), None),
            P(("fsdp", "dp"), None),
            P(("fsdp", "dp"), None, None),
            P("fsdp"),
            P("fsdp"),
            P("fsdp", None),
            P("fsdp", None),
            P("fsdp"),
            P("fsdp"),
            P(None, "fsdp", None),
            P(None, None, "fsdp"),
        ),
        out_specs=(
            P(("fsdp", "dp"), None, None),
            P(("fsdp", "dp"), None, None),
            P("fsdp"),
            P("fsdp"),
            P("fsdp", None),
            P("fsdp", None),
            P("fsdp"),
            P("fsdp"),
            P(None, "fsdp", None),
            P(None, None, "fsdp"),
            P(),
        ),
        check_vma=False,
    )
```

```python
import functools

import jax
import jax.numpy as jnp
from jax import lax
from jax.experimental import pallas as pl
from jax.experimental.pallas import tpu as pltpu
from jax.sharding import PartitionSpec as P

HEADS = 12
HEAD = 64
TILE = 256
WINDOW = 3
PATCHES = 197
MIB = 1024 * 1024
BF = jnp.bfloat16
F32 = jnp.float32


def dot(left, right, left_dim=1, right_dim=0):
    return lax.dot_general(
        left, right, (((left_dim,), (right_dim,)), ((), ())), preferred_element_type=F32
    )


def moments(values):
    center = values - jnp.mean(values, -1, keepdims=True)
    inverse = lax.rsqrt(jnp.mean(center * center, -1, keepdims=True) + 1e-06)
    return center * inverse, inverse


def norm_backward(grad, unit, inverse, gain):
    scaled = grad * gain
    slope = jnp.mean(scaled * unit, -1, keepdims=True)
    result = inverse * (scaled - jnp.mean(scaled, -1, keepdims=True) - unit * slope)
    return result, jnp.sum(grad * unit, 0, keepdims=True), jnp.sum(grad, 0, keepdims=True)


def gelu_parts(pre):
    share = 0.5 + 0.5 * lax.erf(pre * 0.7071067811865476)
    density = jnp.exp(-0.5 * pre * pre) * 0.3989422804014327
    return pre * share, share + pre * density


def run_copies(copies):
    for copy in copies:
        copy.start()
    for copy in copies:
        copy.wait()


def tile(at):
    return pl.ds(pl.multiple_of(at * TILE, TILE), TILE)


def every(count, body):
    lax.fori_loop(0, count, lambda at, carry: (body(at), carry)[1], 0, unroll=3)


def start_copies(pairs, sems):
    copies = [
        pltpu.make_async_copy(source, target, sems.at[at])
        for at, (source, target) in enumerate(pairs)
    ]
    for copy in copies:
        copy.start()
    return copies


def wait_copies(copies):
    for copy in copies:
        copy.wait()


def gather_vectors(facts, count, rows, width):
    lane = lax.broadcasted_iota(jnp.int32, (8, width), 1)
    vectors = [jnp.zeros((8, width), F32)] * 4
    for owner in range(count):
        sent = facts[0, owner, 0:8].astype(F32)
        inside = (lane >= owner * rows) & (lane < (owner + 1) * rows)
        for at in range(4):
            shift = (owner - at) * rows % width
            moved = pltpu.roll(sent, shift, 1) if shift else sent
            row = jnp.broadcast_to(moved[0:1], (8, width))
            vectors[at] = jnp.where(inside, row, vectors[at])
    return jnp.concatenate([vector[0:1] for vector in vectors], 0)


def attention_forward(rows, length, pieces, place, tok, *refs):
    fresh = rows > 0
    if fresh:
        gains, refs = refs[-1], refs[:-1]
    else:
        gains, refs = refs[0], refs[1:]
    sources, refs = refs[:pieces], refs[pieces:]
    if fresh:
        step = rows + 16
        sources = [
            ref.at[pl.ds(first, step)] for ref in sources for first in range(0, ref.shape[0], step)
        ]
        pieces = len(sources)
    first_out, qkv_out, probs_out, context_out, hidden_out, second_out = refs[:6]
    if fresh:
        weights_out, facts_out, gains_out, refs = refs[6], refs[7], refs[8], refs[9:]
        facts, fact_sems, refs = refs[0], refs[1], refs[2:]
    else:
        refs = refs[6:]
    first_in, qkv, probs, context, hidden, second_in, weights, sems, out_sems = refs
    if fresh:
        fact_copies = [
            pltpu.make_async_copy(
                source.at[pl.ds(rows, 16)], facts.at[place[2 * at], place[2 * pieces + at]], fact_sems.at[at]
            )
            for at, source in enumerate(sources)
        ]
        for copy in fact_copies:
            copy.start()
        pairs = [
            (
                source.at[pl.ds(0, rows)],
                weights.at[place[2 * at], pl.ds(pl.multiple_of(place[2 * at + 1], 32), rows)],
            )
            for at, source in enumerate(sources)
        ]
    else:
        pairs = [(source, weights) for source in sources]
    copies = start_copies(pairs, sems)
    if fresh:
        wait_copies(fact_copies)
        shards = facts.shape[1]
        gains[...] = gather_vectors(facts, shards, rows, tok.shape[1])
        gains_out[...] = gains[...]
        fact_copy = pltpu.make_async_copy(facts, facts_out, fact_sems.at[0])
        fact_copy.start()
    inputs = tok[...].astype(F32)
    padded, width = inputs.shape
    tiles = width // TILE
    unit, _ = moments(inputs)
    first_in[...] = (unit * gains[0:1] + gains[1:2]).astype(BF)
    wait_copies(copies)
    results = [pltpu.make_async_copy(first_in, first_out, out_sems.at[0])]
    results[0].start()
    if fresh:
        results.append(pltpu.make_async_copy(weights, weights_out, out_sems.at[6]))
        results[-1].start()
        results.append(fact_copy)

    def project(at):
        block = weights[at // tiles, :, tile(at % tiles)]
        qkv[:, tile(at)] = dot(first_in[...], block).astype(BF)

    every(3 * tiles, project)
    results.append(pltpu.make_async_copy(qkv, qkv_out, out_sems.at[1]))
    results[-1].start()
    pair = 2 * HEAD
    low_half = lax.broadcasted_iota(jnp.int32, (padded, pair), 1) < HEAD
    real = lax.broadcasted_iota(jnp.int32, (padded, padded), 1) < length

    def heads(at):
        lanes = pl.multiple_of(at * pair, pair)
        query = qkv[:, pl.ds(lanes, pair)]
        key = qkv[:, pl.ds(width + lanes, pair)]
        value = qkv[:, pl.ds(2 * width + lanes, pair)]
        total = jnp.zeros((padded, pair), F32)
        for half in range(2):
            keep = low_half if half == 0 else jnp.logical_not(low_half)
            scores = dot(jnp.where(keep, query, 0), key, 1, 1) * HEAD ** (-0.5)
            scores = jnp.where(real, scores, -1e30)
            grown = jnp.exp(scores - jnp.max(scores, -1, keepdims=True))
            prob = (grown / jnp.sum(grown, -1, keepdims=True)).astype(BF)
            probs[2 * at + half] = prob
            total += dot(prob, jnp.where(keep, value, 0))
        context[:, pl.ds(lanes, pair)] = total.astype(BF)

    every(HEADS // 2, heads)
    results.append(pltpu.make_async_copy(probs, probs_out, out_sems.at[2]))
    results[-1].start()
    results.append(pltpu.make_async_copy(context, context_out, out_sems.at[3]))
    results[-1].start()

    def project_out(at):
        added = dot(context[...], weights[3, :, tile(at)])
        hidden[:, tile(at)] = tok[:, tile(at)].astype(F32) + added

    every(tiles, project_out)
    results.append(pltpu.make_async_copy(hidden, hidden_out, out_sems.at[4]))
    results[-1].start()
    unit, _ = moments(hidden[...])
    second_in[...] = (unit * gains[2:3] + gains[3:4]).astype(BF)
    results.append(pltpu.make_async_copy(second_in, second_out, out_sems.at[5]))
    results[-1].start()
    wait_copies(results)


def block_copies(sources, target, sems, main, tail):
    left = sources[0].shape[0] - tail
    pairs = [
        (source.at[pl.ds(tail, left)], target.at[0, pl.ds(at * left, left)])
        for at, source in enumerate(sources)
    ]
    pairs += [(source.at[pl.ds(0, main)], target.at[1 + at]) for at, source in enumerate(sources)]
    return [
        pltpu.make_async_copy(source, there, sems.at[at])
        for at, (source, there) in enumerate(pairs)
    ]


def expert_copies(place, pieces, weights, sems):
    copies = []
    for at, piece in enumerate(pieces):
        first = pl.multiple_of(place[at], 32)
        copies.append(
            pltpu.make_async_copy(
                piece, weights.at[:, pl.ds(first, piece.shape[1])], sems.at[at]
            )
        )
    return copies


def expert_layer(half, main, tail, place, kinds, *refs):
    states, grads = refs[:4], refs[4:8]
    pieces, refs = refs[8:-21], refs[-21:]
    act_out, dpre_out = refs[:2]
    results = refs[2:6]
    weights, state, grad, act, dpre, state_end, grad_end, *held = refs[6:]
    sems, state_sems, grad_sems, out_sems, held = held[-4], held[-3], held[-2], held[-1], held[:-4]
    width, hidden = weights.shape[1:]
    left = state_end.shape[0] // 4
    state_copies = block_copies(states, state, state_sems, main, tail)
    grad_copies = block_copies([ref.at[half] for ref in grads], grad, grad_sems, main, tail)
    copies = expert_copies(place, pieces, weights, sems)
    copies += state_copies[:4] + grad_copies[:4]
    for copy in copies:
        copy.start()
    spare = main - 4 * left
    state[0, 4 * left :] = jnp.zeros((spare, width), BF)
    grad[0, 4 * left :] = jnp.zeros((spare, width), BF)
    wait_copies(copies)
    for copy in state_copies[4:] + grad_copies[4:]:
        copy.start()
    spot = lax.broadcasted_iota(jnp.int32, (main, 1), 0)
    image = spot < PATCHES
    text = (spot % left + tail >= PATCHES) & (spot < 4 * left)

    def forward(at, expert, mine):
        def body(step):
            columns = tile(step)
            pre = dot(state[at], weights[expert, :, columns])
            dact = dot(grad[at], weights[2 + expert, :, columns])
            value, slope = gelu_parts(pre)
            act[at, :, columns] = jnp.where(mine, value, 0).astype(BF)
            dpre[at, :, columns] = jnp.where(mine, dact * slope, 0).astype(BF)

        every(hidden // TILE, body)

    forward(0, 0, text)
    outs = []
    for index, (source, target) in enumerate(((act, act_out), (dpre, dpre_out))):
        outs.append(pltpu.make_async_copy(source.at[0], target.at[0], out_sems.at[index]))
        outs[-1].start()

    def end_body(step):
        columns = tile(step)
        rows = pl.ds(0, 4 * left)
        grad_end[:, columns] = dot(dpre[0, rows], weights[0, columns], 1, 1).astype(BF)
        state_end[:, columns] = dot(act[0, rows], weights[2, columns], 1, 1).astype(BF)

    every(width // TILE, end_body)
    for rel in range(4):
        at = rel + 1
        expert = kinds[rel]
        state_copies[4 + rel].wait()
        grad_copies[4 + rel].wait()
        forward(at, expert, image)
        for index, (source, target) in enumerate(((act, act_out), (dpre, dpre_out))):
            outs.append(
                pltpu.make_async_copy(source.at[at], target.at[at], out_sems.at[2 * at + index])
            )
            outs[-1].start()
        grad_to, out_to = held[rel % 2], held[2 + rel % 2]
        place_at = rel // 2
        end = rel * left

        def body(step):
            columns = tile(step)
            there = pl.ds(0, main)
            for source, weight, target, ends in (
                (dpre, weights.at[expert], grad_to, grad_end),
                (act, weights.at[2 + expert], out_to, state_end),
            ):
                value = dot(source[at], weight[columns], 1, 1)
                target[place_at, 0:tail, columns] = value[:tail].astype(BF)
                shared = ends[end : end + main - tail, columns].astype(F32)
                target[place_at, tail:main, columns] = (value[tail:] + shared).astype(BF)
                target[place_at, main:, columns] = ends[end + main - tail : end + left, columns]

        every(width // TILE, body)
    for index, (source, target) in enumerate(zip(held, results)):
        outs.append(pltpu.make_async_copy(source, target, out_sems.at[10 + index]))
        outs[-1].start()
    wait_copies(outs)


def expert_weight_grads(main, tail, halves, spots, place, kinds, *refs):
    states, refs = refs[: 4 * halves], refs[4 * halves :]
    grads, refs = refs[:4], refs[4:]
    acts, refs = refs[:halves], refs[halves:]
    dpres, refs = refs[:halves], refs[halves:]
    outs, rest = refs[:-10], refs[-10:]
    total, rounded, state, grad, act, dpre, sems, state_sems, grad_sems, rest_sems = rest
    width = total.shape[1]
    left = states[0].shape[0] - tail
    ready = []
    for half in range(halves):
        there = pl.ds(5 * half, 5)
        moves = block_copies(
            states[4 * half : 4 * half + 4], state.at[there], state_sems.at[half], main, tail
        )
        grad_moves = block_copies(
            [ref.at[half] for ref in grads], grad.at[there], grad_sems.at[half], main, tail
        )
        for block in range(5):
            spot = 5 * half + block
            needed = [
                pltpu.make_async_copy(
                    acts[half].at[block], act.at[spot], rest_sems.at[half, block, 0]
                ),
                pltpu.make_async_copy(
                    dpres[half].at[block], dpre.at[spot], rest_sems.at[half, block, 1]
                ),
            ]
            chosen = slice(0, 4) if block == 0 else slice(3 + block, 4 + block)
            needed += moves[chosen] + grad_moves[chosen]
            ready.append(needed)
    for needed in ready[:WINDOW]:
        for copy in needed:
            copy.start()
    spare = main - 4 * left
    for half in range(halves):
        state[5 * half, 4 * left :] = jnp.zeros((spare, width), BF)
        grad[5 * half, 4 * left :] = jnp.zeros((spare, width), BF)
    total[1] = jnp.zeros(total.shape[1:], F32)
    total[3] = jnp.zeros(total.shape[1:], F32)
    for at, needed in enumerate(ready):
        half, block = divmod(at, 5)
        expert = kinds[4 * half + block - 1] if block else 0
        for copy in (ready[at + WINDOW] if at + WINDOW < len(ready) else []):
            copy.start()
        wait_copies(needed)

        def body(step):
            columns = tile(step)
            up = dot(state[at, :, columns], dpre[at], 0, 0)
            down = dot(grad[at, :, columns], act[at], 0, 0)
            if at == 0:
                total[0, columns] = up
                total[2, columns] = down
            else:
                total[expert, columns] += up
                total[2 + expert, columns] += down

        every(width // TILE, body)
    copies = []
    for part in range(4):
        rounded[part] = total[part].astype(BF)
        for piece, (out, at) in enumerate(spots):
            first = pl.multiple_of(place[piece], 32)
            target = outs[out].at[at, part]
            copies.append(
                pltpu.make_async_copy(
                    rounded.at[part, pl.ds(first, target.shape[0])], target, sems.at[piece, part]
                )
            )
            copies[-1].start()
    wait_copies(copies)


def attention_backward(length, tok, gains, near, far, dmixed, hidden, *refs):
    qkv_from, probs_from, weights_from, refs = refs[0], refs[1], refs[2], refs[4:]
    low, dqkv, input_grad, norm_grads, qkv, probs, weights, total, sems = refs
    copies = start_copies(
        [(weights_from.at[pl.ds(3, 1)], weights.at[pl.ds(3, 1)])]
        + [(qkv_from, qkv), (probs_from, probs)]
        + [(weights_from.at[pl.ds(0, 3)], weights.at[pl.ds(0, 3)])],
        sems,
    )
    padded, width = tok.shape
    tiles = width // TILE
    unit, inverse = moments(hidden[...])
    second = near[...].astype(F32) + far[...].astype(F32)
    part, gain_two, bias_two = norm_backward(second, unit, inverse, gains[2:3])
    dhidden = dmixed[...].astype(F32) + part
    low[...] = dhidden.astype(BF)
    total[...] = dhidden
    norm_grads[2:3] = gain_two
    norm_grads[3:4] = bias_two
    copies[0].wait()

    def project_out(at):
        dqkv[:, tile(at)] = dot(low[...], weights[3, tile(at)], 1, 1).astype(BF)

    every(tiles, project_out)
    pair = 2 * HEAD
    low_half = lax.broadcasted_iota(jnp.int32, (padded, pair), 1) < HEAD
    copies[1].wait()
    copies[2].wait()

    def heads(at):
        lanes = pl.multiple_of(at * pair, pair)
        query = qkv[:, pl.ds(lanes, pair)]
        key = qkv[:, pl.ds(width + lanes, pair)]
        value = qkv[:, pl.ds(2 * width + lanes, pair)]
        upper = dqkv[:, pl.ds(lanes, pair)]
        dquery = jnp.zeros((padded, pair), F32)
        dkey = jnp.zeros((padded, pair), F32)
        dvalue = jnp.zeros((padded, pair), F32)
        for half in range(2):
            keep = low_half if half == 0 else jnp.logical_not(low_half)
            prob = probs[2 * at + half]
            wide = prob.astype(F32)
            upper_half = jnp.where(keep, upper, 0)
            dprob = dot(upper_half, value, 1, 1)
            dscore = (wide * (dprob - jnp.sum(dprob * wide, -1, keepdims=True))).astype(BF)
            dquery += dot(dscore, jnp.where(keep, key, 0))
            dkey += dot(dscore, jnp.where(keep, query, 0), 0, 0)
            dvalue += dot(prob, upper_half, 0, 0)
        dqkv[:, pl.ds(lanes, pair)] = (dquery * HEAD ** (-0.5)).astype(BF)
        dqkv[:, pl.ds(width + lanes, pair)] = (dkey * HEAD ** (-0.5)).astype(BF)
        dqkv[:, pl.ds(2 * width + lanes, pair)] = dvalue.astype(BF)

    every(HEADS // 2, heads)
    copies[3].wait()
    dfirst = []
    for at in range(tiles):
        columns = slice(at * TILE, (at + 1) * TILE)
        part = dot(dqkv[:, 0:width], weights[0, columns], 1, 1)
        part += dot(dqkv[:, width : 2 * width], weights[1, columns], 1, 1)
        part += dot(dqkv[:, 2 * width : 3 * width], weights[2, columns], 1, 1)
        dfirst.append(part)
    unit, inverse = moments(tok[...].astype(F32))
    part, gain_one, bias_one = norm_backward(
        jnp.concatenate(dfirst, 1), unit, inverse, gains[0:1]
    )
    norm_grads[0:1] = gain_one
    norm_grads[1:2] = bias_one
    input_grad[...] = (part + total[...])[:length]


def attention_weight_grads(halves, place, *refs):
    norms, refs = refs[:halves], refs[halves:]
    inputs, refs = refs[: 4 * halves], refs[4 * halves :]
    keep, *sends = refs[:5]
    first, context, low, dqkv, total, vectors, in_sems, sems = refs[5:]
    width = first.shape[2]
    owners, _, rows, columns = total.shape
    part = width // 2
    group = owners // 2
    moves = []
    for half in range(halves):
        for at, target in enumerate((first, dqkv, context, low)):
            source = inputs[halves * at + half]
            if at == 1:
                for which in range(3):
                    there = pl.ds(which * width, width)
                    pair = source.at[:, there], target.at[half, :, there]
                    moves.append((which, *pair))
            else:
                moves.append((0 if at == 0 else 2, source, target.at[half]))
    stages = [[], [], []]
    for at, (stage, source, target) in enumerate(moves):
        stages[stage].append(pltpu.make_async_copy(source, target, in_sems.at[at]))
    for copy in stages[0] + stages[1]:
        copy.start()
    norm = norms[0][...]
    for ref in norms[1:]:
        norm += ref[...]
    vectors[...] = jnp.zeros(vectors.shape, BF)
    vectors[0:1, :width] = norm[0:1].astype(BF)
    vectors[0:1, width:] = norm[1:2].astype(BF)
    vectors[1:2, :width] = norm[2:3].astype(BF)
    vectors[1:2, width:] = norm[3:4].astype(BF)

    def project(left, right, which):
        def body(step):
            chosen = pl.ds(pl.multiple_of(step * part, 128), part)
            there = pl.ds(which % 3 * width, width)
            value = dot(left[0, :, chosen], right[0, :, there], 0, 0)
            for half in range(1, halves):
                value += dot(left[half, :, chosen], right[half, :, there], 0, 0)
            owner = pl.ds(step * group, group)
            target = pl.ds(which * width, width)
            total[owner, :, :, target] = value.astype(BF).reshape(group, 2, rows, width)

        lax.fori_loop(0, 2, lambda at, carry: (body(at), carry)[1], 0, unroll=2)

    results = []

    def send(row):
        there = pl.ds(row * owners, owners)
        mine = pl.multiple_of(place[2 * row + 1], 128)
        pairs = [(total.at[:, place[0], :, pl.ds(mine, columns // 2)], keep.at[there])]
        for piece in range(2):
            some = pl.ds(piece * group, group)
            target = sends[2 * row + piece].at[pl.ds(0, group)]
            pairs.append((total.at[some, place[2], :, pl.ds(mine, columns // 2)], target))
        for source, target in pairs:
            results.append(pltpu.make_async_copy(source, target, sems.at[len(results)]))
            results[-1].start()

    wait_copies(stages[0])
    for copy in stages[2]:
        copy.start()
    project(first, dqkv, 0)
    wait_copies(stages[1])
    project(first, dqkv, 1)
    wait_copies(stages[2])
    project(first, dqkv, 2)
    project(context, low, 3)
    send(0)
    send(1)
    for source, target in ((vectors, keep.at[2 * owners]), (vectors, sends[3].at[group])):
        results.append(pltpu.make_async_copy(source, target, sems.at[len(results)]))
        results[-1].start()
    wait_copies(results)


ANYWHERE = pl.BlockSpec(memory_space=pl.ANY)
SCALARS = pl.BlockSpec(memory_space=pltpu.SMEM)
WHOLE = pl.BlockSpec(memory_space=pltpu.VMEM)


def one_of(array, index):
    tail = (0,) * (array.ndim - 1)
    return pl.BlockSpec((None,) + array.shape[1:], lambda step: (index,) + tail)


def shaped(shape, dtype=BF):
    return jax.ShapeDtypeStruct(shape, dtype)


def call(kernel, out_shape, in_specs, out_specs, scratch, args, time):
    return pl.pallas_call(
        kernel,
        grid=(1,),
        out_shape=out_shape,
        in_specs=in_specs,
        out_specs=out_specs,
        scratch_shapes=scratch,
        compiler_params=pltpu.CompilerParams(vmem_limit_bytes=60 * MIB),
        cost_estimate=pl.CostEstimate(
            flops=1024, bytes_accessed=int(1.5e6 * time), transcendentals=0
        ),
    )(*args)


def add(left, right):
    return (left.astype(F32) + right.astype(F32)).astype(BF)


def per_device(
    tokens,
    token_type,
    mlm_mask,
    cotangent,
    ln1_gain,
    ln1_bias,
    w_qkv,
    w_out,
    ln2_gain,
    ln2_bias,
    w_up,
    w_down,
):
    halves, length, width = tokens.shape
    shards, replicas = lax.axis_size("fsdp"), lax.axis_size("dp")
    shard, replica = lax.axis_index("fsdp"), lax.axis_index("dp")
    rows = width // shards
    lines = shards // 2
    line, side = shard // 2, shard % 2
    columns = w_up.shape[2] // replicas
    padded = -(-length // 16) * 16
    main = -(-PATCHES // 16) * 16
    tail = PATCHES // 16 * 16
    ringed = rows % 32 == 0 and lines == 4
    extra = 16 if ringed else 0
    spans = rows if ringed else width

    def swap(axis, size, bit):
        return lambda value: lax.ppermute(value, axis, [(i, i ^ bit) for i in range(size)])

    swap_core = swap("dp", replicas, 1)
    swap_row = swap("dp", replicas, 2)
    swap_side = swap("fsdp", shards, 1)

    def step_line(value):
        return lax.ppermute(value, "fsdp", [(i, (i + 2) % shards) for i in range(shards)])

    def all_replicas(value):
        across = swap_row(value)
        return jnp.stack([value, swap_core(value), across, swap_core(across)])

    def in_order(found):
        return [
            lax.dynamic_index_in_dim(found, jnp.bitwise_xor(replica, at), 0, keepdims=False)
            for at in range(4)
        ]

    def shift_line(value, steps):
        return lax.ppermute(value, "fsdp", [(i, (i + 2 * steps) % shards) for i in range(shards)])

    def cross(value):
        return lax.ppermute(
            value, "fsdp", [(i, ((i + 6) % shards) ^ 1) for i in range(shards)]
        )

    def owner(steps, other):
        return 2 * jnp.mod(line - steps, lines) + jnp.bitwise_xor(side, other)

    order = [(steps, other) for steps in range(lines) for other in range(2)]

    clock = [jnp.zeros((), jnp.int32)]

    def tied(value):
        return lax.optimization_barrier((value, clock[0]))[0]

    def wait(*values):
        found = lax.optimization_barrier((clock[0], *values))
        clock[0] = found[0]
        return found[1] if len(values) == 1 else found[1:]

    block = jnp.where(
        replica < 3,
        lax.dynamic_slice(w_qkv, (0, jnp.minimum(replica, 2) * width), (rows, width)),
        w_out,
    )
    vectors = jnp.stack([ln1_gain, ln1_bias, ln2_gain, ln2_bias])
    kinds_here = token_type[:, 0]
    image_counts = jnp.sum(mlm_mask * token_type, 1)
    text_counts = jnp.sum(mlm_mask, 1) - image_counts
    if ringed:
        facts = jnp.concatenate([kinds_here, text_counts, image_counts]).astype(BF)
        facts = jnp.concatenate([vectors.reshape(-1), facts])
        fact_row = jnp.zeros((extra, width), BF).at[0, : facts.shape[0]].set(facts)
        block = jnp.concatenate([block, fact_row], 0)
    expert_block = jnp.concatenate(
        [
            lax.dynamic_slice(w_up, (0, 0, replica * columns), (2, rows, columns)),
            lax.dynamic_slice(w_down, (0, replica * columns, 0), (2, columns, rows)).transpose(
                0, 2, 1
            ),
        ],
        0,
    )
    def pad_rows(value):
        return jnp.pad(value, ((0, 0), (0, padded - length), (0, 0)))

    if ringed:
        span = rows
        side_block = swap_side(block)
        ring = [shift_line(block, steps) for steps in range(1, lines)]
        row_block = swap_row(block)
        experts, near = [expert_block, step_line(expert_block)], [swap_side(expert_block)]
        dmixed = pad_rows(cotangent * mlm_mask[..., None].astype(BF))
        dmixed_row = swap_row(dmixed)
        wait(side_block, *ring, row_block)
        lined = jnp.concatenate([side_block, *ring], 0)
        side_ring = swap_side(tied(jnp.concatenate(ring, 0)))
        row_lined = swap_row(tied(lined))
        core_parts = [swap_core(tied(part)) for part in (block, row_block, lined)]
        wait(dmixed_row, near[0], *core_parts)
        grads = [dmixed, swap_core(tied(dmixed)), dmixed_row]
        tok = pad_rows(tied(tokens))
        wait(experts[1])
        experts.append(step_line(tied(experts[1])))
        wait(side_ring, row_lined, tok)
        row_side_ring = swap_row(tied(side_ring))
        near.append(swap_side(tied(experts[1])))
        core_parts += [swap_core(tied(part)) for part in (side_ring, row_lined)]
        wait(*core_parts[3:], grads[1])
        wait(experts[2])
        experts.append(step_line(tied(experts[2])))
        wait(row_side_ring)
        core_parts.append(swap_core(tied(row_side_ring)))
        wait(core_parts[5], near[1])
        near.append(swap_side(tied(experts[2])))
        first_line = [(0, 0)]
        later = [(steps, 0) for steps in range(1, lines)]
        later_sides = [(steps, 1) for steps in range(1, lines)]
        held = [
            (0, block, first_line),
            (0, lined, [(0, 1)] + later),
            (0, side_ring, later_sides),
            (2, row_block, first_line),
            (2, row_lined, [(0, 1)] + later),
            (2, row_side_ring, later_sides),
            (1, core_parts[0], first_line),
            (3, core_parts[1], first_line),
            (1, core_parts[2], [(0, 1)] + later),
            (1, core_parts[3], later_sides),
            (3, core_parts[4], [(0, 1)] + later),
            (3, core_parts[5], later_sides),
        ]
        attn_pieces = [part for _, part, _ in held]
        spots = [(rel, spot) for rel, _, spots_of in held for spot in spots_of]
        attn_place = jnp.stack(
            [
                value
                for rel, spot in spots
                for value in (jnp.bitwise_xor(replica, rel), owner(*spot) * rows)
            ]
            + [owner(*spot) for _, spot in spots]
        ).astype(jnp.int32)
        expert_place = jnp.stack([owner(*at) * rows for at in order]).astype(jnp.int32)
    else:
        span = 0
        whole = lax.all_gather(block, "fsdp", axis=0, tiled=True)
        attn_pieces = [jnp.stack(in_order(all_replicas(whole)))]
        attn_place = jnp.zeros((1,), jnp.int32)
        gains = lax.all_gather(vectors, "fsdp", axis=1, tiled=True).astype(F32)
        expert_pieces = [lax.all_gather(expert_block, "fsdp", axis=1, tiled=True)]
        expert_place = jnp.zeros((1,), jnp.int32)
        kinds = all_replicas(kinds_here).T
        counts = jnp.stack([jnp.sum(text_counts), jnp.sum(image_counts)])
        counts = lax.psum(counts, ("fsdp", "dp"))
        dmixed = pad_rows(cotangent * mlm_mask[..., None].astype(BF))
        tok = pad_rows(tokens)
        dmixed_row = swap_row(dmixed)
        grads = [dmixed, swap_core(dmixed), dmixed_row]
    attn_weights = pltpu.VMEM((4, width, width), BF)
    head_probs = pltpu.VMEM((HEADS, padded, padded), BF)
    states_of, kept = [], []
    for half in range(halves):
        fresh = ringed and half == 0
        sources = attn_pieces if half == 0 or not ringed else [all_weights]
        first_in, qkv, probs, context, hidden, second_in, *found = call(
            functools.partial(attention_forward, span if fresh else 0, length, len(sources)),
            [
                shaped((padded, width)),
                shaped((padded, 3 * width)),
                shaped((HEADS, padded, padded)),
                shaped((padded, width)),
                shaped((padded, width), F32),
                shaped((padded, width)),
            ]
            + [shaped((4, width, width)), shaped((4, shards, 16, width)), shaped((4, width), F32)]
            * fresh,
            [SCALARS, one_of(tok, half)] + [WHOLE] * (not fresh) + [ANYWHERE] * len(sources),
            [ANYWHERE] * 6 + [ANYWHERE, ANYWHERE, WHOLE] * fresh,
            [
                pltpu.VMEM((4, shards, 16, width), BF),
                pltpu.SemaphoreType.DMA((4 * shards,)),
            ]
            * fresh
            + [
                pltpu.VMEM((padded, width), BF),
                pltpu.VMEM((padded, 3 * width), BF),
                head_probs,
                pltpu.VMEM((padded, width), BF),
                pltpu.VMEM((padded, width), F32),
                pltpu.VMEM((padded, width), BF),
                attn_weights,
                pltpu.SemaphoreType.DMA((4 * shards,)),
                pltpu.SemaphoreType.DMA((7,)),
            ]
            + [pltpu.VMEM((4, width), F32)] * fresh,
            (tied(attn_place), tok, *([] if fresh else [gains]), *sources),
            time=9,
        )
        kept.append((first_in, qkv, probs, context, hidden))
        if half == 0:
            all_weights = attn_pieces[0]
            if ringed:
                all_weights, facts, gains = found
                wait(gains)
        if half == 0 or not ringed:
            states_of.append(
                [second_in, swap_core(tied(second_in)), swap_row(tied(second_in))]
            )
        if half == 0 and ringed:
            wait(experts[3], near[2], states_of[0][1])
            near.append(swap_side(tied(experts[3])))
    if ringed:
        wait(second_in, states_of[0][2], near[2], near[3])
        beside_core = swap_core(tied(second_in))
        grads.append(swap_core(tied(dmixed_row)))
        states_of[0].append(swap_core(tied(states_of[0][2])))
        wait(grads[3], beside_core, states_of[0][3])
        before_row = clock[0]
        states_of.append([second_in, beside_core, swap_row(tied(second_in))])
        numbers = facts[:, :, 0, 4 * rows : 4 * rows + 3 * halves].astype(F32)
        kinds = lax.dynamic_index_in_dim(numbers, shard, 1, keepdims=False)
        kinds = jnp.stack(
            [
                lax.dynamic_index_in_dim(kinds, jnp.bitwise_xor(replica, rel), 0, keepdims=False)
                for rel in range(4)
            ]
        )
        kinds = kinds[:, :halves].astype(jnp.int32).T
        counts = numbers.reshape(-1, 3, halves).sum((0, 2))[1:].astype(jnp.int32)
        expert_pieces = [part for both in zip(experts, near) for part in both]
        states_of[1].append(swap_core(states_of[1][2]))
    else:
        grads.append(swap_core(dmixed_row))
        for states in states_of:
            states.append(swap_core(states[2]))

    left = padded - tail
    expert_scratch = [
        pltpu.VMEM((4, width, columns), BF),
        *[pltpu.VMEM((5, main, width), BF)] * 2,
        *[pltpu.VMEM((5, main, columns), BF)] * 2,
        *[pltpu.VMEM((4 * left, width), BF)] * 2,
        *[pltpu.VMEM((2, padded, width), BF)] * 4,
        pltpu.SemaphoreType.DMA((len(expert_pieces),)),
        pltpu.SemaphoreType.DMA((8,)),
        pltpu.SemaphoreType.DMA((8,)),
        pltpu.SemaphoreType.DMA((14,)),
    ]
    acts, dpres, outs, arriving = [], [], [], []
    for half in range(halves):
        act, dpre, keep_grad, send_grad, keep_out, send_out = call(
            functools.partial(expert_layer, half, main, tail),
            [shaped((5, main, columns))] * 2 + [shaped((2, padded, width))] * 4,
            [SCALARS] * 2 + [ANYWHERE] * (8 + len(expert_pieces)),
            [ANYWHERE] * 6,
            expert_scratch,
            (tied(expert_place), kinds[half], *states_of[half], *grads, *expert_pieces),
            time=12.5,
        )
        acts.append(act)
        dpres.append(dpre)
        if half == 0:
            wait(states_of[1][2])
        else:
            wait(arriving[half - 1][1])
        summed = add(keep_grad, swap_core(tied(send_grad)))
        outs.append((keep_out, swap_core(tied(send_out))))
        if half + 1 < halves:
            wait(summed, outs[-1][1])
        arriving.append((summed, swap_row(summed[1])))

    piece_count = len(expert_pieces)
    if ringed:
        spots = [
            (steps, 0) if other == 0 else {1: (4, 0), 2: (5, 0), 3: (6, 0), 0: (6, 1)}[steps]
            for steps, other in order
        ]
        grad_sizes = [1, 1, 1, 1, 1, 1, 2]
    else:
        spots, grad_sizes = [(0, 0)], [1]
    expert_parts = call(
        functools.partial(expert_weight_grads, main, tail, halves, spots),
        [shaped((size, 4, spans, columns)) for size in grad_sizes],
        [SCALARS] * 2 + [ANYWHERE] * (4 * halves + 4 + 2 * halves),
        [ANYWHERE] * len(grad_sizes),
        [
            pltpu.VMEM((4, width, columns), F32),
            pltpu.VMEM((4, width, columns), BF),
            *[pltpu.VMEM((5 * halves, main, width), BF)] * 2,
            *[pltpu.VMEM((5 * halves, main, columns), BF)] * 2,
            pltpu.SemaphoreType.DMA((piece_count, 4)),
            pltpu.SemaphoreType.DMA((halves, 8)),
            pltpu.SemaphoreType.DMA((halves, 8)),
            pltpu.SemaphoreType.DMA((halves, 5, 2)),
        ],
        (
            tied(expert_place),
            kinds.reshape(-1),
            *[state for states in states_of for state in states],
            *grads,
            *acts,
            *dpres,
        ),
        time=13.5,
    )

    wait(expert_parts[0])
    if ringed:
        sent_one = swap_side(tied(expert_parts[4]))
    wait(outs[-1][1])
    out_sum = jnp.stack([add(*pair) for pair in outs])
    out_rest = None
    lows, dqkvs, norm_parts, input_grads = [], [], [], []
    for half in range(halves):
        first_in, qkv, probs, context, hidden = kept[half]
        summed, far = arriving[half]
        low, dqkv, input_grad, norm_grads = call(
            functools.partial(attention_backward, length),
            [
                shaped((padded, width)),
                shaped((padded, 3 * width)),
                shaped((length, width), F32),
                shaped((4, width), F32),
            ],
            [one_of(tok, half), WHOLE, one_of(summed, 0), WHOLE, one_of(dmixed, half), WHOLE]
            + [ANYWHERE] * 4,
            [WHOLE] * 4,
            [
                pltpu.VMEM((padded, 3 * width), BF),
                head_probs,
                attn_weights,
                pltpu.VMEM((padded, width), F32),
                pltpu.SemaphoreType.DMA((4,)),
            ],
            (tok, tied(gains), summed, far, dmixed, hidden, qkv, probs, all_weights, expert_parts[0]),
            time=10,
        )
        wait(norm_grads)
        if half == 0:
            wait(arriving[1][1])
            out_rest = swap_row(tied(out_sum[:, 1]))
            if ringed:
                current = step_line(tied(add(expert_parts[1], wait(sent_one))))
                sent_two = swap_side(tied(expert_parts[5]))
        elif ringed:
            sent_rest = swap_side(tied(expert_parts[6]))
        lows.append(low)
        dqkvs.append(dqkv)
        norm_parts.append(norm_grads)
        input_grads.append(input_grad)
    input_grad = jnp.stack(input_grads)

    core, row = replica % 2, replica // 2
    grad_place = jnp.stack([core, row * 2 * width, 1 - core, (1 - row) * 2 * width])
    grad_place = grad_place.astype(jnp.int32)
    owners = shards if ringed else 2
    core_rows = width // (2 * owners)
    keep, *sends = call(
        functools.partial(attention_weight_grads, halves),
        [
            shaped((size, core_rows, 2 * width))
            for size in (2 * owners + 1, *[owners // 2] * 3, owners // 2 + 1)
        ],
        [SCALARS] + [WHOLE] * halves + [ANYWHERE] * (4 * halves),
        [ANYWHERE] * 5,
        [
            *[pltpu.VMEM((halves, padded, width), BF)] * 3,
            pltpu.VMEM((halves, padded, 3 * width), BF),
            pltpu.VMEM((owners, 2, core_rows, 4 * width), BF),
            pltpu.VMEM((core_rows, 2 * width), BF),
            pltpu.SemaphoreType.DMA((6 * halves,)),
            pltpu.SemaphoreType.DMA((8,)),
        ],
        (
            tied(grad_place),
            *norm_parts,
            *[kept[h][0] for h in range(halves)],
            *dqkvs,
            *[kept[h][3] for h in range(halves)],
            *lows,
        ),
        time=8.5,
    )
    wait(keep, out_rest)
    if ringed:
        ready = add(wait(current), add(expert_parts[2], wait(sent_two)))
    received = [swap_core(tied(part)) for part in sends]
    divisor = counts.astype(F32)[:, None, None]

    def join_replicas(value, axis, row_axis):
        across = swap_row(value)
        mine, other = value, swap_core(value)
        far, far_other = across, swap_core(across)
        near_parts = jnp.where(core == 0, mine, other), jnp.where(core == 0, other, mine)
        far_parts = jnp.where(core == 0, far, far_other), jnp.where(core == 0, far_other, far)
        near_part = jnp.concatenate(near_parts, axis)
        far_part = jnp.concatenate(far_parts, axis)
        return jnp.concatenate(
            [jnp.where(row == 0, near_part, far_part), jnp.where(row == 0, far_part, near_part)],
            row_axis,
        )

    if ringed:
        current = step_line(tied(ready))
        received = wait(*received)
        half_shards = shards // 2
        mine = add(keep[:shards], jnp.concatenate(received[:2], 0))
        theirs = add(keep[shards:-1], jnp.concatenate([received[2], received[3][:-1]], 0))
        vector_block = add(keep[-1, :8], received[3][-1, :8])

        def by_side(value, other):
            pairs_of = value.reshape(-1, 2, *value.shape[1:])
            return lax.dynamic_index_in_dim(
                pairs_of, jnp.bitwise_xor(side, other), 1, keepdims=False
            )

        def with_vectors(value):
            return jnp.concatenate([value.reshape(-1, 2 * width), vector_block], 0)

        def split_vectors(value):
            return value[:-8].reshape(-1, core_rows, 2 * width), value[-8:]

        first_sent = swap_row(tied(with_vectors(theirs[:half_shards])))
        both = jnp.concatenate([mine[half_shards:], theirs[half_shards:]], 0)
        second_sent = swap_side(tied(by_side(both, 1)))
        rest_part = wait(sent_rest)
        current = add(wait(current), add(expert_parts[3], rest_part[0:1]))
        current = step_line(tied(current))
        first_done, second_done = wait(first_sent, second_sent)
        first_done, vectors_done = split_vectors(first_done)
        first = add(mine[:half_shards], first_done)
        vector_block = add(vector_block, vectors_done)
        first_next = swap_side(tied(with_vectors(by_side(first, 1))))
        second = add(by_side(both, 0), second_done)
        middle = lines // 2
        second_next = swap_row(tied(second[middle:]))
        first_last, second_last = wait(first_next, second_next)
        first_last, vectors_done = split_vectors(first_last)
        first = add(by_side(first, 0), first_last)
        vector_block = add(vector_block, vectors_done)
        second = add(second[:middle], second_last)
        lined = jnp.concatenate([first, second], 0)

        def lined_block(steps):
            return with_vectors(
                lax.dynamic_index_in_dim(lined, jnp.mod(line - steps, lines), 0)
            )

        expert_mine = add(wait(current), add(expert_parts[0], rest_part[1:2]))[0]
        expert_all = all_replicas(tied(expert_mine))
        arrived = [
            shift_line(tied(lined_block(steps)), lines - steps) for steps in range(1, lines)
        ]
        wait(*arrived)
        reduced = sum([part.astype(F32) for part in arrived], lined_block(0).astype(F32))
        vectors_sum = reduced[core_rows : core_rows + 2].reshape(4, width)
        vectors_sum = lax.dynamic_slice_in_dim(vectors_sum, shard * rows, rows, 1)
        attn_mine = reduced[:core_rows].astype(BF)
        attn_grad = join_replicas(tied(attn_mine), 0, 1)
    else:
        summed = add(keep, jnp.concatenate(received, 0))
        mine = add(summed[:owners], swap_row(summed[owners:-1]))
        attn_grad = join_replicas(mine, 1, 2).reshape(width, 4 * width)
        attn_grad = lax.psum_scatter(attn_grad, "fsdp", scatter_dimension=0, tiled=True)
        vectors_sum = functools.reduce(jnp.add, norm_parts)
        vectors_sum = lax.psum_scatter(vectors_sum, "fsdp", scatter_dimension=1, tiled=True)
        vectors_sum = lax.psum(vectors_sum, "dp")
        expert_mine = lax.psum_scatter(
            expert_parts[0][0], "fsdp", scatter_dimension=1, tiled=True
        )
        expert_all = all_replicas(expert_mine)
    expert_all = in_order(expert_all)
    up_grad = jnp.concatenate([part[:2] for part in expert_all], 2).astype(F32) / divisor
    down_grad = (
        jnp.concatenate([part[2:] for part in expert_all], 2).astype(F32).transpose(0, 2, 1)
        / divisor
    )
    mixed = jnp.stack(
        [
            (kept[h][4] + out_sum[h, 0].astype(F32) + out_rest[h].astype(F32))[:length]
            for h in range(halves)
        ]
    ).astype(BF)
    vector_grads = [vectors_sum[at] for at in range(4)]
    attn_grad = attn_grad.astype(F32)
    return (
        mixed,
        input_grad,
        vector_grads[0],
        vector_grads[1],
        attn_grad[:, : 3 * width],
        attn_grad[:, 3 * width :],
        vector_grads[2],
        vector_grads[3],
        up_grad,
        down_grad,
        counts,
    )


def solution(mesh):
    return jax.shard_map(
        per_device,
        mesh=mesh,
        in_specs=(
            P(("fsdp", "dp"), None, None),
            P(("fsdp", "dp"), None),
            P(("fsdp", "dp"), None),
            P(("fsdp", "dp"), None, None),
            P("fsdp"),
            P("fsdp"),
            P("fsdp", None),
            P("fsdp", None),
            P("fsdp"),
            P("fsdp"),
            P(None, "fsdp", None),
            P(None, None, "fsdp"),
        ),
        out_specs=(
            P(("fsdp", "dp"), None, None),
            P(("fsdp", "dp"), None, None),
            P("fsdp"),
            P("fsdp"),
            P("fsdp", None),
            P("fsdp", None),
            P("fsdp"),
            P("fsdp"),
            P(None, "fsdp", None),
            P(None, None, "fsdp"),
            P(),
        ),
        check_vma=False,
    )
```

```python
import functools

import jax
import jax.numpy as jnp
from jax import lax
from jax.experimental import pallas as pl
from jax.experimental.pallas import tpu as pltpu
from jax.sharding import PartitionSpec as P

HEADS = 12
HEAD = 64
TILE = 256
WINDOW = 3
PATCHES = 197
MIB = 1024 * 1024
BF = jnp.bfloat16
F32 = jnp.float32


def dot(left, right, left_dim=1, right_dim=0):
    return lax.dot_general(
        left, right, (((left_dim,), (right_dim,)), ((), ())), preferred_element_type=F32
    )


def moments(values):
    center = values - jnp.mean(values, -1, keepdims=True)
    inverse = lax.rsqrt(jnp.mean(center * center, -1, keepdims=True) + 1e-06)
    return center * inverse, inverse


def norm_backward(grad, unit, inverse, gain):
    scaled = grad * gain
    slope = jnp.mean(scaled * unit, -1, keepdims=True)
    result = inverse * (scaled - jnp.mean(scaled, -1, keepdims=True) - unit * slope)
    return result, jnp.sum(grad * unit, 0, keepdims=True), jnp.sum(grad, 0, keepdims=True)


def gelu_parts(pre):
    share = 0.5 + 0.5 * lax.erf(pre * 0.7071067811865476)
    density = jnp.exp(-0.5 * pre * pre) * 0.3989422804014327
    return pre * share, share + pre * density


def run_copies(copies):
    for copy in copies:
        copy.start()
    for copy in copies:
        copy.wait()


def tile(at):
    return pl.ds(pl.multiple_of(at * TILE, TILE), TILE)


def every(count, body):
    lax.fori_loop(0, count, lambda at, carry: (body(at), carry)[1], 0, unroll=3)


def start_copies(pairs, sems):
    copies = [
        pltpu.make_async_copy(source, target, sems.at[at])
        for at, (source, target) in enumerate(pairs)
    ]
    for copy in copies:
        copy.start()
    return copies


def wait_copies(copies):
    for copy in copies:
        copy.wait()


def gather_vectors(facts, count, rows, width):
    lane = lax.broadcasted_iota(jnp.int32, (8, width), 1)
    vectors = [jnp.zeros((8, width), F32)] * 4
    for owner in range(count):
        sent = facts[0, owner, 0:8].astype(F32)
        inside = (lane >= owner * rows) & (lane < (owner + 1) * rows)
        for at in range(4):
            shift = (owner - at) * rows % width
            moved = pltpu.roll(sent, shift, 1) if shift else sent
            row = jnp.broadcast_to(moved[0:1], (8, width))
            vectors[at] = jnp.where(inside, row, vectors[at])
    return jnp.concatenate([vector[0:1] for vector in vectors], 0)


def attention_forward(rows, length, pieces, place, tok, *refs):
    fresh = rows > 0
    if fresh:
        gains, refs = refs[-1], refs[:-1]
    else:
        gains, refs = refs[0], refs[1:]
    sources, refs = refs[:pieces], refs[pieces:]
    if fresh:
        step = rows + 16
        sources = [
            ref.at[pl.ds(first, step)] for ref in sources for first in range(0, ref.shape[0], step)
        ]
        pieces = len(sources)
    first_out, qkv_out, probs_out, context_out, hidden_out, second_out = refs[:6]
    if fresh:
        weights_out, facts_out, gains_out, refs = refs[6], refs[7], refs[8], refs[9:]
        facts, fact_sems, refs = refs[0], refs[1], refs[2:]
    else:
        refs = refs[6:]
    first_in, qkv, probs, context, hidden, second_in, weights, sems, out_sems = refs
    if fresh:
        fact_copies = [
            pltpu.make_async_copy(
                source.at[pl.ds(rows, 16)], facts.at[place[2 * at], place[2 * pieces + at]], fact_sems.at[at]
            )
            for at, source in enumerate(sources)
        ]
        for copy in fact_copies:
            copy.start()
        pairs = [
            (
                source.at[pl.ds(0, rows)],
                weights.at[place[2 * at], pl.ds(pl.multiple_of(place[2 * at + 1], 32), rows)],
            )
            for at, source in enumerate(sources)
        ]
    else:
        pairs = [(source, weights) for source in sources]
    copies = start_copies(pairs, sems)
    if fresh:
        wait_copies(fact_copies)
        shards = facts.shape[1]
        gains[...] = gather_vectors(facts, shards, rows, tok.shape[1])
        gains_out[...] = gains[...]
        fact_copy = pltpu.make_async_copy(facts, facts_out, fact_sems.at[0])
        fact_copy.start()
    inputs = tok[...].astype(F32)
    padded, width = inputs.shape
    tiles = width // TILE
    unit, _ = moments(inputs)
    first_in[...] = (unit * gains[0:1] + gains[1:2]).astype(BF)
    wait_copies(copies)
    results = [pltpu.make_async_copy(first_in, first_out, out_sems.at[0])]
    results[0].start()
    if fresh:
        results.append(pltpu.make_async_copy(weights, weights_out, out_sems.at[6]))
        results[-1].start()
        results.append(fact_copy)

    def project(at):
        block = weights[at // tiles, :, tile(at % tiles)]
        qkv[:, tile(at)] = dot(first_in[...], block).astype(BF)

    every(3 * tiles, project)
    results.append(pltpu.make_async_copy(qkv, qkv_out, out_sems.at[1]))
    results[-1].start()
    pair = 2 * HEAD
    low_half = lax.broadcasted_iota(jnp.int32, (padded, pair), 1) < HEAD
    real = lax.broadcasted_iota(jnp.int32, (padded, padded), 1) < length

    def heads(at):
        lanes = pl.multiple_of(at * pair, pair)
        query = qkv[:, pl.ds(lanes, pair)]
        key = qkv[:, pl.ds(width + lanes, pair)]
        value = qkv[:, pl.ds(2 * width + lanes, pair)]
        total = jnp.zeros((padded, pair), F32)
        for half in range(2):
            keep = low_half if half == 0 else jnp.logical_not(low_half)
            scores = dot(jnp.where(keep, query, 0), key, 1, 1) * HEAD ** (-0.5)
            scores = jnp.where(real, scores, -1e30)
            grown = jnp.exp(scores - jnp.max(scores, -1, keepdims=True))
            prob = (grown / jnp.sum(grown, -1, keepdims=True)).astype(BF)
            probs[2 * at + half] = prob
            total += dot(prob, jnp.where(keep, value, 0))
        context[:, pl.ds(lanes, pair)] = total.astype(BF)

    every(HEADS // 2, heads)
    results.append(pltpu.make_async_copy(probs, probs_out, out_sems.at[2]))
    results[-1].start()
    results.append(pltpu.make_async_copy(context, context_out, out_sems.at[3]))
    results[-1].start()

    def project_out(at):
        added = dot(context[...], weights[3, :, tile(at)])
        hidden[:, tile(at)] = tok[:, tile(at)].astype(F32) + added

    every(tiles, project_out)
    results.append(pltpu.make_async_copy(hidden, hidden_out, out_sems.at[4]))
    results[-1].start()
    unit, _ = moments(hidden[...])
    second_in[...] = (unit * gains[2:3] + gains[3:4]).astype(BF)
    results.append(pltpu.make_async_copy(second_in, second_out, out_sems.at[5]))
    results[-1].start()
    wait_copies(results)


def block_copies(sources, target, sems, main, tail):
    left = sources[0].shape[0] - tail
    pairs = [
        (source.at[pl.ds(tail, left)], target.at[0, pl.ds(at * left, left)])
        for at, source in enumerate(sources)
    ]
    pairs += [(source.at[pl.ds(0, main)], target.at[1 + at]) for at, source in enumerate(sources)]
    return [
        pltpu.make_async_copy(source, there, sems.at[at])
        for at, (source, there) in enumerate(pairs)
    ]


def expert_copies(place, pieces, weights, sems):
    copies = []
    for at, piece in enumerate(pieces):
        first = pl.multiple_of(place[at], 32)
        copies.append(
            pltpu.make_async_copy(
                piece, weights.at[:, pl.ds(first, piece.shape[1])], sems.at[at]
            )
        )
    return copies


def expert_layer(half, main, tail, place, kinds, *refs):
    states, grads = refs[:4], refs[4:8]
    pieces, refs = refs[8:-21], refs[-21:]
    act_out, dpre_out = refs[:2]
    results = refs[2:6]
    weights, state, grad, act, dpre, state_end, grad_end, *held = refs[6:]
    sems, state_sems, grad_sems, out_sems, held = held[-4], held[-3], held[-2], held[-1], held[:-4]
    width, hidden = weights.shape[1:]
    left = state_end.shape[0] // 4
    state_copies = block_copies(states, state, state_sems, main, tail)
    grad_copies = block_copies([ref.at[half] for ref in grads], grad, grad_sems, main, tail)
    copies = expert_copies(place, pieces, weights, sems)
    copies += state_copies[:4] + grad_copies[:4]
    for copy in copies:
        copy.start()
    spare = main - 4 * left
    state[0, 4 * left :] = jnp.zeros((spare, width), BF)
    grad[0, 4 * left :] = jnp.zeros((spare, width), BF)
    wait_copies(copies)
    for copy in state_copies[4:] + grad_copies[4:]:
        copy.start()
    spot = lax.broadcasted_iota(jnp.int32, (main, 1), 0)
    image = spot < PATCHES
    text = (spot % left + tail >= PATCHES) & (spot < 4 * left)

    def forward(at, expert, mine):
        def body(step):
            columns = tile(step)
            pre = dot(state[at], weights[expert, :, columns])
            dact = dot(grad[at], weights[2 + expert, :, columns])
            value, slope = gelu_parts(pre)
            act[at, :, columns] = jnp.where(mine, value, 0).astype(BF)
            dpre[at, :, columns] = jnp.where(mine, dact * slope, 0).astype(BF)

        every(hidden // TILE, body)

    forward(0, 0, text)
    outs = []
    for index, (source, target) in enumerate(((act, act_out), (dpre, dpre_out))):
        outs.append(pltpu.make_async_copy(source.at[0], target.at[0], out_sems.at[index]))
        outs[-1].start()

    def end_body(step):
        columns = tile(step)
        rows = pl.ds(0, 4 * left)
        grad_end[:, columns] = dot(dpre[0, rows], weights[0, columns], 1, 1).astype(BF)
        state_end[:, columns] = dot(act[0, rows], weights[2, columns], 1, 1).astype(BF)

    every(width // TILE, end_body)
    for rel in range(4):
        at = rel + 1
        expert = kinds[rel]
        state_copies[4 + rel].wait()
        grad_copies[4 + rel].wait()
        forward(at, expert, image)
        for index, (source, target) in enumerate(((act, act_out), (dpre, dpre_out))):
            outs.append(
                pltpu.make_async_copy(source.at[at], target.at[at], out_sems.at[2 * at + index])
            )
            outs[-1].start()
        grad_to, out_to = held[rel % 2], held[2 + rel % 2]
        place_at = rel // 2
        end = rel * left

        def body(step):
            columns = tile(step)
            there = pl.ds(0, main)
            for source, weight, target, ends in (
                (dpre, weights.at[expert], grad_to, grad_end),
                (act, weights.at[2 + expert], out_to, state_end),
            ):
                value = dot(source[at], weight[columns], 1, 1)
                target[place_at, 0:tail, columns] = value[:tail].astype(BF)
                shared = ends[end : end + main - tail, columns].astype(F32)
                target[place_at, tail:main, columns] = (value[tail:] + shared).astype(BF)
                target[place_at, main:, columns] = ends[end + main - tail : end + left, columns]

        every(width // TILE, body)
    for index, (source, target) in enumerate(zip(held, results)):
        outs.append(pltpu.make_async_copy(source, target, out_sems.at[10 + index]))
        outs[-1].start()
    wait_copies(outs)


def expert_weight_grads(main, tail, halves, spots, place, kinds, *refs):
    states, refs = refs[: 4 * halves], refs[4 * halves :]
    grads, refs = refs[:4], refs[4:]
    acts, refs = refs[:halves], refs[halves:]
    dpres, refs = refs[:halves], refs[halves:]
    outs, rest = refs[:-10], refs[-10:]
    total, rounded, state, grad, act, dpre, sems, state_sems, grad_sems, rest_sems = rest
    width = total.shape[1]
    left = states[0].shape[0] - tail
    ready = []
    for half in range(halves):
        there = pl.ds(5 * half, 5)
        moves = block_copies(
            states[4 * half : 4 * half + 4], state.at[there], state_sems.at[half], main, tail
        )
        grad_moves = block_copies(
            [ref.at[half] for ref in grads], grad.at[there], grad_sems.at[half], main, tail
        )
        for block in range(5):
            spot = 5 * half + block
            needed = [
                pltpu.make_async_copy(
                    acts[half].at[block], act.at[spot], rest_sems.at[half, block, 0]
                ),
                pltpu.make_async_copy(
                    dpres[half].at[block], dpre.at[spot], rest_sems.at[half, block, 1]
                ),
            ]
            chosen = slice(0, 4) if block == 0 else slice(3 + block, 4 + block)
            needed += moves[chosen] + grad_moves[chosen]
            ready.append(needed)
    for needed in ready[:WINDOW]:
        for copy in needed:
            copy.start()
    spare = main - 4 * left
    for half in range(halves):
        state[5 * half, 4 * left :] = jnp.zeros((spare, width), BF)
        grad[5 * half, 4 * left :] = jnp.zeros((spare, width), BF)
    total[1] = jnp.zeros(total.shape[1:], F32)
    total[3] = jnp.zeros(total.shape[1:], F32)
    for at, needed in enumerate(ready):
        half, block = divmod(at, 5)
        expert = kinds[4 * half + block - 1] if block else 0
        for copy in (ready[at + WINDOW] if at + WINDOW < len(ready) else []):
            copy.start()
        wait_copies(needed)

        def body(step):
            columns = tile(step)
            up = dot(state[at, :, columns], dpre[at], 0, 0)
            down = dot(grad[at, :, columns], act[at], 0, 0)
            if at == 0:
                total[0, columns] = up
                total[2, columns] = down
            else:
                total[expert, columns] += up
                total[2 + expert, columns] += down

        every(width // TILE, body)
    copies = []
    for part in range(4):
        rounded[part] = total[part].astype(BF)
        for piece, (out, at) in enumerate(spots):
            first = pl.multiple_of(place[piece], 32)
            target = outs[out].at[at, part]
            copies.append(
                pltpu.make_async_copy(
                    rounded.at[part, pl.ds(first, target.shape[0])], target, sems.at[piece, part]
                )
            )
            copies[-1].start()
    wait_copies(copies)


def attention_backward(length, tok, gains, near, far, dmixed, hidden, *refs):
    qkv_from, probs_from, weights_from, refs = refs[0], refs[1], refs[2], refs[4:]
    low, dqkv, input_grad, norm_grads, qkv, probs, weights, total, sems = refs
    copies = start_copies(
        [(weights_from.at[pl.ds(3, 1)], weights.at[pl.ds(3, 1)])]
        + [(qkv_from, qkv), (probs_from, probs)]
        + [(weights_from.at[pl.ds(0, 3)], weights.at[pl.ds(0, 3)])],
        sems,
    )
    padded, width = tok.shape
    tiles = width // TILE
    unit, inverse = moments(hidden[...])
    second = near[...].astype(F32) + far[...].astype(F32)
    part, gain_two, bias_two = norm_backward(second, unit, inverse, gains[2:3])
    dhidden = dmixed[...].astype(F32) + part
    low[...] = dhidden.astype(BF)
    total[...] = dhidden
    norm_grads[2:3] = gain_two
    norm_grads[3:4] = bias_two
    copies[0].wait()

    def project_out(at):
        dqkv[:, tile(at)] = dot(low[...], weights[3, tile(at)], 1, 1).astype(BF)

    every(tiles, project_out)
    pair = 2 * HEAD
    low_half = lax.broadcasted_iota(jnp.int32, (padded, pair), 1) < HEAD
    copies[1].wait()
    copies[2].wait()

    def heads(at):
        lanes = pl.multiple_of(at * pair, pair)
        query = qkv[:, pl.ds(lanes, pair)]
        key = qkv[:, pl.ds(width + lanes, pair)]
        value = qkv[:, pl.ds(2 * width + lanes, pair)]
        upper = dqkv[:, pl.ds(lanes, pair)]
        dquery = jnp.zeros((padded, pair), F32)
        dkey = jnp.zeros((padded, pair), F32)
        dvalue = jnp.zeros((padded, pair), F32)
        for half in range(2):
            keep = low_half if half == 0 else jnp.logical_not(low_half)
            prob = probs[2 * at + half]
            wide = prob.astype(F32)
            upper_half = jnp.where(keep, upper, 0)
            dprob = dot(upper_half, value, 1, 1)
            dscore = (wide * (dprob - jnp.sum(dprob * wide, -1, keepdims=True))).astype(BF)
            dquery += dot(dscore, jnp.where(keep, key, 0))
            dkey += dot(dscore, jnp.where(keep, query, 0), 0, 0)
            dvalue += dot(prob, upper_half, 0, 0)
        dqkv[:, pl.ds(lanes, pair)] = (dquery * HEAD ** (-0.5)).astype(BF)
        dqkv[:, pl.ds(width + lanes, pair)] = (dkey * HEAD ** (-0.5)).astype(BF)
        dqkv[:, pl.ds(2 * width + lanes, pair)] = dvalue.astype(BF)

    every(HEADS // 2, heads)
    copies[3].wait()
    dfirst = []
    for at in range(tiles):
        columns = slice(at * TILE, (at + 1) * TILE)
        part = dot(dqkv[:, 0:width], weights[0, columns], 1, 1)
        part += dot(dqkv[:, width : 2 * width], weights[1, columns], 1, 1)
        part += dot(dqkv[:, 2 * width : 3 * width], weights[2, columns], 1, 1)
        dfirst.append(part)
    unit, inverse = moments(tok[...].astype(F32))
    part, gain_one, bias_one = norm_backward(
        jnp.concatenate(dfirst, 1), unit, inverse, gains[0:1]
    )
    norm_grads[0:1] = gain_one
    norm_grads[1:2] = bias_one
    input_grad[...] = (part + total[...])[:length]


def attention_weight_grads(halves, place, *refs):
    norms, refs = refs[:halves], refs[halves:]
    inputs, refs = refs[: 4 * halves], refs[4 * halves :]
    keep, *sends = refs[:5]
    first, context, low, dqkv, total, vectors, in_sems, sems = refs[5:]
    width = first.shape[2]
    owners, _, rows, columns = total.shape
    part = width // 2
    group = owners // 2
    moves = []
    for half in range(halves):
        for at, target in enumerate((first, dqkv, context, low)):
            source = inputs[halves * at + half]
            if at == 1:
                for which in range(3):
                    there = pl.ds(which * width, width)
                    pair = source.at[:, there], target.at[half, :, there]
                    moves.append((which, *pair))
            else:
                moves.append((0 if at == 0 else 2, source, target.at[half]))
    stages = [[], [], []]
    for at, (stage, source, target) in enumerate(moves):
        stages[stage].append(pltpu.make_async_copy(source, target, in_sems.at[at]))
    for copy in stages[0] + stages[1]:
        copy.start()
    norm = norms[0][...]
    for ref in norms[1:]:
        norm += ref[...]
    vectors[...] = jnp.zeros(vectors.shape, BF)
    vectors[0:1, :width] = norm[0:1].astype(BF)
    vectors[0:1, width:] = norm[1:2].astype(BF)
    vectors[1:2, :width] = norm[2:3].astype(BF)
    vectors[1:2, width:] = norm[3:4].astype(BF)

    def project(left, right, which):
        def body(step):
            chosen = pl.ds(pl.multiple_of(step * part, 128), part)
            there = pl.ds(which % 3 * width, width)
            value = dot(left[0, :, chosen], right[0, :, there], 0, 0)
            for half in range(1, halves):
                value += dot(left[half, :, chosen], right[half, :, there], 0, 0)
            owner = pl.ds(step * group, group)
            target = pl.ds(which * width, width)
            total[owner, :, :, target] = value.astype(BF).reshape(group, 2, rows, width)

        lax.fori_loop(0, 2, lambda at, carry: (body(at), carry)[1], 0, unroll=2)

    results = []

    def send(row):
        there = pl.ds(row * owners, owners)
        mine = pl.multiple_of(place[2 * row + 1], 128)
        pairs = [(total.at[:, place[0], :, pl.ds(mine, columns // 2)], keep.at[there])]
        for piece in range(2):
            some = pl.ds(piece * group, group)
            target = sends[2 * row + piece].at[pl.ds(0, group)]
            pairs.append((total.at[some, place[2], :, pl.ds(mine, columns // 2)], target))
        for source, target in pairs:
            results.append(pltpu.make_async_copy(source, target, sems.at[len(results)]))
            results[-1].start()

    wait_copies(stages[0])
    for copy in stages[2]:
        copy.start()
    project(first, dqkv, 0)
    wait_copies(stages[1])
    project(first, dqkv, 1)
    wait_copies(stages[2])
    project(first, dqkv, 2)
    project(context, low, 3)
    send(0)
    send(1)
    for source, target in ((vectors, keep.at[2 * owners]), (vectors, sends[3].at[group])):
        results.append(pltpu.make_async_copy(source, target, sems.at[len(results)]))
        results[-1].start()
    wait_copies(results)


ANYWHERE = pl.BlockSpec(memory_space=pl.ANY)
SCALARS = pl.BlockSpec(memory_space=pltpu.SMEM)
WHOLE = pl.BlockSpec(memory_space=pltpu.VMEM)


def one_of(array, index):
    tail = (0,) * (array.ndim - 1)
    return pl.BlockSpec((None,) + array.shape[1:], lambda step: (index,) + tail)


def shaped(shape, dtype=BF):
    return jax.ShapeDtypeStruct(shape, dtype)


def call(kernel, out_shape, in_specs, out_specs, scratch, args, time):
    return pl.pallas_call(
        kernel,
        grid=(1,),
        out_shape=out_shape,
        in_specs=in_specs,
        out_specs=out_specs,
        scratch_shapes=scratch,
        compiler_params=pltpu.CompilerParams(vmem_limit_bytes=60 * MIB),
        cost_estimate=pl.CostEstimate(
            flops=1024, bytes_accessed=int(1.5e6 * time), transcendentals=0
        ),
    )(*args)


def add(left, right):
    return (left.astype(F32) + right.astype(F32)).astype(BF)


def per_device(
    tokens,
    token_type,
    mlm_mask,
    cotangent,
    ln1_gain,
    ln1_bias,
    w_qkv,
    w_out,
    ln2_gain,
    ln2_bias,
    w_up,
    w_down,
):
    halves, length, width = tokens.shape
    shards, replicas = lax.axis_size("fsdp"), lax.axis_size("dp")
    shard, replica = lax.axis_index("fsdp"), lax.axis_index("dp")
    rows = width // shards
    lines = shards // 2
    line, side = shard // 2, shard % 2
    columns = w_up.shape[2] // replicas
    padded = -(-length // 16) * 16
    main = -(-PATCHES // 16) * 16
    tail = PATCHES // 16 * 16
    ringed = rows % 32 == 0 and lines == 4
    extra = 16 if ringed else 0
    spans = rows if ringed else width

    def swap(axis, size, bit):
        return lambda value: lax.ppermute(value, axis, [(i, i ^ bit) for i in range(size)])

    swap_core = swap("dp", replicas, 1)
    swap_row = swap("dp", replicas, 2)
    swap_side = swap("fsdp", shards, 1)

    def step_line(value):
        return lax.ppermute(value, "fsdp", [(i, (i + 2) % shards) for i in range(shards)])

    def all_replicas(value):
        across = swap_row(value)
        return jnp.stack([value, swap_core(value), across, swap_core(across)])

    def in_order(found):
        return [
            lax.dynamic_index_in_dim(found, jnp.bitwise_xor(replica, at), 0, keepdims=False)
            for at in range(4)
        ]

    def shift_line(value, steps):
        return lax.ppermute(value, "fsdp", [(i, (i + 2 * steps) % shards) for i in range(shards)])

    def cross(value):
        return lax.ppermute(
            value, "fsdp", [(i, ((i + 6) % shards) ^ 1) for i in range(shards)]
        )

    def owner(steps, other):
        return 2 * jnp.mod(line - steps, lines) + jnp.bitwise_xor(side, other)

    order = [(steps, other) for steps in range(lines) for other in range(2)]

    clock = [jnp.zeros((), jnp.int32)]

    def tied(value):
        return lax.optimization_barrier((value, clock[0]))[0]

    def wait(*values):
        found = lax.optimization_barrier((clock[0], *values))
        clock[0] = found[0]
        return found[1] if len(values) == 1 else found[1:]

    block = jnp.where(
        replica < 3,
        lax.dynamic_slice(w_qkv, (0, jnp.minimum(replica, 2) * width), (rows, width)),
        w_out,
    )
    vectors = jnp.stack([ln1_gain, ln1_bias, ln2_gain, ln2_bias])
    kinds_here = token_type[:, 0]
    image_counts = jnp.sum(mlm_mask * token_type, 1)
    text_counts = jnp.sum(mlm_mask, 1) - image_counts
    if ringed:
        facts = jnp.concatenate([kinds_here, text_counts, image_counts]).astype(BF)
        facts = jnp.concatenate([vectors.reshape(-1), facts])
        fact_row = jnp.zeros((extra, width), BF).at[0, : facts.shape[0]].set(facts)
        block = jnp.concatenate([block, fact_row], 0)
    expert_block = jnp.concatenate(
        [
            lax.dynamic_slice(w_up, (0, 0, replica * columns), (2, rows, columns)),
            lax.dynamic_slice(w_down, (0, replica * columns, 0), (2, columns, rows)).transpose(
                0, 2, 1
            ),
        ],
        0,
    )
    def pad_rows(value):
        return jnp.pad(value, ((0, 0), (0, padded - length), (0, 0)))

    if ringed:
        span = rows
        side_block = swap_side(block)
        ring = [shift_line(block, steps) for steps in range(1, lines)]
        row_block = swap_row(block)
        experts, near = [expert_block, step_line(expert_block)], [swap_side(expert_block)]
        dmixed = pad_rows(cotangent * mlm_mask[..., None].astype(BF))
        dmixed_row = swap_row(dmixed)
        wait(side_block, *ring, row_block)
        lined = jnp.concatenate([side_block, *ring], 0)
        side_ring = swap_side(tied(jnp.concatenate(ring, 0)))
        row_lined = swap_row(tied(lined))
        core_parts = [swap_core(tied(part)) for part in (block, row_block, lined)]
        wait(dmixed_row, near[0], *core_parts)
        grads = [dmixed, swap_core(tied(dmixed)), dmixed_row]
        tok = pad_rows(tied(tokens))
        wait(experts[1])
        experts.append(step_line(tied(experts[1])))
        wait(side_ring, row_lined, tok)
        row_side_ring = swap_row(tied(side_ring))
        near.append(swap_side(tied(experts[1])))
        core_parts += [swap_core(tied(part)) for part in (side_ring, row_lined)]
        wait(*core_parts[3:], grads[1])
        wait(experts[2])
        experts.append(step_line(tied(experts[2])))
        wait(row_side_ring)
        core_parts.append(swap_core(tied(row_side_ring)))
        wait(core_parts[5], near[1])
        near.append(swap_side(tied(experts[2])))
        first_line = [(0, 0)]
        later = [(steps, 0) for steps in range(1, lines)]
        later_sides = [(steps, 1) for steps in range(1, lines)]
        held = [
            (0, block, first_line),
            (0, lined, [(0, 1)] + later),
            (0, side_ring, later_sides),
            (2, row_block, first_line),
            (2, row_lined, [(0, 1)] + later),
            (2, row_side_ring, later_sides),
            (1, core_parts[0], first_line),
            (3, core_parts[1], first_line),
            (1, core_parts[2], [(0, 1)] + later),
            (1, core_parts[3], later_sides),
            (3, core_parts[4], [(0, 1)] + later),
            (3, core_parts[5], later_sides),
        ]
        attn_pieces = [part for _, part, _ in held]
        spots = [(rel, spot) for rel, _, spots_of in held for spot in spots_of]
        attn_place = jnp.stack(
            [
                value
                for rel, spot in spots
                for value in (jnp.bitwise_xor(replica, rel), owner(*spot) * rows)
            ]
            + [owner(*spot) for _, spot in spots]
        ).astype(jnp.int32)
        expert_place = jnp.stack([owner(*at) * rows for at in order]).astype(jnp.int32)
    else:
        span = 0
        whole = lax.all_gather(block, "fsdp", axis=0, tiled=True)
        attn_pieces = [jnp.stack(in_order(all_replicas(whole)))]
        attn_place = jnp.zeros((1,), jnp.int32)
        gains = lax.all_gather(vectors, "fsdp", axis=1, tiled=True).astype(F32)
        expert_pieces = [lax.all_gather(expert_block, "fsdp", axis=1, tiled=True)]
        expert_place = jnp.zeros((1,), jnp.int32)
        kinds = all_replicas(kinds_here).T
        counts = jnp.stack([jnp.sum(text_counts), jnp.sum(image_counts)])
        counts = lax.psum(counts, ("fsdp", "dp"))
        dmixed = pad_rows(cotangent * mlm_mask[..., None].astype(BF))
        tok = pad_rows(tokens)
        dmixed_row = swap_row(dmixed)
        grads = [dmixed, swap_core(dmixed), dmixed_row]
    attn_weights = pltpu.VMEM((4, width, width), BF)
    head_probs = pltpu.VMEM((HEADS, padded, padded), BF)
    states_of, kept = [], []
    for half in range(halves):
        fresh = ringed and half == 0
        sources = attn_pieces if half == 0 or not ringed else [all_weights]
        first_in, qkv, probs, context, hidden, second_in, *found = call(
            functools.partial(attention_forward, span if fresh else 0, length, len(sources)),
            [
                shaped((padded, width)),
                shaped((padded, 3 * width)),
                shaped((HEADS, padded, padded)),
                shaped((padded, width)),
                shaped((padded, width), F32),
                shaped((padded, width)),
            ]
            + [shaped((4, width, width)), shaped((4, shards, 16, width)), shaped((4, width), F32)]
            * fresh,
            [SCALARS, one_of(tok, half)] + [WHOLE] * (not fresh) + [ANYWHERE] * len(sources),
            [ANYWHERE] * 6 + [ANYWHERE, ANYWHERE, WHOLE] * fresh,
            [
                pltpu.VMEM((4, shards, 16, width), BF),
                pltpu.SemaphoreType.DMA((4 * shards,)),
            ]
            * fresh
            + [
                pltpu.VMEM((padded, width), BF),
                pltpu.VMEM((padded, 3 * width), BF),
                head_probs,
                pltpu.VMEM((padded, width), BF),
                pltpu.VMEM((padded, width), F32),
                pltpu.VMEM((padded, width), BF),
                attn_weights,
                pltpu.SemaphoreType.DMA((4 * shards,)),
                pltpu.SemaphoreType.DMA((7,)),
            ]
            + [pltpu.VMEM((4, width), F32)] * fresh,
            (tied(attn_place), tok, *([] if fresh else [gains]), *sources),
            time=9,
        )
        kept.append((first_in, qkv, probs, context, hidden))
        if half == 0:
            all_weights = attn_pieces[0]
            if ringed:
                all_weights, facts, gains = found
                wait(gains)
        if half == 0 or not ringed:
            states_of.append(
                [second_in, swap_core(tied(second_in)), swap_row(tied(second_in))]
            )
        if half == 0 and ringed:
            wait(experts[3], near[2], states_of[0][1])
            near.append(swap_side(tied(experts[3])))
    if ringed:
        wait(second_in, states_of[0][2], near[2], near[3])
        beside_core = swap_core(tied(second_in))
        grads.append(swap_core(tied(dmixed_row)))
        states_of[0].append(swap_core(tied(states_of[0][2])))
        wait(grads[3], beside_core, states_of[0][3])
        before_row = clock[0]
        states_of.append([second_in, beside_core, swap_row(tied(second_in))])
        numbers = facts[:, :, 0, 4 * rows : 4 * rows + 3 * halves].astype(F32)
        kinds = lax.dynamic_index_in_dim(numbers, shard, 1, keepdims=False)
        kinds = jnp.stack(
            [
                lax.dynamic_index_in_dim(kinds, jnp.bitwise_xor(replica, rel), 0, keepdims=False)
                for rel in range(4)
            ]
        )
        kinds = kinds[:, :halves].astype(jnp.int32).T
        counts = numbers.reshape(-1, 3, halves).sum((0, 2))[1:].astype(jnp.int32)
        expert_pieces = [part for both in zip(experts, near) for part in both]
        states_of[1].append(swap_core(states_of[1][2]))
    else:
        grads.append(swap_core(dmixed_row))
        for states in states_of:
            states.append(swap_core(states[2]))

    left = padded - tail
    expert_scratch = [
        pltpu.VMEM((4, width, columns), BF),
        *[pltpu.VMEM((5, main, width), BF)] * 2,
        *[pltpu.VMEM((5, main, columns), BF)] * 2,
        *[pltpu.VMEM((4 * left, width), BF)] * 2,
        *[pltpu.VMEM((2, padded, width), BF)] * 4,
        pltpu.SemaphoreType.DMA((len(expert_pieces),)),
        pltpu.SemaphoreType.DMA((8,)),
        pltpu.SemaphoreType.DMA((8,)),
        pltpu.SemaphoreType.DMA((14,)),
    ]
    acts, dpres, outs, arriving = [], [], [], []
    for half in range(halves):
        act, dpre, keep_grad, send_grad, keep_out, send_out = call(
            functools.partial(expert_layer, half, main, tail),
            [shaped((5, main, columns))] * 2 + [shaped((2, padded, width))] * 4,
            [SCALARS] * 2 + [ANYWHERE] * (8 + len(expert_pieces)),
            [ANYWHERE] * 6,
            expert_scratch,
            (tied(expert_place), kinds[half], *states_of[half], *grads, *expert_pieces),
            time=12.5,
        )
        acts.append(act)
        dpres.append(dpre)
        if half == 0:
            wait(states_of[1][2])
        else:
            wait(arriving[half - 1][1])
        summed = add(keep_grad, swap_core(tied(send_grad)))
        outs.append((keep_out, swap_core(tied(send_out))))
        if half + 1 < halves:
            wait(summed, outs[-1][1])
        arriving.append((summed, swap_row(summed[1])))

    piece_count = len(expert_pieces)
    if ringed:
        spots = [(0, 0), (1, 0), (2, 0), (2, 1), (3, 0), (4, 0), (5, 0), (6, 0)]
        grad_sizes = [1, 1, 2, 1, 1, 1, 1]
    else:
        spots, grad_sizes = [(0, 0)], [1]
    expert_parts = call(
        functools.partial(expert_weight_grads, main, tail, halves, spots),
        [shaped((size, 4, spans, columns)) for size in grad_sizes],
        [SCALARS] * 2 + [ANYWHERE] * (4 * halves + 4 + 2 * halves),
        [ANYWHERE] * len(grad_sizes),
        [
            pltpu.VMEM((4, width, columns), F32),
            pltpu.VMEM((4, width, columns), BF),
            *[pltpu.VMEM((5 * halves, main, width), BF)] * 2,
            *[pltpu.VMEM((5 * halves, main, columns), BF)] * 2,
            pltpu.SemaphoreType.DMA((piece_count, 4)),
            pltpu.SemaphoreType.DMA((halves, 8)),
            pltpu.SemaphoreType.DMA((halves, 8)),
            pltpu.SemaphoreType.DMA((halves, 5, 2)),
        ],
        (
            tied(expert_place),
            kinds.reshape(-1),
            *[state for states in states_of for state in states],
            *grads,
            *acts,
            *dpres,
        ),
        time=13.5,
    )

    wait(expert_parts[0])
    if ringed:
        direct = shift_line(tied(expert_parts[2]), lines - 1)
        sent_two = swap_side(tied(expert_parts[4]))
    wait(outs[-1][1])
    out_sum = jnp.stack([add(*pair) for pair in outs])
    out_rest = None
    lows, dqkvs, norm_parts, input_grads = [], [], [], []
    for half in range(halves):
        first_in, qkv, probs, context, hidden = kept[half]
        summed, far = arriving[half]
        low, dqkv, input_grad, norm_grads = call(
            functools.partial(attention_backward, length),
            [
                shaped((padded, width)),
                shaped((padded, 3 * width)),
                shaped((length, width), F32),
                shaped((4, width), F32),
            ],
            [one_of(tok, half), WHOLE, one_of(summed, 0), WHOLE, one_of(dmixed, half), WHOLE]
            + [ANYWHERE] * 4,
            [WHOLE] * 4,
            [
                pltpu.VMEM((padded, 3 * width), BF),
                head_probs,
                attn_weights,
                pltpu.VMEM((padded, width), F32),
                pltpu.SemaphoreType.DMA((4,)),
            ],
            (tok, tied(gains), summed, far, dmixed, hidden, qkv, probs, all_weights, expert_parts[0]),
            time=10,
        )
        wait(norm_grads)
        if half == 0:
            wait(arriving[1][1])
            out_rest = swap_row(tied(out_sum[:, 1]))
            if ringed:
                current = step_line(tied(add(expert_parts[3], wait(sent_two))))
                sent_three = swap_side(tied(expert_parts[6]))
        elif ringed:
            direct = wait(direct)
            sent_home = swap_side(tied(add(expert_parts[1], direct[1:2])))
        lows.append(low)
        dqkvs.append(dqkv)
        norm_parts.append(norm_grads)
        input_grads.append(input_grad)
    input_grad = jnp.stack(input_grads)

    core, row = replica % 2, replica // 2
    grad_place = jnp.stack([core, row * 2 * width, 1 - core, (1 - row) * 2 * width])
    grad_place = grad_place.astype(jnp.int32)
    owners = shards if ringed else 2
    core_rows = width // (2 * owners)
    keep, *sends = call(
        functools.partial(attention_weight_grads, halves),
        [
            shaped((size, core_rows, 2 * width))
            for size in (2 * owners + 1, *[owners // 2] * 3, owners // 2 + 1)
        ],
        [SCALARS] + [WHOLE] * halves + [ANYWHERE] * (4 * halves),
        [ANYWHERE] * 5,
        [
            *[pltpu.VMEM((halves, padded, width), BF)] * 3,
            pltpu.VMEM((halves, padded, 3 * width), BF),
            pltpu.VMEM((owners, 2, core_rows, 4 * width), BF),
            pltpu.VMEM((core_rows, 2 * width), BF),
            pltpu.SemaphoreType.DMA((6 * halves,)),
            pltpu.SemaphoreType.DMA((8,)),
        ],
        (
            tied(grad_place),
            *norm_parts,
            *[kept[h][0] for h in range(halves)],
            *dqkvs,
            *[kept[h][3] for h in range(halves)],
            *lows,
        ),
        time=8.5,
    )
    wait(keep, out_rest)
    if ringed:
        ready = add(wait(current), add(expert_parts[5], wait(sent_three)))
    received = [swap_core(tied(part)) for part in sends]
    divisor = counts.astype(F32)[:, None, None]

    def join_replicas(value, axis, row_axis):
        across = swap_row(value)
        mine, other = value, swap_core(value)
        far, far_other = across, swap_core(across)
        near_parts = jnp.where(core == 0, mine, other), jnp.where(core == 0, other, mine)
        far_parts = jnp.where(core == 0, far, far_other), jnp.where(core == 0, far_other, far)
        near_part = jnp.concatenate(near_parts, axis)
        far_part = jnp.concatenate(far_parts, axis)
        return jnp.concatenate(
            [jnp.where(row == 0, near_part, far_part), jnp.where(row == 0, far_part, near_part)],
            row_axis,
        )

    if ringed:
        current = step_line(tied(ready))
        received = wait(*received)
        half_shards = shards // 2
        mine = add(keep[:shards], jnp.concatenate(received[:2], 0))
        theirs = add(keep[shards:-1], jnp.concatenate([received[2], received[3][:-1]], 0))
        vector_block = add(keep[-1, :8], received[3][-1, :8])

        def by_side(value, other):
            pairs_of = value.reshape(-1, 2, *value.shape[1:])
            return lax.dynamic_index_in_dim(
                pairs_of, jnp.bitwise_xor(side, other), 1, keepdims=False
            )

        def with_vectors(value):
            return jnp.concatenate([value.reshape(-1, 2 * width), vector_block], 0)

        def split_vectors(value):
            return value[:-8].reshape(-1, core_rows, 2 * width), value[-8:]

        first_sent = swap_row(tied(with_vectors(theirs[:half_shards])))
        both = jnp.concatenate([mine[half_shards:], theirs[half_shards:]], 0)
        second_sent = swap_side(tied(by_side(both, 1)))
        home = add(wait(sent_home), expert_parts[0])
        home = add(home, direct[0:1])
        expert_mine = add(wait(current), home)[0]
        expert_row = swap_row(tied(expert_mine))
        expert_core = swap_core(tied(expert_mine))
        first_done, second_done = wait(first_sent, second_sent)
        first_done, vectors_done = split_vectors(first_done)
        first = add(mine[:half_shards], first_done)
        vector_block = add(vector_block, vectors_done)
        first_next = swap_side(tied(with_vectors(by_side(first, 1))))
        second = add(by_side(both, 0), second_done)
        middle = lines // 2
        second_next = swap_row(tied(second[middle:]))
        first_last, second_last = wait(first_next, second_next)
        first_last, vectors_done = split_vectors(first_last)
        first = add(by_side(first, 0), first_last)
        vector_block = add(vector_block, vectors_done)
        second = add(second[:middle], second_last)
        lined = jnp.concatenate([first, second], 0)

        def lined_block(steps):
            return with_vectors(
                lax.dynamic_index_in_dim(lined, jnp.mod(line - steps, lines), 0)
            )

        arrived = [
            shift_line(tied(lined_block(steps)), lines - steps) for steps in range(1, lines)
        ]
        wait(*arrived, expert_row, expert_core)
        expert_all = jnp.stack(
            [expert_mine, expert_core, expert_row, swap_core(tied(expert_row))]
        )
        reduced = sum([part.astype(F32) for part in arrived], lined_block(0).astype(F32))
        vectors_sum = reduced[core_rows : core_rows + 2].reshape(4, width)
        vectors_sum = lax.dynamic_slice_in_dim(vectors_sum, shard * rows, rows, 1)
        attn_mine = reduced[:core_rows].astype(BF)
        attn_grad = join_replicas(tied(attn_mine), 0, 1)
    else:
        summed = add(keep, jnp.concatenate(received, 0))
        mine = add(summed[:owners], swap_row(summed[owners:-1]))
        attn_grad = join_replicas(mine, 1, 2).reshape(width, 4 * width)
        attn_grad = lax.psum_scatter(attn_grad, "fsdp", scatter_dimension=0, tiled=True)
        vectors_sum = functools.reduce(jnp.add, norm_parts)
        vectors_sum = lax.psum_scatter(vectors_sum, "fsdp", scatter_dimension=1, tiled=True)
        vectors_sum = lax.psum(vectors_sum, "dp")
        expert_mine = lax.psum_scatter(
            expert_parts[0][0], "fsdp", scatter_dimension=1, tiled=True
        )
        expert_all = all_replicas(expert_mine)
    expert_all = in_order(expert_all)
    up_grad = jnp.concatenate([part[:2] for part in expert_all], 2).astype(F32) / divisor
    down_grad = (
        jnp.concatenate([part[2:] for part in expert_all], 2).astype(F32).transpose(0, 2, 1)
        / divisor
    )
    mixed = jnp.stack(
        [
            (kept[h][4] + out_sum[h, 0].astype(F32) + out_rest[h].astype(F32))[:length]
            for h in range(halves)
        ]
    ).astype(BF)
    vector_grads = [vectors_sum[at] for at in range(4)]
    attn_grad = attn_grad.astype(F32)
    return (
        mixed,
        input_grad,
        vector_grads[0],
        vector_grads[1],
        attn_grad[:, : 3 * width],
        attn_grad[:, 3 * width :],
        vector_grads[2],
        vector_grads[3],
        up_grad,
        down_grad,
        counts,
    )


def solution(mesh):
    return jax.shard_map(
        per_device,
        mesh=mesh,
        in_specs=(
            P(("fsdp", "dp"), None, None),
            P(("fsdp", "dp"), None),
            P(("fsdp", "dp"), None),
            P(("fsdp", "dp"), None, None),
            P("fsdp"),
            P("fsdp"),
            P("fsdp", None),
            P("fsdp", None),
            P("fsdp"),
            P("fsdp"),
            P(None, "fsdp", None),
            P(None, None, "fsdp"),
        ),
        out_specs=(
            P(("fsdp", "dp"), None, None),
            P(("fsdp", "dp"), None, None),
            P("fsdp"),
            P("fsdp"),
            P("fsdp", None),
            P("fsdp", None),
            P("fsdp"),
            P("fsdp"),
            P(None, "fsdp", None),
            P(None, None, "fsdp"),
            P(),
        ),
        check_vma=False,
    )
```

```python
import functools

import jax
import jax.numpy as jnp
from jax import lax
from jax.experimental import pallas as pl
from jax.experimental.pallas import tpu as pltpu
from jax.sharding import PartitionSpec as P

HEADS = 12
HEAD = 64
TILE = 256
WINDOW = 3
PATCHES = 197
MIB = 1024 * 1024
BF = jnp.bfloat16
F32 = jnp.float32


def dot(left, right, left_dim=1, right_dim=0):
    return lax.dot_general(
        left, right, (((left_dim,), (right_dim,)), ((), ())), preferred_element_type=F32
    )


def moments(values):
    center = values - jnp.mean(values, -1, keepdims=True)
    inverse = lax.rsqrt(jnp.mean(center * center, -1, keepdims=True) + 1e-06)
    return center * inverse, inverse


def norm_backward(grad, unit, inverse, gain):
    scaled = grad * gain
    slope = jnp.mean(scaled * unit, -1, keepdims=True)
    result = inverse * (scaled - jnp.mean(scaled, -1, keepdims=True) - unit * slope)
    return result, jnp.sum(grad * unit, 0, keepdims=True), jnp.sum(grad, 0, keepdims=True)


def gelu_parts(pre):
    share = 0.5 + 0.5 * lax.erf(pre * 0.7071067811865476)
    density = jnp.exp(-0.5 * pre * pre) * 0.3989422804014327
    return pre * share, share + pre * density


def run_copies(copies):
    for copy in copies:
        copy.start()
    for copy in copies:
        copy.wait()


def tile(at):
    return pl.ds(pl.multiple_of(at * TILE, TILE), TILE)


def every(count, body):
    lax.fori_loop(0, count, lambda at, carry: (body(at), carry)[1], 0, unroll=min(6, count))


def start_copies(pairs, sems):
    copies = [
        pltpu.make_async_copy(source, target, sems.at[at])
        for at, (source, target) in enumerate(pairs)
    ]
    for copy in copies:
        copy.start()
    return copies


def wait_copies(copies):
    for copy in copies:
        copy.wait()


def gather_vectors(facts, count, rows, width):
    lane = lax.broadcasted_iota(jnp.int32, (8, width), 1)
    vectors = [jnp.zeros((8, width), F32)] * 4
    for owner in range(count):
        sent = facts[0, owner, 0:8].astype(F32)
        inside = (lane >= owner * rows) & (lane < (owner + 1) * rows)
        for at in range(4):
            shift = (owner - at) * rows % width
            moved = pltpu.roll(sent, shift, 1) if shift else sent
            row = jnp.broadcast_to(moved[0:1], (8, width))
            vectors[at] = jnp.where(inside, row, vectors[at])
    return jnp.concatenate([vector[0:1] for vector in vectors], 0)


def attention_forward(rows, length, pieces, place, tok, *refs):
    fresh = rows > 0
    if fresh:
        gains, refs = refs[-1], refs[:-1]
    else:
        gains, refs = refs[0], refs[1:]
    sources, refs = refs[:pieces], refs[pieces:]
    if fresh:
        step = rows + 16
        sources = [
            ref.at[pl.ds(first, step)] for ref in sources for first in range(0, ref.shape[0], step)
        ]
        pieces = len(sources)
    first_out, qkv_out, probs_out, context_out, hidden_out, second_out = refs[:6]
    if fresh:
        weights_out, facts_out, gains_out, refs = refs[6], refs[7], refs[8], refs[9:]
        facts, fact_sems, refs = refs[0], refs[1], refs[2:]
    else:
        refs = refs[6:]
    first_in, qkv, probs, context, hidden, second_in, weights, sems, out_sems = refs
    if fresh:
        fact_copies = [
            pltpu.make_async_copy(
                source.at[pl.ds(rows, 16)], facts.at[place[2 * at], place[2 * pieces + at]], fact_sems.at[at]
            )
            for at, source in enumerate(sources)
        ]
        for copy in fact_copies:
            copy.start()
        pairs = [
            (
                source.at[pl.ds(0, rows)],
                weights.at[place[2 * at], pl.ds(pl.multiple_of(place[2 * at + 1], 32), rows)],
            )
            for at, source in enumerate(sources)
        ]
    else:
        pairs = [(source, weights) for source in sources]
    copies = start_copies(pairs, sems)
    if fresh:
        wait_copies(fact_copies)
        shards = facts.shape[1]
        gains[...] = gather_vectors(facts, shards, rows, tok.shape[1])
        gains_out[...] = gains[...]
        fact_copy = pltpu.make_async_copy(facts, facts_out, fact_sems.at[0])
        fact_copy.start()
    inputs = tok[...].astype(F32)
    padded, width = inputs.shape
    tiles = width // TILE
    unit, _ = moments(inputs)
    first_in[...] = (unit * gains[0:1] + gains[1:2]).astype(BF)
    wait_copies(copies)
    results = [pltpu.make_async_copy(first_in, first_out, out_sems.at[0])]
    results[0].start()
    if fresh:
        results.append(pltpu.make_async_copy(weights, weights_out, out_sems.at[6]))
        results[-1].start()
        results.append(fact_copy)

    def project(at):
        block = weights[at // tiles, :, tile(at % tiles)]
        qkv[:, tile(at)] = dot(first_in[...], block).astype(BF)

    every(3 * tiles, project)
    results.append(pltpu.make_async_copy(qkv, qkv_out, out_sems.at[1]))
    results[-1].start()
    pair = 2 * HEAD
    low_half = lax.broadcasted_iota(jnp.int32, (padded, pair), 1) < HEAD
    real = lax.broadcasted_iota(jnp.int32, (padded, padded), 1) < length

    def heads(at):
        lanes = pl.multiple_of(at * pair, pair)
        query = qkv[:, pl.ds(lanes, pair)]
        key = qkv[:, pl.ds(width + lanes, pair)]
        value = qkv[:, pl.ds(2 * width + lanes, pair)]
        total = jnp.zeros((padded, pair), F32)
        for half in range(2):
            keep = low_half if half == 0 else jnp.logical_not(low_half)
            scores = dot(jnp.where(keep, query, 0), key, 1, 1) * HEAD ** (-0.5)
            scores = jnp.where(real, scores, -1e30)
            grown = jnp.exp(scores - jnp.max(scores, -1, keepdims=True))
            prob = (grown / jnp.sum(grown, -1, keepdims=True)).astype(BF)
            probs[2 * at + half] = prob
            total += dot(prob, jnp.where(keep, value, 0))
        context[:, pl.ds(lanes, pair)] = total.astype(BF)

    every(HEADS // 2, heads)
    results.append(pltpu.make_async_copy(probs, probs_out, out_sems.at[2]))
    results[-1].start()
    results.append(pltpu.make_async_copy(context, context_out, out_sems.at[3]))
    results[-1].start()

    def project_out(at):
        added = dot(context[...], weights[3, :, tile(at)])
        hidden[:, tile(at)] = tok[:, tile(at)].astype(F32) + added

    every(tiles, project_out)
    results.append(pltpu.make_async_copy(hidden, hidden_out, out_sems.at[4]))
    results[-1].start()
    unit, _ = moments(hidden[...])
    second_in[...] = (unit * gains[2:3] + gains[3:4]).astype(BF)
    results.append(pltpu.make_async_copy(second_in, second_out, out_sems.at[5]))
    results[-1].start()
    wait_copies(results)


def block_copies(sources, target, sems, main, tail):
    left = sources[0].shape[0] - tail
    pairs = [
        (source.at[pl.ds(tail, left)], target.at[0, pl.ds(at * left, left)])
        for at, source in enumerate(sources)
    ]
    pairs += [(source.at[pl.ds(0, main)], target.at[1 + at]) for at, source in enumerate(sources)]
    return [
        pltpu.make_async_copy(source, there, sems.at[at])
        for at, (source, there) in enumerate(pairs)
    ]


def expert_copies(place, pieces, weights, sems):
    copies = []
    for at, piece in enumerate(pieces):
        first = pl.multiple_of(place[at], 32)
        copies.append(
            pltpu.make_async_copy(
                piece, weights.at[:, pl.ds(first, piece.shape[1])], sems.at[at]
            )
        )
    return copies


def expert_layer(half, main, tail, place, kinds, *refs):
    states, grads = refs[:4], refs[4:8]
    pieces, refs = refs[8:-21], refs[-21:]
    act_out, dpre_out = refs[:2]
    results = refs[2:6]
    weights, state, grad, act, dpre, state_end, grad_end, *held = refs[6:]
    sems, state_sems, grad_sems, out_sems, held = held[-4], held[-3], held[-2], held[-1], held[:-4]
    width, hidden = weights.shape[1:]
    left = state_end.shape[0] // 4
    state_copies = block_copies(states, state, state_sems, main, tail)
    grad_copies = block_copies([ref.at[half] for ref in grads], grad, grad_sems, main, tail)
    copies = expert_copies(place, pieces, weights, sems)
    copies += state_copies[:4] + grad_copies[:4]
    for copy in copies:
        copy.start()
    spare = main - 4 * left
    state[0, 4 * left :] = jnp.zeros((spare, width), BF)
    grad[0, 4 * left :] = jnp.zeros((spare, width), BF)
    wait_copies(copies)
    for copy in state_copies[4:] + grad_copies[4:]:
        copy.start()
    spot = lax.broadcasted_iota(jnp.int32, (main, 1), 0)
    image = spot < PATCHES
    text = (spot % left + tail >= PATCHES) & (spot < 4 * left)

    def forward(at, expert, mine):
        def body(step):
            columns = tile(step)
            pre = dot(state[at], weights[expert, :, columns])
            dact = dot(grad[at], weights[2 + expert, :, columns])
            value, slope = gelu_parts(pre)
            act[at, :, columns] = jnp.where(mine, value, 0).astype(BF)
            dpre[at, :, columns] = jnp.where(mine, dact * slope, 0).astype(BF)

        every(hidden // TILE, body)

    forward(0, 0, text)
    outs = []
    for index, (source, target) in enumerate(((act, act_out), (dpre, dpre_out))):
        outs.append(pltpu.make_async_copy(source.at[0], target.at[0], out_sems.at[index]))
        outs[-1].start()

    def end_body(step):
        columns = tile(step)
        rows = pl.ds(0, 4 * left)
        grad_end[:, columns] = dot(dpre[0, rows], weights[0, columns], 1, 1).astype(BF)
        state_end[:, columns] = dot(act[0, rows], weights[2, columns], 1, 1).astype(BF)

    every(width // TILE, end_body)
    for rel in range(4):
        at = rel + 1
        expert = kinds[rel]
        state_copies[4 + rel].wait()
        grad_copies[4 + rel].wait()
        forward(at, expert, image)
        for index, (source, target) in enumerate(((act, act_out), (dpre, dpre_out))):
            outs.append(
                pltpu.make_async_copy(source.at[at], target.at[at], out_sems.at[2 * at + index])
            )
            outs[-1].start()
        grad_to, out_to = held[rel % 2], held[2 + rel % 2]
        place_at = rel // 2
        end = rel * left

        def body(step):
            columns = tile(step)
            there = pl.ds(0, main)
            for source, weight, target, ends in (
                (dpre, weights.at[expert], grad_to, grad_end),
                (act, weights.at[2 + expert], out_to, state_end),
            ):
                value = dot(source[at], weight[columns], 1, 1)
                target[place_at, 0:tail, columns] = value[:tail].astype(BF)
                shared = ends[end : end + main - tail, columns].astype(F32)
                target[place_at, tail:main, columns] = (value[tail:] + shared).astype(BF)
                target[place_at, main:, columns] = ends[end + main - tail : end + left, columns]

        every(width // TILE, body)
    for index, (source, target) in enumerate(zip(held, results)):
        outs.append(pltpu.make_async_copy(source, target, out_sems.at[10 + index]))
        outs[-1].start()
    wait_copies(outs)


def expert_weight_grads(main, tail, halves, spots, place, kinds, *refs):
    states, refs = refs[: 4 * halves], refs[4 * halves :]
    grads, refs = refs[:4], refs[4:]
    acts, refs = refs[:halves], refs[halves:]
    dpres, refs = refs[:halves], refs[halves:]
    outs, rest = refs[:-10], refs[-10:]
    total, rounded, state, grad, act, dpre, sems, state_sems, grad_sems, rest_sems = rest
    width = total.shape[1]
    left = states[0].shape[0] - tail
    ready = []
    for half in range(halves):
        there = pl.ds(5 * half, 5)
        moves = block_copies(
            states[4 * half : 4 * half + 4], state.at[there], state_sems.at[half], main, tail
        )
        grad_moves = block_copies(
            [ref.at[half] for ref in grads], grad.at[there], grad_sems.at[half], main, tail
        )
        for block in range(5):
            spot = 5 * half + block
            needed = [
                pltpu.make_async_copy(
                    acts[half].at[block], act.at[spot], rest_sems.at[half, block, 0]
                ),
                pltpu.make_async_copy(
                    dpres[half].at[block], dpre.at[spot], rest_sems.at[half, block, 1]
                ),
            ]
            chosen = slice(0, 4) if block == 0 else slice(3 + block, 4 + block)
            needed += moves[chosen] + grad_moves[chosen]
            ready.append(needed)
    for needed in ready[:WINDOW]:
        for copy in needed:
            copy.start()
    spare = main - 4 * left
    for half in range(halves):
        state[5 * half, 4 * left :] = jnp.zeros((spare, width), BF)
        grad[5 * half, 4 * left :] = jnp.zeros((spare, width), BF)
    total[1] = jnp.zeros(total.shape[1:], F32)
    total[3] = jnp.zeros(total.shape[1:], F32)
    for at, needed in enumerate(ready):
        half, block = divmod(at, 5)
        expert = kinds[4 * half + block - 1] if block else 0
        for copy in (ready[at + WINDOW] if at + WINDOW < len(ready) else []):
            copy.start()
        wait_copies(needed)

        def body(step):
            columns = tile(step)
            up = dot(state[at, :, columns], dpre[at], 0, 0)
            down = dot(grad[at, :, columns], act[at], 0, 0)
            if at == 0:
                total[0, columns] = up
                total[2, columns] = down
            else:
                total[expert, columns] += up
                total[2 + expert, columns] += down

        every(width // TILE, body)
    copies = []
    for part in range(4):
        rounded[part] = total[part].astype(BF)
        for piece, (out, at) in enumerate(spots):
            first = pl.multiple_of(place[piece], 32)
            target = outs[out].at[at, part]
            copies.append(
                pltpu.make_async_copy(
                    rounded.at[part, pl.ds(first, target.shape[0])], target, sems.at[piece, part]
                )
            )
            copies[-1].start()
    wait_copies(copies)


def attention_backward(length, tok, gains, near, far, dmixed, hidden, *refs):
    qkv_from, probs_from, weights_from, refs = refs[0], refs[1], refs[2], refs[4:]
    low, dqkv, input_grad, norm_grads, qkv, probs, weights, total, sems = refs
    copies = start_copies(
        [(weights_from.at[pl.ds(3, 1)], weights.at[pl.ds(3, 1)])]
        + [(qkv_from, qkv), (probs_from, probs)]
        + [(weights_from.at[pl.ds(0, 3)], weights.at[pl.ds(0, 3)])],
        sems,
    )
    padded, width = tok.shape
    tiles = width // TILE
    unit, inverse = moments(hidden[...])
    second = near[...].astype(F32) + far[...].astype(F32)
    part, gain_two, bias_two = norm_backward(second, unit, inverse, gains[2:3])
    dhidden = dmixed[...].astype(F32) + part
    low[...] = dhidden.astype(BF)
    total[...] = dhidden
    norm_grads[2:3] = gain_two
    norm_grads[3:4] = bias_two
    copies[0].wait()

    def project_out(at):
        dqkv[:, tile(at)] = dot(low[...], weights[3, tile(at)], 1, 1).astype(BF)

    every(tiles, project_out)
    pair = 2 * HEAD
    low_half = lax.broadcasted_iota(jnp.int32, (padded, pair), 1) < HEAD
    copies[1].wait()
    copies[2].wait()

    def heads(at):
        lanes = pl.multiple_of(at * pair, pair)
        query = qkv[:, pl.ds(lanes, pair)]
        key = qkv[:, pl.ds(width + lanes, pair)]
        value = qkv[:, pl.ds(2 * width + lanes, pair)]
        upper = dqkv[:, pl.ds(lanes, pair)]
        dquery = jnp.zeros((padded, pair), F32)
        dkey = jnp.zeros((padded, pair), F32)
        dvalue = jnp.zeros((padded, pair), F32)
        for half in range(2):
            keep = low_half if half == 0 else jnp.logical_not(low_half)
            prob = probs[2 * at + half]
            wide = prob.astype(F32)
            upper_half = jnp.where(keep, upper, 0)
            dprob = dot(upper_half, value, 1, 1)
            dscore = (wide * (dprob - jnp.sum(dprob * wide, -1, keepdims=True))).astype(BF)
            dquery += dot(dscore, jnp.where(keep, key, 0))
            dkey += dot(dscore, jnp.where(keep, query, 0), 0, 0)
            dvalue += dot(prob, upper_half, 0, 0)
        dqkv[:, pl.ds(lanes, pair)] = (dquery * HEAD ** (-0.5)).astype(BF)
        dqkv[:, pl.ds(width + lanes, pair)] = (dkey * HEAD ** (-0.5)).astype(BF)
        dqkv[:, pl.ds(2 * width + lanes, pair)] = dvalue.astype(BF)

    every(HEADS // 2, heads)
    copies[3].wait()
    dfirst = []
    for at in range(tiles):
        columns = slice(at * TILE, (at + 1) * TILE)
        part = dot(dqkv[:, 0:width], weights[0, columns], 1, 1)
        part += dot(dqkv[:, width : 2 * width], weights[1, columns], 1, 1)
        part += dot(dqkv[:, 2 * width : 3 * width], weights[2, columns], 1, 1)
        dfirst.append(part)
    unit, inverse = moments(tok[...].astype(F32))
    part, gain_one, bias_one = norm_backward(
        jnp.concatenate(dfirst, 1), unit, inverse, gains[0:1]
    )
    norm_grads[0:1] = gain_one
    norm_grads[1:2] = bias_one
    input_grad[...] = (part + total[...])[:length]


def attention_weight_grads(halves, place, *refs):
    norms, refs = refs[:halves], refs[halves:]
    inputs, refs = refs[: 4 * halves], refs[4 * halves :]
    keep, *sends = refs[:5]
    first, context, low, dqkv, total, vectors, in_sems, sems = refs[5:]
    width = first.shape[2]
    owners, _, rows, columns = total.shape
    part = width // 2
    group = owners // 2
    moves = []
    for half in range(halves):
        for at, target in enumerate((first, dqkv, context, low)):
            source = inputs[halves * at + half]
            if at == 1:
                for which in range(3):
                    there = pl.ds(which * width, width)
                    pair = source.at[:, there], target.at[half, :, there]
                    moves.append((which, *pair))
            else:
                moves.append((0 if at == 0 else 2, source, target.at[half]))
    stages = [[], [], []]
    for at, (stage, source, target) in enumerate(moves):
        stages[stage].append(pltpu.make_async_copy(source, target, in_sems.at[at]))
    for copy in stages[0] + stages[1]:
        copy.start()
    norm = norms[0][...]
    for ref in norms[1:]:
        norm += ref[...]
    vectors[...] = jnp.zeros(vectors.shape, BF)
    vectors[0:1, :width] = norm[0:1].astype(BF)
    vectors[0:1, width:] = norm[1:2].astype(BF)
    vectors[1:2, :width] = norm[2:3].astype(BF)
    vectors[1:2, width:] = norm[3:4].astype(BF)

    def project(left, right, which):
        def body(step):
            chosen = pl.ds(pl.multiple_of(step * part, 128), part)
            there = pl.ds(which % 3 * width, width)
            value = dot(left[0, :, chosen], right[0, :, there], 0, 0)
            for half in range(1, halves):
                value += dot(left[half, :, chosen], right[half, :, there], 0, 0)
            owner = pl.ds(step * group, group)
            target = pl.ds(which * width, width)
            total[owner, :, :, target] = value.astype(BF).reshape(group, 2, rows, width)

        lax.fori_loop(0, 2, lambda at, carry: (body(at), carry)[1], 0, unroll=2)

    results = []

    def send(row):
        there = pl.ds(row * owners, owners)
        mine = pl.multiple_of(place[2 * row + 1], 128)
        pairs = [(total.at[:, place[0], :, pl.ds(mine, columns // 2)], keep.at[there])]
        for piece in range(2):
            some = pl.ds(piece * group, group)
            target = sends[2 * row + piece].at[pl.ds(0, group)]
            pairs.append((total.at[some, place[2], :, pl.ds(mine, columns // 2)], target))
        for source, target in pairs:
            results.append(pltpu.make_async_copy(source, target, sems.at[len(results)]))
            results[-1].start()

    wait_copies(stages[0])
    for copy in stages[2]:
        copy.start()
    project(first, dqkv, 0)
    wait_copies(stages[1])
    project(first, dqkv, 1)
    wait_copies(stages[2])
    project(first, dqkv, 2)
    project(context, low, 3)
    send(0)
    send(1)
    for source, target in ((vectors, keep.at[2 * owners]), (vectors, sends[3].at[group])):
        results.append(pltpu.make_async_copy(source, target, sems.at[len(results)]))
        results[-1].start()
    wait_copies(results)


ANYWHERE = pl.BlockSpec(memory_space=pl.ANY)
SCALARS = pl.BlockSpec(memory_space=pltpu.SMEM)
WHOLE = pl.BlockSpec(memory_space=pltpu.VMEM)


def one_of(array, index):
    tail = (0,) * (array.ndim - 1)
    return pl.BlockSpec((None,) + array.shape[1:], lambda step: (index,) + tail)


def shaped(shape, dtype=BF):
    return jax.ShapeDtypeStruct(shape, dtype)


def call(kernel, out_shape, in_specs, out_specs, scratch, args, time):
    return pl.pallas_call(
        kernel,
        grid=(1,),
        out_shape=out_shape,
        in_specs=in_specs,
        out_specs=out_specs,
        scratch_shapes=scratch,
        compiler_params=pltpu.CompilerParams(vmem_limit_bytes=60 * MIB),
        cost_estimate=pl.CostEstimate(
            flops=1024, bytes_accessed=int(1.5e6 * time), transcendentals=0
        ),
    )(*args)


def add(left, right):
    return (left.astype(F32) + right.astype(F32)).astype(BF)


def per_device(
    tokens,
    token_type,
    mlm_mask,
    cotangent,
    ln1_gain,
    ln1_bias,
    w_qkv,
    w_out,
    ln2_gain,
    ln2_bias,
    w_up,
    w_down,
):
    halves, length, width = tokens.shape
    shards, replicas = lax.axis_size("fsdp"), lax.axis_size("dp")
    shard, replica = lax.axis_index("fsdp"), lax.axis_index("dp")
    rows = width // shards
    lines = shards // 2
    line, side = shard // 2, shard % 2
    columns = w_up.shape[2] // replicas
    padded = -(-length // 16) * 16
    main = -(-PATCHES // 16) * 16
    tail = PATCHES // 16 * 16
    ringed = rows % 32 == 0 and lines == 4
    extra = 16 if ringed else 0
    spans = rows if ringed else width

    def swap(axis, size, bit):
        return lambda value: lax.ppermute(value, axis, [(i, i ^ bit) for i in range(size)])

    swap_core = swap("dp", replicas, 1)
    swap_row = swap("dp", replicas, 2)
    swap_side = swap("fsdp", shards, 1)

    def step_line(value):
        return lax.ppermute(value, "fsdp", [(i, (i + 2) % shards) for i in range(shards)])

    def all_replicas(value):
        across = swap_row(value)
        return jnp.stack([value, swap_core(value), across, swap_core(across)])

    def in_order(found):
        return [
            lax.dynamic_index_in_dim(found, jnp.bitwise_xor(replica, at), 0, keepdims=False)
            for at in range(4)
        ]

    def shift_line(value, steps):
        return lax.ppermute(value, "fsdp", [(i, (i + 2 * steps) % shards) for i in range(shards)])

    def cross(value):
        return lax.ppermute(
            value, "fsdp", [(i, ((i + 6) % shards) ^ 1) for i in range(shards)]
        )

    def owner(steps, other):
        return 2 * jnp.mod(line - steps, lines) + jnp.bitwise_xor(side, other)

    order = [(steps, other) for steps in range(lines) for other in range(2)]

    clock = [jnp.zeros((), jnp.int32)]

    def tied(value):
        return lax.optimization_barrier((value, clock[0]))[0]

    def wait(*values):
        found = lax.optimization_barrier((clock[0], *values))
        clock[0] = found[0]
        return found[1] if len(values) == 1 else found[1:]

    block = jnp.where(
        replica < 3,
        lax.dynamic_slice(w_qkv, (0, jnp.minimum(replica, 2) * width), (rows, width)),
        w_out,
    )
    vectors = jnp.stack([ln1_gain, ln1_bias, ln2_gain, ln2_bias])
    kinds_here = token_type[:, 0]
    image_counts = jnp.sum(mlm_mask * token_type, 1)
    text_counts = jnp.sum(mlm_mask, 1) - image_counts
    if ringed:
        facts = jnp.concatenate([kinds_here, text_counts, image_counts]).astype(BF)
        facts = jnp.concatenate([vectors.reshape(-1), facts])
        fact_row = jnp.zeros((extra, width), BF).at[0, : facts.shape[0]].set(facts)
        block = jnp.concatenate([block, fact_row], 0)
    expert_block = jnp.concatenate(
        [
            lax.dynamic_slice(w_up, (0, 0, replica * columns), (2, rows, columns)),
            lax.dynamic_slice(w_down, (0, replica * columns, 0), (2, columns, rows)).transpose(
                0, 2, 1
            ),
        ],
        0,
    )
    def pad_rows(value):
        return jnp.pad(value, ((0, 0), (0, padded - length), (0, 0)))

    if ringed:
        span = rows
        side_block = swap_side(block)
        ring = [shift_line(block, steps) for steps in range(1, lines)]
        row_block = swap_row(block)
        experts, near = [expert_block, step_line(expert_block)], [swap_side(expert_block)]
        dmixed = pad_rows(cotangent * mlm_mask[..., None].astype(BF))
        dmixed_row = swap_row(dmixed)
        wait(side_block, *ring, row_block)
        lined = jnp.concatenate([side_block, *ring], 0)
        side_ring = swap_side(tied(jnp.concatenate(ring, 0)))
        row_lined = swap_row(tied(lined))
        core_parts = [swap_core(tied(part)) for part in (block, row_block, lined)]
        wait(dmixed_row, near[0], *core_parts)
        grads = [dmixed, swap_core(tied(dmixed)), dmixed_row]
        tok = pad_rows(tied(tokens))
        wait(experts[1])
        experts.append(step_line(tied(experts[1])))
        wait(side_ring, row_lined, tok)
        row_side_ring = swap_row(tied(side_ring))
        near.append(swap_side(tied(experts[1])))
        core_parts += [swap_core(tied(part)) for part in (side_ring, row_lined)]
        wait(*core_parts[3:], grads[1])
        wait(experts[2])
        experts.append(step_line(tied(experts[2])))
        wait(row_side_ring)
        core_parts.append(swap_core(tied(row_side_ring)))
        wait(core_parts[5], near[1])
        near.append(swap_side(tied(experts[2])))
        first_line = [(0, 0)]
        later = [(steps, 0) for steps in range(1, lines)]
        later_sides = [(steps, 1) for steps in range(1, lines)]
        held = [
            (0, block, first_line),
            (0, lined, [(0, 1)] + later),
            (0, side_ring, later_sides),
            (2, row_block, first_line),
            (2, row_lined, [(0, 1)] + later),
            (2, row_side_ring, later_sides),
            (1, core_parts[0], first_line),
            (3, core_parts[1], first_line),
            (1, core_parts[2], [(0, 1)] + later),
            (1, core_parts[3], later_sides),
            (3, core_parts[4], [(0, 1)] + later),
            (3, core_parts[5], later_sides),
        ]
        attn_pieces = [part for _, part, _ in held]
        spots = [(rel, spot) for rel, _, spots_of in held for spot in spots_of]
        attn_place = jnp.stack(
            [
                value
                for rel, spot in spots
                for value in (jnp.bitwise_xor(replica, rel), owner(*spot) * rows)
            ]
            + [owner(*spot) for _, spot in spots]
        ).astype(jnp.int32)
        expert_place = jnp.stack([owner(*at) * rows for at in order]).astype(jnp.int32)
    else:
        span = 0
        whole = lax.all_gather(block, "fsdp", axis=0, tiled=True)
        attn_pieces = [jnp.stack(in_order(all_replicas(whole)))]
        attn_place = jnp.zeros((1,), jnp.int32)
        gains = lax.all_gather(vectors, "fsdp", axis=1, tiled=True).astype(F32)
        expert_pieces = [lax.all_gather(expert_block, "fsdp", axis=1, tiled=True)]
        expert_place = jnp.zeros((1,), jnp.int32)
        kinds = all_replicas(kinds_here).T
        counts = jnp.stack([jnp.sum(text_counts), jnp.sum(image_counts)])
        counts = lax.psum(counts, ("fsdp", "dp"))
        dmixed = pad_rows(cotangent * mlm_mask[..., None].astype(BF))
        tok = pad_rows(tokens)
        dmixed_row = swap_row(dmixed)
        grads = [dmixed, swap_core(dmixed), dmixed_row]
    attn_weights = pltpu.VMEM((4, width, width), BF)
    head_probs = pltpu.VMEM((HEADS, padded, padded), BF)
    states_of, kept = [], []
    for half in range(halves):
        fresh = ringed and half == 0
        sources = attn_pieces if half == 0 or not ringed else [all_weights]
        first_in, qkv, probs, context, hidden, second_in, *found = call(
            functools.partial(attention_forward, span if fresh else 0, length, len(sources)),
            [
                shaped((padded, width)),
                shaped((padded, 3 * width)),
                shaped((HEADS, padded, padded)),
                shaped((padded, width)),
                shaped((padded, width), F32),
                shaped((padded, width)),
            ]
            + [shaped((4, width, width)), shaped((4, shards, 16, width)), shaped((4, width), F32)]
            * fresh,
            [SCALARS, one_of(tok, half)] + [WHOLE] * (not fresh) + [ANYWHERE] * len(sources),
            [ANYWHERE] * 6 + [ANYWHERE, ANYWHERE, WHOLE] * fresh,
            [
                pltpu.VMEM((4, shards, 16, width), BF),
                pltpu.SemaphoreType.DMA((4 * shards,)),
            ]
            * fresh
            + [
                pltpu.VMEM((padded, width), BF),
                pltpu.VMEM((padded, 3 * width), BF),
                head_probs,
                pltpu.VMEM((padded, width), BF),
                pltpu.VMEM((padded, width), F32),
                pltpu.VMEM((padded, width), BF),
                attn_weights,
                pltpu.SemaphoreType.DMA((4 * shards,)),
                pltpu.SemaphoreType.DMA((7,)),
            ]
            + [pltpu.VMEM((4, width), F32)] * fresh,
            (tied(attn_place), tok, *([] if fresh else [gains]), *sources),
            time=9,
        )
        kept.append((first_in, qkv, probs, context, hidden))
        if half == 0:
            all_weights = attn_pieces[0]
            if ringed:
                all_weights, facts, gains = found
                wait(gains)
        if half == 0 or not ringed:
            states_of.append(
                [second_in, swap_core(tied(second_in)), swap_row(tied(second_in))]
            )
        if half == 0 and ringed:
            wait(experts[3], near[2], states_of[0][1])
            near.append(swap_side(tied(experts[3])))
    if ringed:
        wait(second_in, states_of[0][2], near[2], near[3])
        beside_core = swap_core(tied(second_in))
        grads.append(swap_core(tied(dmixed_row)))
        states_of[0].append(swap_core(tied(states_of[0][2])))
        wait(grads[3], beside_core, states_of[0][3])
        before_row = clock[0]
        states_of.append([second_in, beside_core, swap_row(tied(second_in))])
        numbers = facts[:, :, 0, 4 * rows : 4 * rows + 3 * halves].astype(F32)
        kinds = lax.dynamic_index_in_dim(numbers, shard, 1, keepdims=False)
        kinds = jnp.stack(
            [
                lax.dynamic_index_in_dim(kinds, jnp.bitwise_xor(replica, rel), 0, keepdims=False)
                for rel in range(4)
            ]
        )
        kinds = kinds[:, :halves].astype(jnp.int32).T
        counts = numbers.reshape(-1, 3, halves).sum((0, 2))[1:].astype(jnp.int32)
        expert_pieces = [part for both in zip(experts, near) for part in both]
        states_of[1].append(swap_core(states_of[1][2]))
    else:
        grads.append(swap_core(dmixed_row))
        for states in states_of:
            states.append(swap_core(states[2]))

    left = padded - tail
    expert_scratch = [
        pltpu.VMEM((4, width, columns), BF),
        *[pltpu.VMEM((5, main, width), BF)] * 2,
        *[pltpu.VMEM((5, main, columns), BF)] * 2,
        *[pltpu.VMEM((4 * left, width), BF)] * 2,
        *[pltpu.VMEM((2, padded, width), BF)] * 4,
        pltpu.SemaphoreType.DMA((len(expert_pieces),)),
        pltpu.SemaphoreType.DMA((8,)),
        pltpu.SemaphoreType.DMA((8,)),
        pltpu.SemaphoreType.DMA((14,)),
    ]
    acts, dpres, outs, arriving = [], [], [], []
    for half in range(halves):
        act, dpre, keep_grad, send_grad, keep_out, send_out = call(
            functools.partial(expert_layer, half, main, tail),
            [shaped((5, main, columns))] * 2 + [shaped((2, padded, width))] * 4,
            [SCALARS] * 2 + [ANYWHERE] * (8 + len(expert_pieces)),
            [ANYWHERE] * 6,
            expert_scratch,
            (tied(expert_place), kinds[half], *states_of[half], *grads, *expert_pieces),
            time=12.5,
        )
        acts.append(act)
        dpres.append(dpre)
        if half == 0:
            wait(states_of[1][2])
        else:
            wait(arriving[half - 1][1])
        summed = add(keep_grad, swap_core(tied(send_grad)))
        outs.append((keep_out, swap_core(tied(send_out))))
        if half + 1 < halves:
            wait(summed, outs[-1][1])
        arriving.append((summed, swap_row(summed[1])))

    piece_count = len(expert_pieces)
    if ringed:
        spots = [(0, 0), (1, 0), (2, 0), (2, 1), (3, 0), (4, 0), (5, 0), (6, 0)]
        grad_sizes = [1, 1, 2, 1, 1, 1, 1]
    else:
        spots, grad_sizes = [(0, 0)], [1]
    expert_parts = call(
        functools.partial(expert_weight_grads, main, tail, halves, spots),
        [shaped((size, 4, spans, columns)) for size in grad_sizes],
        [SCALARS] * 2 + [ANYWHERE] * (4 * halves + 4 + 2 * halves),
        [ANYWHERE] * len(grad_sizes),
        [
            pltpu.VMEM((4, width, columns), F32),
            pltpu.VMEM((4, width, columns), BF),
            *[pltpu.VMEM((5 * halves, main, width), BF)] * 2,
            *[pltpu.VMEM((5 * halves, main, columns), BF)] * 2,
            pltpu.SemaphoreType.DMA((piece_count, 4)),
            pltpu.SemaphoreType.DMA((halves, 8)),
            pltpu.SemaphoreType.DMA((halves, 8)),
            pltpu.SemaphoreType.DMA((halves, 5, 2)),
        ],
        (
            tied(expert_place),
            kinds.reshape(-1),
            *[state for states in states_of for state in states],
            *grads,
            *acts,
            *dpres,
        ),
        time=13.5,
    )

    wait(expert_parts[0])
    if ringed:
        direct = shift_line(tied(expert_parts[2]), lines - 1)
        sent_two = swap_side(tied(expert_parts[4]))
    wait(outs[-1][1])
    out_sum = jnp.stack([add(*pair) for pair in outs])
    out_rest = None
    lows, dqkvs, norm_parts, input_grads = [], [], [], []
    for half in range(halves):
        first_in, qkv, probs, context, hidden = kept[half]
        summed, far = arriving[half]
        low, dqkv, input_grad, norm_grads = call(
            functools.partial(attention_backward, length),
            [
                shaped((padded, width)),
                shaped((padded, 3 * width)),
                shaped((length, width), F32),
                shaped((4, width), F32),
            ],
            [one_of(tok, half), WHOLE, one_of(summed, 0), WHOLE, one_of(dmixed, half), WHOLE]
            + [ANYWHERE] * 4,
            [WHOLE] * 4,
            [
                pltpu.VMEM((padded, 3 * width), BF),
                head_probs,
                attn_weights,
                pltpu.VMEM((padded, width), F32),
                pltpu.SemaphoreType.DMA((4,)),
            ],
            (tok, tied(gains), summed, far, dmixed, hidden, qkv, probs, all_weights, expert_parts[0]),
            time=10,
        )
        wait(norm_grads)
        if half == 0:
            wait(arriving[1][1])
            out_rest = swap_row(tied(out_sum[:, 1]))
            if ringed:
                current = step_line(tied(add(expert_parts[3], wait(sent_two))))
                sent_three = swap_side(tied(expert_parts[6]))
        elif ringed:
            direct = wait(direct)
            sent_home = swap_side(tied(add(expert_parts[1], direct[1:2])))
        lows.append(low)
        dqkvs.append(dqkv)
        norm_parts.append(norm_grads)
        input_grads.append(input_grad)
    input_grad = jnp.stack(input_grads)

    core, row = replica % 2, replica // 2
    grad_place = jnp.stack([core, row * 2 * width, 1 - core, (1 - row) * 2 * width])
    grad_place = grad_place.astype(jnp.int32)
    owners = shards if ringed else 2
    core_rows = width // (2 * owners)
    keep, *sends = call(
        functools.partial(attention_weight_grads, halves),
        [
            shaped((size, core_rows, 2 * width))
            for size in (2 * owners + 1, *[owners // 2] * 3, owners // 2 + 1)
        ],
        [SCALARS] + [WHOLE] * halves + [ANYWHERE] * (4 * halves),
        [ANYWHERE] * 5,
        [
            *[pltpu.VMEM((halves, padded, width), BF)] * 3,
            pltpu.VMEM((halves, padded, 3 * width), BF),
            pltpu.VMEM((owners, 2, core_rows, 4 * width), BF),
            pltpu.VMEM((core_rows, 2 * width), BF),
            pltpu.SemaphoreType.DMA((6 * halves,)),
            pltpu.SemaphoreType.DMA((8,)),
        ],
        (
            tied(grad_place),
            *norm_parts,
            *[kept[h][0] for h in range(halves)],
            *dqkvs,
            *[kept[h][3] for h in range(halves)],
            *lows,
        ),
        time=8.5,
    )
    wait(keep, out_rest)
    if ringed:
        ready = add(wait(current), add(expert_parts[5], wait(sent_three)))
    received = [swap_core(tied(part)) for part in sends]
    divisor = counts.astype(F32)[:, None, None]

    def join_replicas(value, axis, row_axis):
        across = swap_row(value)
        mine, other = value, swap_core(value)
        far, far_other = across, swap_core(across)
        near_parts = jnp.where(core == 0, mine, other), jnp.where(core == 0, other, mine)
        far_parts = jnp.where(core == 0, far, far_other), jnp.where(core == 0, far_other, far)
        near_part = jnp.concatenate(near_parts, axis)
        far_part = jnp.concatenate(far_parts, axis)
        return jnp.concatenate(
            [jnp.where(row == 0, near_part, far_part), jnp.where(row == 0, far_part, near_part)],
            row_axis,
        )

    if ringed:
        current = step_line(tied(ready))
        received = wait(*received)
        half_shards = shards // 2
        parts = [
            add(keep[at * half_shards : (at + 1) * half_shards], received[at][:half_shards])
            for at in range(4)
        ]
        vector_block = add(keep[-1, :8], received[3][-1, :8])

        def by_side(value, other):
            pairs_of = value.reshape(-1, 2, *value.shape[1:])
            return lax.dynamic_index_in_dim(
                pairs_of, jnp.bitwise_xor(side, other), 1, keepdims=False
            )

        def with_vectors(value):
            return jnp.concatenate([value.reshape(-1, 2 * width), vector_block], 0)

        def split_vectors(value):
            return value[:-8].reshape(-1, core_rows, 2 * width), value[-8:]

        first_sent = swap_row(tied(with_vectors(parts[2])))
        both = jnp.concatenate([parts[1], parts[3]], 0)
        second_sent = swap_side(tied(by_side(both, 1)))
        home = add(wait(sent_home), expert_parts[0])
        home = add(home, direct[0:1])
        expert_mine = add(wait(current), home)[0]
        expert_row = swap_row(tied(expert_mine))
        expert_core = swap_core(tied(expert_mine))
        first_done, second_done = wait(first_sent, second_sent)
        first_done, vectors_done = split_vectors(first_done)
        first = add(parts[0], first_done)
        vector_block = add(vector_block, vectors_done)
        first_next = swap_side(tied(with_vectors(by_side(first, 1))))
        second = add(by_side(both, 0), second_done)
        middle = lines // 2
        second_next = swap_row(tied(second[middle:]))
        first_last, second_last, *_ = wait(first_next, second_next, expert_row, expert_core)
        first_last, vectors_done = split_vectors(first_last)
        first = add(by_side(first, 0), first_last)
        vector_block = add(vector_block, vectors_done)
        second = add(second[:middle], second_last)
        lined = jnp.concatenate([first, second], 0)

        def lined_block(steps):
            return with_vectors(
                lax.dynamic_index_in_dim(lined, jnp.mod(line - steps, lines), 0)
            )

        expert_last = swap_core(tied(expert_row))
        arrived = [
            shift_line(tied(lined_block(steps)), lines - steps) for steps in range(1, lines)
        ]
        wait(*arrived, expert_last)
        expert_all = jnp.stack([expert_mine, expert_core, expert_row, expert_last])
        reduced = sum([part.astype(F32) for part in arrived], lined_block(0).astype(F32))
        vectors_sum = reduced[core_rows : core_rows + 2].reshape(4, width)
        vectors_sum = lax.dynamic_slice_in_dim(vectors_sum, shard * rows, rows, 1)
        attn_mine = reduced[:core_rows].astype(BF)
        attn_grad = join_replicas(tied(attn_mine), 0, 1)
    else:
        summed = add(keep, jnp.concatenate(received, 0))
        mine = add(summed[:owners], swap_row(summed[owners:-1]))
        attn_grad = join_replicas(mine, 1, 2).reshape(width, 4 * width)
        attn_grad = lax.psum_scatter(attn_grad, "fsdp", scatter_dimension=0, tiled=True)
        vectors_sum = functools.reduce(jnp.add, norm_parts)
        vectors_sum = lax.psum_scatter(vectors_sum, "fsdp", scatter_dimension=1, tiled=True)
        vectors_sum = lax.psum(vectors_sum, "dp")
        expert_mine = lax.psum_scatter(
            expert_parts[0][0], "fsdp", scatter_dimension=1, tiled=True
        )
        expert_all = all_replicas(expert_mine)
    expert_all = in_order(expert_all)
    up_grad = jnp.concatenate([part[:2] for part in expert_all], 2).astype(F32) / divisor
    down_grad = (
        jnp.concatenate([part[2:] for part in expert_all], 2).astype(F32).transpose(0, 2, 1)
        / divisor
    )
    mixed = jnp.stack(
        [
            (kept[h][4] + out_sum[h, 0].astype(F32) + out_rest[h].astype(F32))[:length]
            for h in range(halves)
        ]
    ).astype(BF)
    vector_grads = [vectors_sum[at] for at in range(4)]
    attn_grad = attn_grad.astype(F32)
    return (
        mixed,
        input_grad,
        vector_grads[0],
        vector_grads[1],
        attn_grad[:, : 3 * width],
        attn_grad[:, 3 * width :],
        vector_grads[2],
        vector_grads[3],
        up_grad,
        down_grad,
        counts,
    )


def solution(mesh):
    return jax.shard_map(
        per_device,
        mesh=mesh,
        in_specs=(
            P(("fsdp", "dp"), None, None),
            P(("fsdp", "dp"), None),
            P(("fsdp", "dp"), None),
            P(("fsdp", "dp"), None, None),
            P("fsdp"),
            P("fsdp"),
            P("fsdp", None),
            P("fsdp", None),
            P("fsdp"),
            P("fsdp"),
            P(None, "fsdp", None),
            P(None, None, "fsdp"),
        ),
        out_specs=(
            P(("fsdp", "dp"), None, None),
            P(("fsdp", "dp"), None, None),
            P("fsdp"),
            P("fsdp"),
            P("fsdp", None),
            P("fsdp", None),
            P("fsdp"),
            P("fsdp"),
            P(None, "fsdp", None),
            P(None, None, "fsdp"),
            P(),
        ),
        check_vma=False,
    )
```

```python
import functools

import jax
import jax.numpy as jnp
from jax import lax
from jax.experimental import pallas as pl
from jax.experimental.pallas import tpu as pltpu
from jax.sharding import PartitionSpec as P

HEADS = 12
HEAD = 64
TILE = 256
WINDOW = 3
PATCHES = 197
MIB = 1024 * 1024
BF = jnp.bfloat16
F32 = jnp.float32


def dot(left, right, left_dim=1, right_dim=0):
    return lax.dot_general(
        left, right, (((left_dim,), (right_dim,)), ((), ())), preferred_element_type=F32
    )


def moments(values):
    center = values - jnp.mean(values, -1, keepdims=True)
    inverse = lax.rsqrt(jnp.mean(center * center, -1, keepdims=True) + 1e-06)
    return center * inverse, inverse


def norm_backward(grad, unit, inverse, gain):
    scaled = grad * gain
    slope = jnp.mean(scaled * unit, -1, keepdims=True)
    result = inverse * (scaled - jnp.mean(scaled, -1, keepdims=True) - unit * slope)
    return result, jnp.sum(grad * unit, 0, keepdims=True), jnp.sum(grad, 0, keepdims=True)


def gelu_parts(pre):
    share = 0.5 + 0.5 * lax.erf(pre * 0.7071067811865476)
    density = jnp.exp(-0.5 * pre * pre) * 0.3989422804014327
    return pre * share, share + pre * density


def run_copies(copies):
    for copy in copies:
        copy.start()
    for copy in copies:
        copy.wait()


def tile(at):
    return pl.ds(pl.multiple_of(at * TILE, TILE), TILE)


def every(count, body):
    lax.fori_loop(0, count, lambda at, carry: (body(at), carry)[1], 0, unroll=min(6, count))


def start_copies(pairs, sems):
    copies = [
        pltpu.make_async_copy(source, target, sems.at[at])
        for at, (source, target) in enumerate(pairs)
    ]
    for copy in copies:
        copy.start()
    return copies


def wait_copies(copies):
    for copy in copies:
        copy.wait()


def gather_vectors(facts, count, rows, width):
    lane = lax.broadcasted_iota(jnp.int32, (8, width), 1)
    vectors = [jnp.zeros((8, width), F32)] * 4
    for owner in range(count):
        sent = facts[0, owner, 0:8].astype(F32)
        inside = (lane >= owner * rows) & (lane < (owner + 1) * rows)
        for at in range(4):
            shift = (owner - at) * rows % width
            moved = pltpu.roll(sent, shift, 1) if shift else sent
            row = jnp.broadcast_to(moved[0:1], (8, width))
            vectors[at] = jnp.where(inside, row, vectors[at])
    return jnp.concatenate([vector[0:1] for vector in vectors], 0)


def attention_forward(rows, length, pieces, place, tok, *refs):
    fresh = rows > 0
    if fresh:
        gains, refs = refs[-1], refs[:-1]
    else:
        gains, refs = refs[0], refs[1:]
    sources, refs = refs[:pieces], refs[pieces:]
    if fresh:
        step = rows + 16
        sources = [
            ref.at[pl.ds(first, step)] for ref in sources for first in range(0, ref.shape[0], step)
        ]
        pieces = len(sources)
    first_out, qkv_out, probs_out, context_out, hidden_out, second_out = refs[:6]
    if fresh:
        weights_out, facts_out, gains_out, refs = refs[6], refs[7], refs[8], refs[9:]
        facts, fact_sems, refs = refs[0], refs[1], refs[2:]
    else:
        refs = refs[6:]
    first_in, qkv, probs, context, hidden, second_in, weights, sems, out_sems = refs
    if fresh:
        fact_copies = [
            pltpu.make_async_copy(
                source.at[pl.ds(rows, 16)], facts.at[place[2 * at], place[2 * pieces + at]], fact_sems.at[at]
            )
            for at, source in enumerate(sources)
        ]
        for copy in fact_copies:
            copy.start()
        pairs = [
            (
                source.at[pl.ds(0, rows)],
                weights.at[place[2 * at], pl.ds(pl.multiple_of(place[2 * at + 1], 32), rows)],
            )
            for at, source in enumerate(sources)
        ]
    else:
        pairs = [(source, weights) for source in sources]
    copies = start_copies(pairs, sems)
    if fresh:
        wait_copies(fact_copies)
        shards = facts.shape[1]
        gains[...] = gather_vectors(facts, shards, rows, tok.shape[1])
        gains_out[...] = gains[...]
        fact_copy = pltpu.make_async_copy(facts, facts_out, fact_sems.at[0])
        fact_copy.start()
    inputs = tok[...].astype(F32)
    padded, width = inputs.shape
    tiles = width // TILE
    unit, _ = moments(inputs)
    first_in[...] = (unit * gains[0:1] + gains[1:2]).astype(BF)
    wait_copies(copies)
    results = [pltpu.make_async_copy(first_in, first_out, out_sems.at[0])]
    results[0].start()
    if fresh:
        results.append(pltpu.make_async_copy(weights, weights_out, out_sems.at[6]))
        results[-1].start()
        results.append(fact_copy)

    def project(at):
        block = weights[at // tiles, :, tile(at % tiles)]
        qkv[:, tile(at)] = dot(first_in[...], block).astype(BF)

    every(3 * tiles, project)
    results.append(pltpu.make_async_copy(qkv, qkv_out, out_sems.at[1]))
    results[-1].start()
    pair = 2 * HEAD
    low_half = lax.broadcasted_iota(jnp.int32, (padded, pair), 1) < HEAD
    real = lax.broadcasted_iota(jnp.int32, (padded, padded), 1) < length

    def heads(at):
        lanes = pl.multiple_of(at * pair, pair)
        query = qkv[:, pl.ds(lanes, pair)]
        key = qkv[:, pl.ds(width + lanes, pair)]
        value = qkv[:, pl.ds(2 * width + lanes, pair)]
        total = jnp.zeros((padded, pair), F32)
        for half in range(2):
            keep = low_half if half == 0 else jnp.logical_not(low_half)
            scores = dot(jnp.where(keep, query, 0), key, 1, 1) * HEAD ** (-0.5)
            scores = jnp.where(real, scores, -1e30)
            grown = jnp.exp(scores - jnp.max(scores, -1, keepdims=True))
            prob = (grown / jnp.sum(grown, -1, keepdims=True)).astype(BF)
            probs[2 * at + half] = prob
            total += dot(prob, jnp.where(keep, value, 0))
        context[:, pl.ds(lanes, pair)] = total.astype(BF)

    every(HEADS // 2, heads)
    results.append(pltpu.make_async_copy(probs, probs_out, out_sems.at[2]))
    results[-1].start()
    results.append(pltpu.make_async_copy(context, context_out, out_sems.at[3]))
    results[-1].start()

    def project_out(at):
        added = dot(context[...], weights[3, :, tile(at)])
        hidden[:, tile(at)] = tok[:, tile(at)].astype(F32) + added

    every(tiles, project_out)
    results.append(pltpu.make_async_copy(hidden, hidden_out, out_sems.at[4]))
    results[-1].start()
    unit, _ = moments(hidden[...])
    second_in[...] = (unit * gains[2:3] + gains[3:4]).astype(BF)
    results.append(pltpu.make_async_copy(second_in, second_out, out_sems.at[5]))
    results[-1].start()
    wait_copies(results)


def block_copies(sources, target, sems, main, tail):
    left = sources[0].shape[0] - tail
    pairs = [
        (source.at[pl.ds(tail, left)], target.at[0, pl.ds(at * left, left)])
        for at, source in enumerate(sources)
    ]
    pairs += [(source.at[pl.ds(0, main)], target.at[1 + at]) for at, source in enumerate(sources)]
    return [
        pltpu.make_async_copy(source, there, sems.at[at])
        for at, (source, there) in enumerate(pairs)
    ]


def expert_copies(place, pieces, weights, sems):
    copies = []
    for at, piece in enumerate(pieces):
        first = pl.multiple_of(place[at], 32)
        copies.append(
            pltpu.make_async_copy(
                piece, weights.at[:, pl.ds(first, piece.shape[1])], sems.at[at]
            )
        )
    return copies


def expert_layer(half, main, tail, place, kinds, *refs):
    states, grads = refs[:4], refs[4:8]
    pieces, refs = refs[8:-21], refs[-21:]
    act_out, dpre_out = refs[:2]
    results = refs[2:6]
    weights, state, grad, act, dpre, state_end, grad_end, *held = refs[6:]
    sems, state_sems, grad_sems, out_sems, held = held[-4], held[-3], held[-2], held[-1], held[:-4]
    width, hidden = weights.shape[1:]
    left = state_end.shape[0] // 4
    state_copies = block_copies(states, state, state_sems, main, tail)
    grad_copies = block_copies([ref.at[half] for ref in grads], grad, grad_sems, main, tail)
    copies = expert_copies(place, pieces, weights, sems)
    copies += state_copies[:4] + grad_copies[:4]
    for copy in copies:
        copy.start()
    spare = main - 4 * left
    state[0, 4 * left :] = jnp.zeros((spare, width), BF)
    grad[0, 4 * left :] = jnp.zeros((spare, width), BF)
    wait_copies(copies)
    for copy in state_copies[4:] + grad_copies[4:]:
        copy.start()
    spot = lax.broadcasted_iota(jnp.int32, (main, 1), 0)
    image = spot < PATCHES
    text = (spot % left + tail >= PATCHES) & (spot < 4 * left)

    def forward(at, expert, mine):
        def body(step):
            columns = tile(step)
            pre = dot(state[at], weights[expert, :, columns])
            dact = dot(grad[at], weights[2 + expert, :, columns])
            value, slope = gelu_parts(pre)
            act[at, :, columns] = jnp.where(mine, value, 0).astype(BF)
            dpre[at, :, columns] = jnp.where(mine, dact * slope, 0).astype(BF)

        every(hidden // TILE, body)

    forward(0, 0, text)
    outs = []
    for index, (source, target) in enumerate(((act, act_out), (dpre, dpre_out))):
        outs.append(pltpu.make_async_copy(source.at[0], target.at[0], out_sems.at[index]))
        outs[-1].start()

    def end_body(step):
        columns = tile(step)
        rows = pl.ds(0, 4 * left)
        grad_end[:, columns] = dot(dpre[0, rows], weights[0, columns], 1, 1).astype(BF)
        state_end[:, columns] = dot(act[0, rows], weights[2, columns], 1, 1).astype(BF)

    every(width // TILE, end_body)
    for rel in range(4):
        at = rel + 1
        expert = kinds[rel]
        state_copies[4 + rel].wait()
        grad_copies[4 + rel].wait()
        forward(at, expert, image)
        for index, (source, target) in enumerate(((act, act_out), (dpre, dpre_out))):
            outs.append(
                pltpu.make_async_copy(source.at[at], target.at[at], out_sems.at[2 * at + index])
            )
            outs[-1].start()
        grad_to, out_to = held[rel % 2], held[2 + rel % 2]
        place_at = rel // 2
        end = rel * left

        def body(step):
            columns = tile(step)
            there = pl.ds(0, main)
            for source, weight, target, ends in (
                (dpre, weights.at[expert], grad_to, grad_end),
                (act, weights.at[2 + expert], out_to, state_end),
            ):
                value = dot(source[at], weight[columns], 1, 1)
                target[place_at, 0:tail, columns] = value[:tail].astype(BF)
                shared = ends[end : end + main - tail, columns].astype(F32)
                target[place_at, tail:main, columns] = (value[tail:] + shared).astype(BF)
                target[place_at, main:, columns] = ends[end + main - tail : end + left, columns]

        every(width // TILE, body)
    for index, (source, target) in enumerate(zip(held, results)):
        outs.append(pltpu.make_async_copy(source, target, out_sems.at[10 + index]))
        outs[-1].start()
    wait_copies(outs)


def expert_weight_grads(main, tail, halves, spots, place, kinds, *refs):
    states, refs = refs[: 4 * halves], refs[4 * halves :]
    grads, refs = refs[:4], refs[4:]
    acts, refs = refs[:halves], refs[halves:]
    dpres, refs = refs[:halves], refs[halves:]
    outs, rest = refs[:-10], refs[-10:]
    total, rounded, state, grad, act, dpre, sems, state_sems, grad_sems, rest_sems = rest
    width = total.shape[1]
    left = states[0].shape[0] - tail
    ready = []
    for half in range(halves):
        there = pl.ds(5 * half, 5)
        moves = block_copies(
            states[4 * half : 4 * half + 4], state.at[there], state_sems.at[half], main, tail
        )
        grad_moves = block_copies(
            [ref.at[half] for ref in grads], grad.at[there], grad_sems.at[half], main, tail
        )
        for block in range(5):
            spot = 5 * half + block
            needed = [
                pltpu.make_async_copy(
                    acts[half].at[block], act.at[spot], rest_sems.at[half, block, 0]
                ),
                pltpu.make_async_copy(
                    dpres[half].at[block], dpre.at[spot], rest_sems.at[half, block, 1]
                ),
            ]
            chosen = slice(0, 4) if block == 0 else slice(3 + block, 4 + block)
            needed += moves[chosen] + grad_moves[chosen]
            ready.append(needed)
    for needed in ready[:WINDOW]:
        for copy in needed:
            copy.start()
    spare = main - 4 * left
    for half in range(halves):
        state[5 * half, 4 * left :] = jnp.zeros((spare, width), BF)
        grad[5 * half, 4 * left :] = jnp.zeros((spare, width), BF)
    total[1] = jnp.zeros(total.shape[1:], F32)
    total[3] = jnp.zeros(total.shape[1:], F32)
    for at, needed in enumerate(ready):
        half, block = divmod(at, 5)
        expert = kinds[4 * half + block - 1] if block else 0
        for copy in (ready[at + WINDOW] if at + WINDOW < len(ready) else []):
            copy.start()
        wait_copies(needed)

        def body(step):
            columns = tile(step)
            up = dot(state[at, :, columns], dpre[at], 0, 0)
            down = dot(grad[at, :, columns], act[at], 0, 0)
            if at == 0:
                total[0, columns] = up
                total[2, columns] = down
            else:
                total[expert, columns] += up
                total[2 + expert, columns] += down

        every(width // TILE, body)
    copies = []
    for part in range(4):
        rounded[part] = total[part].astype(BF)
        for piece, (out, at) in enumerate(spots):
            first = pl.multiple_of(place[piece], 32)
            target = outs[out].at[at, part]
            copies.append(
                pltpu.make_async_copy(
                    rounded.at[part, pl.ds(first, target.shape[0])], target, sems.at[piece, part]
                )
            )
            copies[-1].start()
    wait_copies(copies)


def attention_backward(length, tok, gains, near, far, dmixed, hidden, *refs):
    qkv_from, probs_from, weights_from, refs = refs[0], refs[1], refs[2], refs[4:]
    low, dqkv, input_grad, norm_grads, qkv, probs, weights, total, sems = refs
    copies = start_copies(
        [(weights_from.at[pl.ds(3, 1)], weights.at[pl.ds(3, 1)])]
        + [(qkv_from, qkv), (probs_from, probs)]
        + [(weights_from.at[pl.ds(0, 3)], weights.at[pl.ds(0, 3)])],
        sems,
    )
    padded, width = tok.shape
    tiles = width // TILE
    unit, inverse = moments(hidden[...])
    second = near[...].astype(F32) + far[...].astype(F32)
    part, gain_two, bias_two = norm_backward(second, unit, inverse, gains[2:3])
    dhidden = dmixed[...].astype(F32) + part
    low[...] = dhidden.astype(BF)
    total[...] = dhidden
    norm_grads[2:3] = gain_two
    norm_grads[3:4] = bias_two
    copies[0].wait()

    def project_out(at):
        dqkv[:, tile(at)] = dot(low[...], weights[3, tile(at)], 1, 1).astype(BF)

    every(tiles, project_out)
    pair = 2 * HEAD
    low_half = lax.broadcasted_iota(jnp.int32, (padded, pair), 1) < HEAD
    copies[1].wait()
    copies[2].wait()

    def heads(at):
        lanes = pl.multiple_of(at * pair, pair)
        query = qkv[:, pl.ds(lanes, pair)]
        key = qkv[:, pl.ds(width + lanes, pair)]
        value = qkv[:, pl.ds(2 * width + lanes, pair)]
        upper = dqkv[:, pl.ds(lanes, pair)]
        dquery = jnp.zeros((padded, pair), F32)
        dkey = jnp.zeros((padded, pair), F32)
        dvalue = jnp.zeros((padded, pair), F32)
        for half in range(2):
            keep = low_half if half == 0 else jnp.logical_not(low_half)
            prob = probs[2 * at + half]
            wide = prob.astype(F32)
            upper_half = jnp.where(keep, upper, 0)
            dprob = dot(upper_half, value, 1, 1)
            dscore = (wide * (dprob - jnp.sum(dprob * wide, -1, keepdims=True))).astype(BF)
            dquery += dot(dscore, jnp.where(keep, key, 0))
            dkey += dot(dscore, jnp.where(keep, query, 0), 0, 0)
            dvalue += dot(prob, upper_half, 0, 0)
        dqkv[:, pl.ds(lanes, pair)] = (dquery * HEAD ** (-0.5)).astype(BF)
        dqkv[:, pl.ds(width + lanes, pair)] = (dkey * HEAD ** (-0.5)).astype(BF)
        dqkv[:, pl.ds(2 * width + lanes, pair)] = dvalue.astype(BF)

    every(HEADS // 2, heads)
    copies[3].wait()
    dfirst = []
    for at in range(tiles):
        columns = slice(at * TILE, (at + 1) * TILE)
        part = dot(dqkv[:, 0:width], weights[0, columns], 1, 1)
        part += dot(dqkv[:, width : 2 * width], weights[1, columns], 1, 1)
        part += dot(dqkv[:, 2 * width : 3 * width], weights[2, columns], 1, 1)
        dfirst.append(part)
    unit, inverse = moments(tok[...].astype(F32))
    part, gain_one, bias_one = norm_backward(
        jnp.concatenate(dfirst, 1), unit, inverse, gains[0:1]
    )
    norm_grads[0:1] = gain_one
    norm_grads[1:2] = bias_one
    input_grad[...] = (part + total[...])[:length]


def attention_weight_grads(halves, place, *refs):
    norms, refs = refs[:halves], refs[halves:]
    inputs, refs = refs[: 4 * halves], refs[4 * halves :]
    keep, *sends = refs[:5]
    first, context, low, dqkv, total, vectors, in_sems, sems = refs[5:]
    width = first.shape[2]
    owners, _, rows, columns = total.shape
    part = width // 2
    group = owners // 2
    moves = []
    for half in range(halves):
        for at, target in enumerate((first, dqkv, context, low)):
            source = inputs[halves * at + half]
            if at == 1:
                for which in range(3):
                    there = pl.ds(which * width, width)
                    pair = source.at[:, there], target.at[half, :, there]
                    moves.append((which, *pair))
            else:
                moves.append((0 if at == 0 else 2, source, target.at[half]))
    stages = [[], [], []]
    for at, (stage, source, target) in enumerate(moves):
        stages[stage].append(pltpu.make_async_copy(source, target, in_sems.at[at]))
    for copy in stages[0] + stages[1]:
        copy.start()
    norm = norms[0][...]
    for ref in norms[1:]:
        norm += ref[...]
    vectors[...] = jnp.zeros(vectors.shape, BF)
    vectors[0:1, :width] = norm[0:1].astype(BF)
    vectors[0:1, width:] = norm[1:2].astype(BF)
    vectors[1:2, :width] = norm[2:3].astype(BF)
    vectors[1:2, width:] = norm[3:4].astype(BF)

    def project(left, right, which):
        def body(step):
            chosen = pl.ds(pl.multiple_of(step * part, 128), part)
            there = pl.ds(which % 3 * width, width)
            value = dot(left[0, :, chosen], right[0, :, there], 0, 0)
            for half in range(1, halves):
                value += dot(left[half, :, chosen], right[half, :, there], 0, 0)
            owner = pl.ds(step * group, group)
            target = pl.ds(which * width, width)
            total[owner, :, :, target] = value.astype(BF).reshape(group, 2, rows, width)

        lax.fori_loop(0, 2, lambda at, carry: (body(at), carry)[1], 0, unroll=2)

    results = []

    def send(row):
        there = pl.ds(row * owners, owners)
        mine = pl.multiple_of(place[2 * row + 1], 128)
        pairs = [(total.at[:, place[0], :, pl.ds(mine, columns // 2)], keep.at[there])]
        for piece in range(2):
            some = pl.ds(piece * group, group)
            target = sends[2 * row + piece].at[pl.ds(0, group)]
            pairs.append((total.at[some, place[2], :, pl.ds(mine, columns // 2)], target))
        for source, target in pairs:
            results.append(pltpu.make_async_copy(source, target, sems.at[len(results)]))
            results[-1].start()

    wait_copies(stages[0])
    for copy in stages[2]:
        copy.start()
    project(first, dqkv, 0)
    wait_copies(stages[1])
    project(first, dqkv, 1)
    wait_copies(stages[2])
    project(first, dqkv, 2)
    project(context, low, 3)
    send(0)
    send(1)
    for source, target in ((vectors, keep.at[2 * owners]), (vectors, sends[3].at[group])):
        results.append(pltpu.make_async_copy(source, target, sems.at[len(results)]))
        results[-1].start()
    wait_copies(results)


ANYWHERE = pl.BlockSpec(memory_space=pl.ANY)
SCALARS = pl.BlockSpec(memory_space=pltpu.SMEM)
WHOLE = pl.BlockSpec(memory_space=pltpu.VMEM)


def one_of(array, index):
    tail = (0,) * (array.ndim - 1)
    return pl.BlockSpec((None,) + array.shape[1:], lambda step: (index,) + tail)


def shaped(shape, dtype=BF):
    return jax.ShapeDtypeStruct(shape, dtype)


def call(kernel, out_shape, in_specs, out_specs, scratch, args, time):
    return pl.pallas_call(
        kernel,
        grid=(1,),
        out_shape=out_shape,
        in_specs=in_specs,
        out_specs=out_specs,
        scratch_shapes=scratch,
        compiler_params=pltpu.CompilerParams(vmem_limit_bytes=60 * MIB),
        cost_estimate=pl.CostEstimate(
            flops=1024, bytes_accessed=int(1.5e6 * time), transcendentals=0
        ),
    )(*args)


def add(left, right):
    return (left.astype(F32) + right.astype(F32)).astype(BF)


def per_device(
    tokens,
    token_type,
    mlm_mask,
    cotangent,
    ln1_gain,
    ln1_bias,
    w_qkv,
    w_out,
    ln2_gain,
    ln2_bias,
    w_up,
    w_down,
):
    halves, length, width = tokens.shape
    shards, replicas = lax.axis_size("fsdp"), lax.axis_size("dp")
    shard, replica = lax.axis_index("fsdp"), lax.axis_index("dp")
    rows = width // shards
    lines = shards // 2
    line, side = shard // 2, shard % 2
    columns = w_up.shape[2] // replicas
    padded = -(-length // 16) * 16
    main = -(-PATCHES // 16) * 16
    tail = PATCHES // 16 * 16
    ringed = rows % 32 == 0 and lines == 4
    extra = 16 if ringed else 0
    spans = rows if ringed else width

    def swap(axis, size, bit):
        return lambda value: lax.ppermute(value, axis, [(i, i ^ bit) for i in range(size)])

    swap_core = swap("dp", replicas, 1)
    swap_row = swap("dp", replicas, 2)
    swap_side = swap("fsdp", shards, 1)

    def step_line(value):
        return lax.ppermute(value, "fsdp", [(i, (i + 2) % shards) for i in range(shards)])

    def all_replicas(value):
        across = swap_row(value)
        return jnp.stack([value, swap_core(value), across, swap_core(across)])

    def in_order(found):
        return [
            lax.dynamic_index_in_dim(found, jnp.bitwise_xor(replica, at), 0, keepdims=False)
            for at in range(4)
        ]

    def shift_line(value, steps):
        return lax.ppermute(value, "fsdp", [(i, (i + 2 * steps) % shards) for i in range(shards)])

    def cross(value):
        return lax.ppermute(
            value, "fsdp", [(i, ((i + 6) % shards) ^ 1) for i in range(shards)]
        )

    def owner(steps, other):
        return 2 * jnp.mod(line - steps, lines) + jnp.bitwise_xor(side, other)

    order = [(steps, other) for steps in range(lines) for other in range(2)]

    clock = [jnp.zeros((), jnp.int32)]

    def tied(value):
        return lax.optimization_barrier((value, clock[0]))[0]

    def wait(*values):
        found = lax.optimization_barrier((clock[0], *values))
        clock[0] = found[0]
        return found[1] if len(values) == 1 else found[1:]

    block = jnp.where(
        replica < 3,
        lax.dynamic_slice(w_qkv, (0, jnp.minimum(replica, 2) * width), (rows, width)),
        w_out,
    )
    vectors = jnp.stack([ln1_gain, ln1_bias, ln2_gain, ln2_bias])
    kinds_here = token_type[:, 0]
    image_counts = jnp.sum(mlm_mask * token_type, 1)
    text_counts = jnp.sum(mlm_mask, 1) - image_counts
    if ringed:
        facts = jnp.concatenate([kinds_here, text_counts, image_counts]).astype(BF)
        facts = jnp.concatenate([vectors.reshape(-1), facts])
        fact_row = jnp.zeros((extra, width), BF).at[0, : facts.shape[0]].set(facts)
        block = jnp.concatenate([block, fact_row], 0)
    expert_block = jnp.concatenate(
        [
            lax.dynamic_slice(w_up, (0, 0, replica * columns), (2, rows, columns)),
            lax.dynamic_slice(w_down, (0, replica * columns, 0), (2, columns, rows)).transpose(
                0, 2, 1
            ),
        ],
        0,
    )
    def pad_rows(value):
        return jnp.pad(value, ((0, 0), (0, padded - length), (0, 0)))

    if ringed:
        span = rows
        side_block = swap_side(block)
        ring = [shift_line(block, steps) for steps in range(1, lines)]
        row_block = swap_row(block)
        experts, near = [expert_block, step_line(expert_block)], [swap_side(expert_block)]
        dmixed = pad_rows(cotangent * mlm_mask[..., None].astype(BF))
        dmixed_row = swap_row(dmixed)
        wait(side_block, *ring, row_block)
        lined = jnp.concatenate([side_block, *ring], 0)
        side_ring = swap_side(tied(jnp.concatenate(ring, 0)))
        row_lined = swap_row(tied(lined))
        core_parts = [swap_core(tied(part)) for part in (block, row_block, lined)]
        wait(dmixed_row, near[0], *core_parts)
        grads = [dmixed, swap_core(tied(dmixed)), dmixed_row]
        tok = pad_rows(tied(tokens))
        wait(experts[1])
        experts.append(step_line(tied(experts[1])))
        wait(side_ring, row_lined, tok)
        row_side_ring = swap_row(tied(side_ring))
        near.append(swap_side(tied(experts[1])))
        core_parts += [swap_core(tied(part)) for part in (side_ring, row_lined)]
        wait(*core_parts[3:], grads[1])
        wait(experts[2])
        experts.append(step_line(tied(experts[2])))
        wait(row_side_ring)
        core_parts.append(swap_core(tied(row_side_ring)))
        wait(core_parts[5], near[1])
        near.append(swap_side(tied(experts[2])))
        first_line = [(0, 0)]
        later = [(steps, 0) for steps in range(1, lines)]
        later_sides = [(steps, 1) for steps in range(1, lines)]
        held = [
            (0, block, first_line),
            (0, lined, [(0, 1)] + later),
            (0, side_ring, later_sides),
            (2, row_block, first_line),
            (2, row_lined, [(0, 1)] + later),
            (2, row_side_ring, later_sides),
            (1, core_parts[0], first_line),
            (3, core_parts[1], first_line),
            (1, core_parts[2], [(0, 1)] + later),
            (1, core_parts[3], later_sides),
            (3, core_parts[4], [(0, 1)] + later),
            (3, core_parts[5], later_sides),
        ]
        attn_pieces = [part for _, part, _ in held]
        spots = [(rel, spot) for rel, _, spots_of in held for spot in spots_of]
        attn_place = jnp.stack(
            [
                value
                for rel, spot in spots
                for value in (jnp.bitwise_xor(replica, rel), owner(*spot) * rows)
            ]
            + [owner(*spot) for _, spot in spots]
        ).astype(jnp.int32)
        expert_place = jnp.stack([owner(*at) * rows for at in order]).astype(jnp.int32)
    else:
        span = 0
        whole = lax.all_gather(block, "fsdp", axis=0, tiled=True)
        attn_pieces = [jnp.stack(in_order(all_replicas(whole)))]
        attn_place = jnp.zeros((1,), jnp.int32)
        gains = lax.all_gather(vectors, "fsdp", axis=1, tiled=True).astype(F32)
        expert_pieces = [lax.all_gather(expert_block, "fsdp", axis=1, tiled=True)]
        expert_place = jnp.zeros((1,), jnp.int32)
        kinds = all_replicas(kinds_here).T
        counts = jnp.stack([jnp.sum(text_counts), jnp.sum(image_counts)])
        counts = lax.psum(counts, ("fsdp", "dp"))
        dmixed = pad_rows(cotangent * mlm_mask[..., None].astype(BF))
        tok = pad_rows(tokens)
        dmixed_row = swap_row(dmixed)
        grads = [dmixed, swap_core(dmixed), dmixed_row]
    attn_weights = pltpu.VMEM((4, width, width), BF)
    head_probs = pltpu.VMEM((HEADS, padded, padded), BF)
    states_of, kept = [], []
    for half in range(halves):
        fresh = ringed and half == 0
        sources = attn_pieces if half == 0 or not ringed else [all_weights]
        first_in, qkv, probs, context, hidden, second_in, *found = call(
            functools.partial(attention_forward, span if fresh else 0, length, len(sources)),
            [
                shaped((padded, width)),
                shaped((padded, 3 * width)),
                shaped((HEADS, padded, padded)),
                shaped((padded, width)),
                shaped((padded, width), F32),
                shaped((padded, width)),
            ]
            + [shaped((4, width, width)), shaped((4, shards, 16, width)), shaped((4, width), F32)]
            * fresh,
            [SCALARS, one_of(tok, half)] + [WHOLE] * (not fresh) + [ANYWHERE] * len(sources),
            [ANYWHERE] * 6 + [ANYWHERE, ANYWHERE, WHOLE] * fresh,
            [
                pltpu.VMEM((4, shards, 16, width), BF),
                pltpu.SemaphoreType.DMA((4 * shards,)),
            ]
            * fresh
            + [
                pltpu.VMEM((padded, width), BF),
                pltpu.VMEM((padded, 3 * width), BF),
                head_probs,
                pltpu.VMEM((padded, width), BF),
                pltpu.VMEM((padded, width), F32),
                pltpu.VMEM((padded, width), BF),
                attn_weights,
                pltpu.SemaphoreType.DMA((4 * shards,)),
                pltpu.SemaphoreType.DMA((7,)),
            ]
            + [pltpu.VMEM((4, width), F32)] * fresh,
            (tied(attn_place), tok, *([] if fresh else [gains]), *sources),
            time=9,
        )
        kept.append((first_in, qkv, probs, context, hidden))
        if half == 0:
            all_weights = attn_pieces[0]
            if ringed:
                all_weights, facts, gains = found
                wait(gains)
        if half == 0 or not ringed:
            states_of.append(
                [second_in, swap_core(tied(second_in)), swap_row(tied(second_in))]
            )
        if half == 0 and ringed:
            wait(experts[3], near[2], states_of[0][1])
            near.append(swap_side(tied(experts[3])))
            grads.append(swap_core(tied(dmixed_row)))
    if ringed:
        wait(second_in, states_of[0][2], near[3], grads[3])
        beside_core = swap_core(tied(second_in))
        states_of[0].append(swap_core(tied(states_of[0][2])))
        wait(beside_core, states_of[0][3])
        before_row = clock[0]
        states_of.append([second_in, beside_core, swap_row(tied(second_in))])
        numbers = facts[:, :, 0, 4 * rows : 4 * rows + 3 * halves].astype(F32)
        kinds = lax.dynamic_index_in_dim(numbers, shard, 1, keepdims=False)
        kinds = jnp.stack(
            [
                lax.dynamic_index_in_dim(kinds, jnp.bitwise_xor(replica, rel), 0, keepdims=False)
                for rel in range(4)
            ]
        )
        kinds = kinds[:, :halves].astype(jnp.int32).T
        counts = numbers.reshape(-1, 3, halves).sum((0, 2))[1:].astype(jnp.int32)
        expert_pieces = [part for both in zip(experts, near) for part in both]
        states_of[1].append(swap_core(states_of[1][2]))
    else:
        grads.append(swap_core(dmixed_row))
        for states in states_of:
            states.append(swap_core(states[2]))

    left = padded - tail
    expert_scratch = [
        pltpu.VMEM((4, width, columns), BF),
        *[pltpu.VMEM((5, main, width), BF)] * 2,
        *[pltpu.VMEM((5, main, columns), BF)] * 2,
        *[pltpu.VMEM((4 * left, width), BF)] * 2,
        *[pltpu.VMEM((2, padded, width), BF)] * 4,
        pltpu.SemaphoreType.DMA((len(expert_pieces),)),
        pltpu.SemaphoreType.DMA((8,)),
        pltpu.SemaphoreType.DMA((8,)),
        pltpu.SemaphoreType.DMA((14,)),
    ]
    acts, dpres, outs, arriving = [], [], [], []
    for half in range(halves):
        act, dpre, keep_grad, send_grad, keep_out, send_out = call(
            functools.partial(expert_layer, half, main, tail),
            [shaped((5, main, columns))] * 2 + [shaped((2, padded, width))] * 4,
            [SCALARS] * 2 + [ANYWHERE] * (8 + len(expert_pieces)),
            [ANYWHERE] * 6,
            expert_scratch,
            (tied(expert_place), kinds[half], *states_of[half], *grads, *expert_pieces),
            time=12.5,
        )
        acts.append(act)
        dpres.append(dpre)
        if half == 0:
            wait(states_of[1][2])
        else:
            wait(arriving[half - 1][1])
        summed = add(keep_grad, swap_core(tied(send_grad)))
        outs.append((keep_out, swap_core(tied(send_out))))
        if half + 1 < halves:
            wait(summed, outs[-1][1])
        arriving.append((summed, swap_row(summed[1])))

    piece_count = len(expert_pieces)
    if ringed:
        spots = [(0, 0), (1, 0), (2, 0), (2, 1), (3, 0), (4, 0), (5, 0), (6, 0)]
        grad_sizes = [1, 1, 2, 1, 1, 1, 1]
    else:
        spots, grad_sizes = [(0, 0)], [1]
    expert_parts = call(
        functools.partial(expert_weight_grads, main, tail, halves, spots),
        [shaped((size, 4, spans, columns)) for size in grad_sizes],
        [SCALARS] * 2 + [ANYWHERE] * (4 * halves + 4 + 2 * halves),
        [ANYWHERE] * len(grad_sizes),
        [
            pltpu.VMEM((4, width, columns), F32),
            pltpu.VMEM((4, width, columns), BF),
            *[pltpu.VMEM((5 * halves, main, width), BF)] * 2,
            *[pltpu.VMEM((5 * halves, main, columns), BF)] * 2,
            pltpu.SemaphoreType.DMA((piece_count, 4)),
            pltpu.SemaphoreType.DMA((halves, 8)),
            pltpu.SemaphoreType.DMA((halves, 8)),
            pltpu.SemaphoreType.DMA((halves, 5, 2)),
        ],
        (
            tied(expert_place),
            kinds.reshape(-1),
            *[state for states in states_of for state in states],
            *grads,
            *acts,
            *dpres,
        ),
        time=13.5,
    )

    wait(expert_parts[0])
    if ringed:
        direct = shift_line(tied(expert_parts[2]), lines - 1)
        sent_two = swap_side(tied(expert_parts[4]))
    wait(outs[-1][1])
    out_sum = jnp.stack([add(*pair) for pair in outs])
    out_rest = None
    lows, dqkvs, norm_parts, input_grads = [], [], [], []
    for half in range(halves):
        first_in, qkv, probs, context, hidden = kept[half]
        summed, far = arriving[half]
        low, dqkv, input_grad, norm_grads = call(
            functools.partial(attention_backward, length),
            [
                shaped((padded, width)),
                shaped((padded, 3 * width)),
                shaped((length, width), F32),
                shaped((4, width), F32),
            ],
            [one_of(tok, half), WHOLE, one_of(summed, 0), WHOLE, one_of(dmixed, half), WHOLE]
            + [ANYWHERE] * 4,
            [WHOLE] * 4,
            [
                pltpu.VMEM((padded, 3 * width), BF),
                head_probs,
                attn_weights,
                pltpu.VMEM((padded, width), F32),
                pltpu.SemaphoreType.DMA((4,)),
            ],
            (tok, tied(gains), summed, far, dmixed, hidden, qkv, probs, all_weights, expert_parts[0]),
            time=10,
        )
        wait(norm_grads)
        if half == 0:
            wait(arriving[1][1])
            out_rest = swap_row(tied(out_sum[:, 1]))
            if ringed:
                current = step_line(tied(add(expert_parts[3], wait(sent_two))))
                sent_three = swap_side(tied(expert_parts[6]))
        elif ringed:
            direct = wait(direct)
            sent_home = swap_side(tied(add(expert_parts[1], direct[1:2])))
        lows.append(low)
        dqkvs.append(dqkv)
        norm_parts.append(norm_grads)
        input_grads.append(input_grad)
    input_grad = jnp.stack(input_grads)

    core, row = replica % 2, replica // 2
    grad_place = jnp.stack([core, row * 2 * width, 1 - core, (1 - row) * 2 * width])
    grad_place = grad_place.astype(jnp.int32)
    owners = shards if ringed else 2
    core_rows = width // (2 * owners)
    keep, *sends = call(
        functools.partial(attention_weight_grads, halves),
        [
            shaped((size, core_rows, 2 * width))
            for size in (2 * owners + 1, *[owners // 2] * 3, owners // 2 + 1)
        ],
        [SCALARS] + [WHOLE] * halves + [ANYWHERE] * (4 * halves),
        [ANYWHERE] * 5,
        [
            *[pltpu.VMEM((halves, padded, width), BF)] * 3,
            pltpu.VMEM((halves, padded, 3 * width), BF),
            pltpu.VMEM((owners, 2, core_rows, 4 * width), BF),
            pltpu.VMEM((core_rows, 2 * width), BF),
            pltpu.SemaphoreType.DMA((6 * halves,)),
            pltpu.SemaphoreType.DMA((8,)),
        ],
        (
            tied(grad_place),
            *norm_parts,
            *[kept[h][0] for h in range(halves)],
            *dqkvs,
            *[kept[h][3] for h in range(halves)],
            *lows,
        ),
        time=8.5,
    )
    wait(keep, out_rest)
    if ringed:
        ready = add(wait(current), add(expert_parts[5], wait(sent_three)))
    received = [swap_core(tied(part)) for part in sends]
    divisor = counts.astype(F32)[:, None, None]

    def join_replicas(value, axis, row_axis):
        across = swap_row(value)
        mine, other = value, swap_core(value)
        far, far_other = across, swap_core(across)
        near_parts = jnp.where(core == 0, mine, other), jnp.where(core == 0, other, mine)
        far_parts = jnp.where(core == 0, far, far_other), jnp.where(core == 0, far_other, far)
        near_part = jnp.concatenate(near_parts, axis)
        far_part = jnp.concatenate(far_parts, axis)
        return jnp.concatenate(
            [jnp.where(row == 0, near_part, far_part), jnp.where(row == 0, far_part, near_part)],
            row_axis,
        )

    if ringed:
        current = step_line(tied(ready))
        received = wait(*received)
        half_shards = shards // 2
        parts = [
            add(keep[at * half_shards : (at + 1) * half_shards], received[at][:half_shards])
            for at in range(4)
        ]
        vector_block = add(keep[-1, :8], received[3][-1, :8])

        def by_side(value, other):
            pairs_of = value.reshape(-1, 2, *value.shape[1:])
            return lax.dynamic_index_in_dim(
                pairs_of, jnp.bitwise_xor(side, other), 1, keepdims=False
            )

        def with_vectors(value):
            return jnp.concatenate([value.reshape(-1, 2 * width), vector_block], 0)

        def split_vectors(value):
            return value[:-8].reshape(-1, core_rows, 2 * width), value[-8:]

        first_sent = swap_row(tied(with_vectors(parts[2])))
        both = jnp.concatenate([parts[1], parts[3]], 0)
        second_sent = swap_side(tied(by_side(both, 1)))
        home = add(wait(sent_home), expert_parts[0])
        home = add(home, direct[0:1])
        expert_mine = add(wait(current), home)[0]
        expert_row = swap_row(tied(expert_mine))
        expert_core = swap_core(tied(expert_mine))
        first_done, second_done = wait(first_sent, second_sent)
        first_done, vectors_done = split_vectors(first_done)
        first = add(parts[0], first_done)
        vector_block = add(vector_block, vectors_done)
        first_next = swap_side(tied(with_vectors(by_side(first, 1))))
        second = add(by_side(both, 0), second_done)
        middle = lines // 2
        second_next = swap_row(tied(second[middle:]))
        first_last, second_last, *_ = wait(first_next, second_next, expert_row, expert_core)
        first_last, vectors_done = split_vectors(first_last)
        first = add(by_side(first, 0), first_last)
        vector_block = add(vector_block, vectors_done)
        second = add(second[:middle], second_last)
        lined = jnp.concatenate([first, second], 0)

        def lined_block(steps):
            return with_vectors(
                lax.dynamic_index_in_dim(lined, jnp.mod(line - steps, lines), 0)
            )

        expert_last = swap_core(tied(expert_row))
        arrived = [
            shift_line(tied(lined_block(steps)), lines - steps) for steps in range(1, lines)
        ]
        wait(*arrived, expert_last)
        expert_all = jnp.stack([expert_mine, expert_core, expert_row, expert_last])
        reduced = sum([part.astype(F32) for part in arrived], lined_block(0).astype(F32))
        vectors_sum = reduced[core_rows : core_rows + 2].reshape(4, width)
        vectors_sum = lax.dynamic_slice_in_dim(vectors_sum, shard * rows, rows, 1)
        attn_mine = reduced[:core_rows].astype(BF)
        attn_grad = join_replicas(tied(attn_mine), 0, 1)
    else:
        summed = add(keep, jnp.concatenate(received, 0))
        mine = add(summed[:owners], swap_row(summed[owners:-1]))
        attn_grad = join_replicas(mine, 1, 2).reshape(width, 4 * width)
        attn_grad = lax.psum_scatter(attn_grad, "fsdp", scatter_dimension=0, tiled=True)
        vectors_sum = functools.reduce(jnp.add, norm_parts)
        vectors_sum = lax.psum_scatter(vectors_sum, "fsdp", scatter_dimension=1, tiled=True)
        vectors_sum = lax.psum(vectors_sum, "dp")
        expert_mine = lax.psum_scatter(
            expert_parts[0][0], "fsdp", scatter_dimension=1, tiled=True
        )
        expert_all = all_replicas(expert_mine)
    expert_all = in_order(expert_all)
    up_grad = jnp.concatenate([part[:2] for part in expert_all], 2).astype(F32) / divisor
    down_grad = (
        jnp.concatenate([part[2:] for part in expert_all], 2).astype(F32).transpose(0, 2, 1)
        / divisor
    )
    mixed = jnp.stack(
        [
            (kept[h][4] + out_sum[h, 0].astype(F32) + out_rest[h].astype(F32))[:length]
            for h in range(halves)
        ]
    ).astype(BF)
    vector_grads = [vectors_sum[at] for at in range(4)]
    attn_grad = attn_grad.astype(F32)
    return (
        mixed,
        input_grad,
        vector_grads[0],
        vector_grads[1],
        attn_grad[:, : 3 * width],
        attn_grad[:, 3 * width :],
        vector_grads[2],
        vector_grads[3],
        up_grad,
        down_grad,
        counts,
    )


def solution(mesh):
    return jax.shard_map(
        per_device,
        mesh=mesh,
        in_specs=(
            P(("fsdp", "dp"), None, None),
            P(("fsdp", "dp"), None),
            P(("fsdp", "dp"), None),
            P(("fsdp", "dp"), None, None),
            P("fsdp"),
            P("fsdp"),
            P("fsdp", None),
            P("fsdp", None),
            P("fsdp"),
            P("fsdp"),
            P(None, "fsdp", None),
            P(None, None, "fsdp"),
        ),
        out_specs=(
            P(("fsdp", "dp"), None, None),
            P(("fsdp", "dp"), None, None),
            P("fsdp"),
            P("fsdp"),
            P("fsdp", None),
            P("fsdp", None),
            P("fsdp"),
            P("fsdp"),
            P(None, "fsdp", None),
            P(None, None, "fsdp"),
            P(),
        ),
        check_vma=False,
    )
```
